32 devices in a mesh: ctx: 8 (over z, y), head: 4 (over x, core).
Axes of the slice: x: 2, y: 2, z: 4, core: 2. Of those that a mesh axis runs over, the one named last changes fastest.
Arguments:
- queries: bfloat16 [8192, 4096], P('ctx', 'head'), may hold values from -6.4 to 6.4
- keys: bfloat16 [8192, 4096], P('ctx', 'head'), may hold values from -0.62 to 0.62
- values: bfloat16 [8192, 4096], P('ctx', 'head'), may hold values from -7.6 to 7.6
- log_decay: float32 [32, 8192], P('head', 'ctx'), may hold values from -1.6 to 0, as said below
- gain: float32 [4096], P('head'), may hold values from 0.1 to 1.9
Outputs:
- shift: float32 [4096], P('head')
- covariance: float32 [4096, 2048], P(('head', 'ctx'))
The draws below stay inside these ranges and needn't reach their ends.
Inputs may be any that keep to these rules, and one draw needn't show every extreme that they name: log_decay is negative everywhere.
All inputs are finite; a program needn't handle non-finite values.
Results may differ from the reference program's by a relative error of at most 0.0045.
The reference program's roundings to bfloat16 on the way (of `weights`, `attended` and `centered`) count: a program that leaves them out, or rounds other values in their place, can miss the bound.
Values may be sent and summed in bfloat16 or wider, within the bound.
No kernel may reach another device: no remote copies, remote signals or barrier semaphores. Data moves between devices by JAX's collectives and lax.ppermute only.
A program may use at most 128 MiB of HBM per device.

```python
import jax
import jax.numpy as jnp
from jax import lax

HEAD_DIM = 128
HEADS = 32
SPAN = 256
TOK_DEV = 1024
TOKENS = 8192
CH = 4096
CH_DEV = 1024
N_CTX = 8


def head_signs(key):
    coin_flips = jax.random.bernoulli(jax.random.fold_in(key, 4), 0.5, (CH,))
    return jnp.where(coin_flips, 1.0, -1.0).astype(jnp.float32)


def draw_queries(key, part):
    sign_vector = head_signs(key)
    jitter = jnp.clip(jax.random.normal(jax.random.fold_in(key, 1), (TOKENS, CH), jnp.float32), -6.0, 6.0)
    return (jitter + 0.3 * sign_vector[None, :]).astype(jnp.bfloat16)


def draw_keys(key, part):
    sign_vector = head_signs(key)
    jitter = jnp.clip(jax.random.normal(jax.random.fold_in(key, 2), (TOKENS, CH), jnp.float32), -6.0, 6.0)
    offset = 0.13 * TOKENS ** (-0.5)
    return (0.1 * jitter + offset * sign_vector[None, :]).astype(jnp.bfloat16)


def draw_values(key, part):
    jitter = jnp.clip(jax.random.normal(jax.random.fold_in(key, 3), (TOKENS, CH), jnp.float32), -6.0, 6.0)
    magnitude = jnp.exp(jax.random.uniform(jax.random.fold_in(key, 5), (CH,), jnp.float32, jnp.log(0.25), 0.0))
    coin_flips = jax.random.bernoulli(jax.random.fold_in(key, 6), 0.5, (CH,))
    value_signs = jnp.where(coin_flips, 1.0, -1.0).astype(jnp.float32)
    shard_count = TOKENS // TOK_DEV
    drift = jax.random.uniform(jax.random.fold_in(key, 7), (shard_count, CH), jnp.float32, 0.5, 1.5)
    shard_drift = jnp.repeat(drift, TOK_DEV, axis=0)
    offset = (magnitude * value_signs)[None, :] * shard_drift
    return (jitter + offset).astype(jnp.bfloat16)


def draw_log_decay(key, part):
    keys = jax.random.split(key, 6)
    fast_share = 0.5
    picks = jax.random.uniform(keys[0], (HEADS, 1), jnp.float32)
    fast_rate = jnp.exp(jax.random.uniform(keys[1], (HEADS, 1), jnp.float32, jnp.log(1.0 / 50.0), jnp.log(1.0 / 30.0)))
    slow_rate = jnp.exp(jax.random.uniform(keys[2], (HEADS, 1), jnp.float32, jnp.log(0.05), jnp.log(0.8))) / TOKENS
    decay_rate = jnp.where(picks < fast_share, fast_rate, slow_rate)
    coarse_estimate = jax.random.uniform(keys[3], (HEADS, TOKENS), jnp.float32, 0.5, 1.5)
    outlier_spots = jax.random.randint(keys[4], (3,), 0, TOKENS)
    dimension_sizes = jax.random.uniform(keys[5], (3,), jnp.float32, 0.22, 0.5)
    token_position = jnp.arange(TOKENS)
    spike_amount = jnp.sum(jnp.where(token_position[None, :] == outlier_spots[:, None], dimension_sizes[:, None], 0.0), axis=0)
    return (-(decay_rate * coarse_estimate + spike_amount[None, :])).astype(jnp.float32)


def setup_inputs(seed: int = 0) -> dict:
    splits = jax.random.split(jax.random.key(seed), 6)
    queries = draw_queries(jax.random.fold_in(splits[5], 71), 0)
    keys = draw_keys(jax.random.fold_in(splits[5], 71), 0)
    values = draw_values(jax.random.fold_in(splits[5], 71), 0)
    log_decay = draw_log_decay(jax.random.fold_in(splits[5], 71), 0)
    gain = jnp.clip(1.0 + 0.18 * jax.random.normal(splits[4], (CH,), jnp.float32), 0.1, 1.9)
    return dict(queries=queries, keys=keys, values=values, log_decay=log_decay, gain=gain)


def block_step(state, inputs):
    query, key, value, decay = inputs
    cumul = jnp.cumsum(decay, axis=1)
    scores = jnp.einsum('thd,shd->hts', query.astype(jnp.float32), key.astype(jnp.float32))
    length = query.shape[0]
    later = jnp.arange(length)[:, None] >= jnp.arange(length)[None, :]
    diff = cumul[:, :, None] - cumul[:, None, :]
    factor = jnp.where(later[None], jnp.exp(jnp.where(later[None], diff, 0.0)), 0.0)
    weights = (scores * factor).astype(jnp.bfloat16)
    inner = jnp.einsum('hts,shd->thd', weights.astype(jnp.float32), value.astype(jnp.float32))
    scaled_q = query.astype(jnp.float32) * jnp.exp(cumul).T[:, :, None]
    outer = jnp.einsum('thd,hde->the', scaled_q, state, precision=lax.Precision.HIGHEST)
    scaled_k = key.astype(jnp.float32) * jnp.exp(cumul[:, -1:] - cumul).T[:, :, None]
    update = jnp.einsum('shd,she->hde', scaled_k, value.astype(jnp.float32), precision=lax.Precision.HIGHEST)
    new_state = jnp.exp(cumul[:, -1])[:, None, None] * state + update
    return (new_state, inner + outer)

def reference(queries, keys, values, log_decay, gain):
    blocks = TOKENS // SPAN
    query = queries.reshape(blocks, SPAN, HEADS, HEAD_DIM)
    key = keys.reshape(blocks, SPAN, HEADS, HEAD_DIM)
    value = values.reshape(blocks, SPAN, HEADS, HEAD_DIM)
    decay = log_decay.reshape(HEADS, blocks, SPAN).transpose(1, 0, 2)
    start = jnp.zeros((HEADS, HEAD_DIM, HEAD_DIM), jnp.float32)
    _, raw = lax.scan(block_step, start, (query, key, value, decay))
    raw = raw.reshape(TOKENS, HEADS, HEAD_DIM)
    scale = jnp.sqrt(lax.optimization_barrier(jnp.mean(raw * raw, axis=-1, keepdims=True)) + 1e-06)
    attended = (raw / scale * gain.reshape(HEADS, HEAD_DIM)).reshape(TOKENS, CH).astype(jnp.bfloat16)
    wide = attended.astype(jnp.float32)
    shift = (lax.optimization_barrier(jnp.max(wide, axis=0)) + lax.optimization_barrier(jnp.min(wide, axis=0))) / 2.0
    shards = attended.reshape(N_CTX, TOK_DEV, CH)
    width = 2 * CH_DEV
    groups = CH // width

    def add_shard(total, shard):
        means = lax.optimization_barrier(jnp.mean(shard.astype(jnp.float32), axis=0))
        centered = (shard.astype(jnp.float32) - means).astype(jnp.bfloat16)
        parts = []
        for group in range(groups):
            piece = centered[:, group * width:(group + 1) * width]
            parts.append(jnp.dot(piece.T, piece, preferred_element_type=jnp.float32))
        return (total + jnp.stack(parts), means)
    zero = jnp.zeros((groups, width, width), jnp.float32)
    gram, shard_means = lax.scan(add_shard, zero, shards)
    channel_spread = shard_means - lax.optimization_barrier(jnp.mean(shard_means, axis=0))
    rows = []
    for group in range(groups):
        piece = channel_spread[:, group * width:(group + 1) * width]
        fix = TOK_DEV * jnp.dot(piece.T, piece, precision=lax.Precision.HIGHEST)
        rows.append((gram[group] + fix) / TOKENS)
    return (shift, jnp.concatenate(rows, axis=0))
```

```python
import functools

import jax
import jax.numpy as jnp
from jax import lax
from jax.experimental import pallas as pl
from jax.experimental.pallas import tpu as pltpu
from jax.sharding import PartitionSpec as P

HEAD_DIM = 128
SPAN = 256
F32 = jnp.float32
BF16 = jnp.bfloat16
HIGHEST = lax.Precision.HIGHEST
MIB = 1 << 20


def params(limit_mib):
    return pltpu.CompilerParams(vmem_limit_bytes=limit_mib * MIB)


def cost(flops, moved, transcendentals=0):
    return pl.CostEstimate(
        flops=int(flops), bytes_accessed=int(moved), transcendentals=int(transcendentals)
    )


def whole(shape):
    return pl.BlockSpec(shape, lambda *_: (0,) * len(shape))


def struct(shape, dtype):
    return jax.ShapeDtypeStruct(shape, dtype)


def dot(a, b):
    return jnp.dot(a, b, preferred_element_type=F32)


def split(value):
    high = value.astype(BF16)
    return high, (value - high.astype(F32)).astype(BF16)


def running_sum(decay):
    rows = lax.broadcasted_iota(jnp.int32, (SPAN, SPAN), 0)
    columns = lax.broadcasted_iota(jnp.int32, (SPAN, SPAN), 1)
    ones = jnp.where(rows <= columns, 1.0, 0.0).astype(F32)
    return jnp.dot(decay, ones, precision=HIGHEST, preferred_element_type=F32)


def head_columns(head):
    return slice(head * HEAD_DIM, (head + 1) * HEAD_DIM)


def states_kernel(shards, me_ref, k_ref, v_ref, decay_ref, entering_ref, before_ref, *rest):
    pieces, (state, total) = rest[:shards], rest[shards:]
    heads = decay_ref.shape[0]
    step = pl.program_id(0)

    @pl.when(step == 0)
    def _():
        state[...] = jnp.zeros_like(state)
        total[...] = jnp.ones_like(total)

    entering_ref[0] = state[...]
    before_ref[0] = total[...]
    cumul = running_sum(decay_ref[...])
    last = cumul[:, SPAN - 1 :]
    weight = jnp.exp(last - cumul)
    drop = jnp.exp(last)
    for head in range(heads):
        cols = head_columns(head)
        scaled = k_ref[:, cols].T.astype(F32) * weight[head : head + 1, :]
        high, low = split(scaled)
        value = v_ref[:, cols]
        update = dot(high, value) + dot(low, value)
        state[cols, :] = state[cols, :] * drop[head : head + 1, :] + update
    total[...] = total[...] * drop

    @pl.when(step == pl.num_programs(0) - 1)
    def _():
        rows = heads * HEAD_DIM // shards
        for index in range(shards):
            start = pl.multiple_of((me_ref[0] ^ index) * rows, rows)
            pieces[index][:rows, :] = state[pl.ds(start, rows), :]
            piece_total = total[pl.ds(start // HEAD_DIM, 1), :]
            pieces[index][rows:, :] = jnp.broadcast_to(piece_total, (8, HEAD_DIM))


def local_states(me, keys, values, log_decay, shards):
    count, width = keys.shape
    heads = width // HEAD_DIM
    blocks = count // SPAN
    rows = width // shards
    piece = (rows + 8, HEAD_DIM)
    shapes = [(blocks, width, HEAD_DIM), (blocks, heads, HEAD_DIM)] + [piece] * shards
    tokens = pl.BlockSpec((SPAN, width), lambda i, me: (i, 0))
    out = pl.pallas_call(
        functools.partial(states_kernel, shards),
        grid_spec=pltpu.PrefetchScalarGridSpec(
            num_scalar_prefetch=1,
            grid=(blocks,),
            in_specs=[tokens, tokens, pl.BlockSpec((heads, SPAN), lambda i, me: (0, i))],
            out_specs=[
                pl.BlockSpec((1, width, HEAD_DIM), lambda i, me: (i, 0, 0)),
                pl.BlockSpec((1, heads, HEAD_DIM), lambda i, me: (i, 0, 0)),
            ]
            + [whole(piece)] * shards,
            scratch_shapes=[pltpu.VMEM((width, HEAD_DIM), F32), pltpu.VMEM((heads, HEAD_DIM), F32)],
        ),
        out_shape=[struct(shape, F32) for shape in shapes],
        compiler_params=params(24),
        cost_estimate=cost(4 * count * width * HEAD_DIM, 4 * count * width),
        name="local_states",
    )(me, keys, values, log_decay)
    return out[0], out[1], out[2:]


def chain_kernel(shards, me_ref, *refs):
    arrived, outs, (ordered, entering) = refs[:shards], refs[shards : 2 * shards], refs[2 * shards :]
    rows = outs[0].shape[0]
    for index in range(shards):
        ordered[me_ref[0] ^ index] = arrived[index][...]
    carried = jnp.zeros((rows, HEAD_DIM), F32)
    for shard in range(shards):
        entering[shard] = carried
        carried = carried * ordered[shard, rows : rows + 1, :] + ordered[shard, :rows, :]
    for index in range(shards):
        outs[index][...] = entering[me_ref[0] ^ index]


def chain(me, pieces):
    shards = len(pieces)
    rows = pieces[0].shape[0] - 8
    return pl.pallas_call(
        functools.partial(chain_kernel, shards),
        grid_spec=pltpu.PrefetchScalarGridSpec(
            num_scalar_prefetch=1,
            grid=(1,),
            in_specs=[whole((rows + 8, HEAD_DIM))] * shards,
            out_specs=[whole((rows, HEAD_DIM))] * shards,
            scratch_shapes=[
                pltpu.VMEM((shards, rows + 8, HEAD_DIM), F32),
                pltpu.VMEM((shards, rows, HEAD_DIM), F32),
            ],
        ),
        out_shape=[struct((rows, HEAD_DIM), F32)] * shards,
        compiler_params=params(16),
        name="chain",
    )(me, *pieces)


def inner_kernel(q_ref, k_ref, v_ref, decay_ref, raw_ref):
    heads = decay_ref.shape[0]
    cumul = running_sum(decay_ref[...])
    columns = cumul.T
    half = SPAN // 2
    for head in range(heads):
        cols = head_columns(head)
        for part in range(2):
            rows = slice(part * half, (part + 1) * half)
            width = (part + 1) * half
            scores = lax.dot_general(
                q_ref[rows, cols],
                k_ref[:width, cols],
                (((1,), (1,)), ((), ())),
                preferred_element_type=F32,
            )
            diff = columns[rows, head : head + 1] - cumul[head : head + 1, :width]
            token = lax.broadcasted_iota(jnp.int32, (half, width), 0) + part * half
            earlier = lax.broadcasted_iota(jnp.int32, (half, width), 1)
            factor = jnp.exp(jnp.where(token >= earlier, diff, -jnp.inf))
            weights = (scores * factor).astype(BF16)
            raw_ref[rows, cols] = dot(weights, v_ref[:width, cols])


def inner(queries, keys, values, log_decay):
    count, width = keys.shape
    heads = width // HEAD_DIM
    tokens = pl.BlockSpec((SPAN, width), lambda i: (i, 0))
    return pl.pallas_call(
        inner_kernel,
        grid=(count // SPAN,),
        in_specs=[tokens, tokens, tokens, pl.BlockSpec((heads, SPAN), lambda i: (0, i))],
        out_specs=tokens,
        out_shape=struct((count, width), F32),
        compiler_params=params(24),
        cost_estimate=cost(4 * count * width * SPAN, 10 * count * width, count * heads * SPAN),
        name="inner",
    )(queries, keys, values, log_decay)


def finish_kernel(
    shards, me_ref, q_ref, raw_ref, entering_ref, before_ref, decay_ref, gain_ref, *rest
):
    pieces, (centered_ref, stats_ref, arrived) = rest[:shards], rest[shards:]
    heads = decay_ref.shape[0]
    width = heads * HEAD_DIM
    rows = width // shards
    step = pl.program_id(0)
    blocks = pl.num_programs(0)
    count = centered_ref.shape[0]

    @pl.when(step == 0)
    def _():
        for index in range(shards):
            start = pl.multiple_of((me_ref[0] ^ index) * rows, rows)
            arrived[pl.ds(start, rows), :] = pieces[index][...]
        stats_ref[0:1, :] = jnp.zeros((1, width), F32)
        stats_ref[1:2, :] = jnp.full((1, width), -jnp.inf, F32)
        stats_ref[2:3, :] = jnp.full((1, width), jnp.inf, F32)
        stats_ref[3:, :] = jnp.zeros((5, width), F32)

    factor = jnp.exp(running_sum(decay_ref[...])).T
    first = pl.multiple_of(step * SPAN, SPAN)
    for head in range(heads):
        cols = head_columns(head)
        state = entering_ref[0, cols, :] + before_ref[0, head : head + 1, :] * arrived[cols, :]
        high, low = split(state)
        query = q_ref[:, cols]
        outer = dot(query, high) + dot(query, low)
        raw = raw_ref[:, cols] + outer * factor[:, head : head + 1]
        power = jnp.mean(raw * raw, axis=1, keepdims=True)
        attended = (raw / jnp.sqrt(power + 1e-06) * gain_ref[:, cols]).astype(BF16)
        centered_ref[pl.ds(first, SPAN), cols] = attended
        wide = attended.astype(F32)
        stats_ref[0:1, cols] += jnp.sum(wide, axis=0, keepdims=True)
        stats_ref[1:2, cols] = jnp.maximum(stats_ref[1:2, cols], jnp.max(wide, axis=0, keepdims=True))
        stats_ref[2:3, cols] = jnp.minimum(stats_ref[2:3, cols], jnp.min(wide, axis=0, keepdims=True))

    @pl.when(step == blocks - 1)
    def _():
        mean = stats_ref[0:1, :] / count
        stats_ref[0:1, :] = mean

        @pl.loop(0, count // 128)
        def _(index):
            part = pl.ds(pl.multiple_of(index * 128, 128), 128)
            centered_ref[part, :] = (centered_ref[part, :].astype(F32) - mean).astype(BF16)


def finish(me, queries, raw, entering, before, log_decay, gain, pieces):
    count, width = queries.shape
    heads = width // HEAD_DIM
    shards = len(pieces)
    tokens = pl.BlockSpec((SPAN, width), lambda i, me: (i, 0))
    return pl.pallas_call(
        functools.partial(finish_kernel, shards),
        grid_spec=pltpu.PrefetchScalarGridSpec(
            num_scalar_prefetch=1,
            grid=(count // SPAN,),
            in_specs=[
                tokens,
                tokens,
                pl.BlockSpec((1, width, HEAD_DIM), lambda i, me: (i, 0, 0)),
                pl.BlockSpec((1, heads, HEAD_DIM), lambda i, me: (i, 0, 0)),
                pl.BlockSpec((heads, SPAN), lambda i, me: (0, i)),
                whole((1, width)),
            ]
            + [whole(pieces[0].shape)] * shards,
            out_specs=[whole((count, width)), whole((8, width))],
            scratch_shapes=[pltpu.VMEM((width, HEAD_DIM), F32)],
        ),
        out_shape=[struct((count, width), BF16), struct((8, width), F32)],
        compiler_params=params(32),
        cost_estimate=cost(4 * count * width * HEAD_DIM, 10 * count * width),
        name="finish",
    )(me, queries, raw, entering, before, log_decay, gain, *pieces)


def gram_kernel(rows, ranges, me_ref, own_ref, other_ref, keep_ref, send_ref, both, sems):
    width = own_ref.shape[1]
    copies = [
        pltpu.make_async_copy(own_ref, both.at[:, :width], sems.at[0]),
        pltpu.make_async_copy(other_ref, both.at[:, width:], sems.at[1]),
    ]
    for copy in copies:
        copy.start()
    for copy in copies:
        copy.wait()
    low = me_ref[0] & 1
    for index in range(keep_ref.shape[0]):
        for out_ref, bit in ((send_ref, 1 - low), (keep_ref, low)):
            start = (2 * index + bit) * rows
            left = both[:, pl.ds(pl.multiple_of(start, rows), rows)].T
            place = 0
            for begin, end in ranges:
                size = (end - begin) * rows
                at = pl.multiple_of(start + begin * rows, rows)
                out = dot(left, both[:, pl.ds(at, size)])
                out_ref[index, :, place : place + size] = out.astype(out_ref.dtype)
                place += size


def gram_parts(me, own, other, rows, ranges):
    count, width = own.shape
    shards = width // rows
    size = sum(end - begin for begin, end in ranges) * rows
    if rows % 128:
        full = lax.dot_general(
            own,
            jnp.concatenate([own, other], axis=1),
            (((0,), (0,)), ((), ())),
            preferred_element_type=F32,
        )
        parts = []
        for shard in range(shards):
            line = full[shard * rows : (shard + 1) * rows]
            slabs = [line[:, (shard + a) * rows : (shard + b) * rows] for a, b in ranges]
            parts.append(jnp.concatenate(slabs, axis=1))
        parts = jnp.stack(parts).reshape(shards // 2, 2, rows, size)
        low = me[0] & 1
        keep = lax.dynamic_index_in_dim(parts, low, 1, False)
        send = lax.dynamic_index_in_dim(parts, 1 - low, 1, False)
        return keep, send.astype(BF16)
    shape = (shards // 2, rows, size)
    anywhere = pl.BlockSpec(memory_space=pl.ANY)
    return pl.pallas_call(
        functools.partial(gram_kernel, rows, ranges),
        grid_spec=pltpu.PrefetchScalarGridSpec(
            num_scalar_prefetch=1,
            grid=(1,),
            in_specs=[anywhere, anywhere],
            out_specs=[whole(shape), whole(shape)],
            scratch_shapes=[pltpu.VMEM((count, 2 * width), BF16), pltpu.SemaphoreType.DMA((2,))],
        ),
        out_shape=[struct(shape, F32), struct(shape, BF16)],
        compiler_params=params(32),
        cost_estimate=cost(2 * count * width * size, 4 * count * width),
        name="gram",
    )(me, own, other)


def cover_kernel(rows, shards, total, order, me_ref, means_ref, others_ref, *refs):
    chunk_count = len(order)
    chunks = refs[:chunk_count]
    mirrors = refs[chunk_count : chunk_count + shards - 1]
    out_ref, spread = refs[chunk_count + shards - 1 :]
    width = rows * shards
    mine, side = me_ref[0], me_ref[1]
    for ref, place in ((means_ref, side), (others_ref, 1 - side)):
        value = ref[...]
        centre = jnp.sum(value, axis=0, keepdims=True) / shards
        spread[:, pl.ds(pl.multiple_of(place * width, width), width)] = value - centre
    block = side * shards + mine
    left = spread[:, pl.ds(pl.multiple_of(block * rows, rows), rows)].T
    count = total // shards
    out_ref[...] = count * jnp.dot(left, spread[...], precision=HIGHEST, preferred_element_type=F32)

    def put(position, gram):
        position = lax.rem(position + 2 * shards, 2 * shards)
        at = pl.ds(pl.multiple_of(position * rows, rows), rows)
        out_ref[:, at] = (out_ref[:, at] + gram) / total

    for chunk, steps in zip(chunks, order):
        for index, step in enumerate(steps):
            put(block + step, chunk[:, index * rows : (index + 1) * rows])
    for index in range(shards - 1):
        put(block - (index + 1), mirrors[index][...].T.astype(F32))


def cover(me, means, others, chunks, mirrors, order, rows, shards, total):
    width = rows * shards
    if rows % 128:
        mine, side = me[0], me[1]
        pair = [jnp.where(side == 0, means, others), jnp.where(side == 0, others, means)]
        spread = jnp.concatenate(pair, axis=1)
        spread = spread - jnp.mean(spread, axis=0)
        block = side * shards + mine
        left = lax.dynamic_slice_in_dim(spread, block * rows, rows, 1)
        fix = (total // shards) * jnp.dot(left.T, spread, precision=HIGHEST)
        ahead = {}
        for chunk, steps in zip(chunks, order):
            for index, step in enumerate(steps):
                ahead[step] = chunk[:, index * rows : (index + 1) * rows]
        slabs = [mirrors[step - 1].T.astype(F32) for step in range(shards - 1, 0, -1)]
        slabs += [ahead[step] for step in range(shards + 1)]
        line = jnp.roll(jnp.concatenate(slabs, axis=1), (block - (shards - 1)) * rows, axis=1)
        return (line + fix) / total
    return pl.pallas_call(
        functools.partial(cover_kernel, rows, shards, total, order),
        grid_spec=pltpu.PrefetchScalarGridSpec(
            num_scalar_prefetch=1,
            grid=(1,),
            in_specs=[whole(value.shape) for value in (means, others, *chunks, *mirrors)],
            out_specs=whole((rows, 2 * width)),
            scratch_shapes=[pltpu.VMEM((shards, 2 * width), F32)],
        ),
        out_shape=struct((rows, 2 * width), F32),
        compiler_params=params(16),
        name="cover",
    )(me, means, others, *chunks, *mirrors)


def body(queries, keys, values, log_decay, gain):
    count, width = queries.shape
    shards = lax.axis_size("ctx")
    sides = lax.axis_size("head")
    rows = width // shards
    mine, head = lax.axis_index("ctx"), lax.axis_index("head")
    me = jnp.stack([mine, head % 2]).astype(jnp.int32)

    def to_shard(value, apart):
        return lax.ppermute(value, "ctx", [(a, a ^ apart) for a in range(shards)])

    def to_partner(value):
        return lax.ppermute(value, "head", [(a, a ^ 1) for a in range(sides)])

    def everywhere(values):
        return [values[0]] + [to_shard(values[k], k) for k in range(1, shards)]

    def forward(value, steps):
        pairs = []
        for shard in range(shards):
            for side in range(sides):
                block = (side % 2) * shards + shard + steps
                other = (block // shards) % 2
                target = (block % shards) * sides + (side // 2) * 2 + other
                pairs.append((shard * sides + side, target))
        return lax.ppermute(value, ("ctx", "head"), pairs)

    entering, before, pieces = local_states(me, keys, values, log_decay, shards)
    arrived = everywhere(pieces)
    raw = inner(queries, keys, values, log_decay)
    entry = everywhere(chain(me, arrived))
    centered, stats = finish(
        me, queries, raw, entering, before, log_decay, gain.reshape(1, width), entry
    )
    partner = to_partner(centered)

    third = (shards - 1) // 2
    order = [
        tuple(range(1, 1 + third)),
        tuple(range(1 + third, 1 + 2 * third)),
        tuple(range(1 + 2 * third, shards + 1)) + (0,),
    ]
    ranges = [
        ((1, 1 + third),),
        ((1 + third, 1 + 2 * third),),
        ((1 + 2 * third, shards + 1), (0, 1)),
    ]
    place = mine // 2
    chunks, mirrors = [], [None] * (shards - 1)
    for spans, steps in zip(ranges, order):
        keep, send = gram_parts(me, centered, partner, rows, spans)
        summed = keep + to_shard(send, 1).astype(F32)
        total = lax.dynamic_index_in_dim(summed, place, 0, False)
        for apart in range(1, shards // 2):
            slab = lax.dynamic_index_in_dim(summed, place ^ apart, 0, False).astype(BF16)
            total = total + to_shard(slab, 2 * apart).astype(F32)
        chunks.append(total)
        for index, step in enumerate(steps):
            if 0 < step < shards:
                slab = total[:, index * rows : (index + 1) * rows].astype(BF16)
                mirrors[step - 1] = forward(slab, step)

    small = stats[:3]
    gathered = jnp.stack(everywhere([small] * shards))
    means = gathered[:, 0]
    shift = (jnp.max(gathered[:, 1], axis=0) + jnp.min(gathered[:, 2], axis=0)) / 2.0
    others = to_partner(means)
    covariance = cover(me, means, others, chunks, mirrors, order, rows, shards, count * shards)
    return (shift, covariance)


def solution(mesh):
    placed = (P("ctx", "head"), P("ctx", "head"), P("ctx", "head"), P("head", "ctx"), P("head"))
    return jax.shard_map(
        body,
        mesh=mesh,
        in_specs=placed,
        out_specs=(P("head"), P(("head", "ctx"), None)),
        check_vma=False,
    )
```

```python
import functools

import jax
import jax.numpy as jnp
from jax import lax
from jax.experimental import pallas as pl
from jax.experimental.pallas import tpu as pltpu
from jax.sharding import PartitionSpec as P

HEAD_DIM = 128
SPAN = 256
F32 = jnp.float32
BF16 = jnp.bfloat16
HIGHEST = lax.Precision.HIGHEST
MIB = 1 << 20


def params(limit_mib):
    return pltpu.CompilerParams(vmem_limit_bytes=limit_mib * MIB)


def cost(flops, moved, transcendentals=0):
    return pl.CostEstimate(
        flops=int(flops), bytes_accessed=int(moved), transcendentals=int(transcendentals)
    )


def whole(shape):
    return pl.BlockSpec(shape, lambda *_: (0,) * len(shape))


def anywhere():
    return pl.BlockSpec(memory_space=pl.ANY)


def vmem():
    return pl.BlockSpec(memory_space=pltpu.VMEM)


def struct(shape, dtype):
    return jax.ShapeDtypeStruct(shape, dtype)


def dot(a, b):
    return jnp.dot(a, b, preferred_element_type=F32)


def split(value):
    high = value.astype(BF16)
    return high, (value - high.astype(F32)).astype(BF16)


def running_sum(decay):
    rows = lax.broadcasted_iota(jnp.int32, (SPAN, SPAN), 0)
    columns = lax.broadcasted_iota(jnp.int32, (SPAN, SPAN), 1)
    ones = jnp.where(rows <= columns, 1.0, 0.0).astype(F32)
    return jnp.dot(decay, ones, precision=HIGHEST, preferred_element_type=F32)


def head_columns(head):
    return slice(head * HEAD_DIM, (head + 1) * HEAD_DIM)


def states_kernel(shards, k_ref, v_ref, decay_ref, entering_ref, before_ref, *rest):
    pieces, (state, total) = rest[:shards], rest[shards:]
    heads = decay_ref.shape[0]
    step = pl.program_id(0)

    @pl.when(step == 0)
    def _():
        state[...] = jnp.zeros_like(state)
        total[...] = jnp.ones_like(total)

    entering_ref[0] = state[...]
    before_ref[0] = total[...]
    cumul = running_sum(decay_ref[...])
    last = cumul[:, SPAN - 1 :]
    weight = jnp.exp(last - cumul)
    drop = jnp.exp(last)
    for group in range(0, heads, 4):
        members = range(group, min(group + 4, heads))
        turned = [k_ref[:, head_columns(head)].T for head in members]
        parts = []
        for head, key in zip(members, turned):
            high, low = split(key.astype(F32) * weight[head : head + 1, :])
            parts.append(jnp.concatenate([high, low], axis=0))
        updates = [dot(part, v_ref[:, head_columns(head)]) for head, part in zip(members, parts)]
        for head, update in zip(members, updates):
            cols = head_columns(head)
            update = update[:HEAD_DIM] + update[HEAD_DIM:]
            state[cols, :] = state[cols, :] * drop[head : head + 1, :] + update
    total[...] = total[...] * drop

    @pl.when(step == pl.num_programs(0) - 1)
    def _():
        mine = lax.axis_index("ctx")
        rows = heads * HEAD_DIM // shards
        for index in range(shards):
            start = pl.multiple_of((mine ^ index) * rows, rows)
            pieces[index][:rows, :] = state[pl.ds(start, rows), :]
            piece_total = total[pl.ds(start // HEAD_DIM, 1), :]
            pieces[index][rows:, :] = jnp.broadcast_to(piece_total, (8, HEAD_DIM))


def local_states(keys, values, log_decay, shards):
    count, width = keys.shape
    heads = width // HEAD_DIM
    blocks = count // SPAN
    rows = width // shards
    piece = (rows + 8, HEAD_DIM)
    shapes = [(blocks, width, HEAD_DIM), (blocks, heads, HEAD_DIM)] + [piece] * shards
    tokens = pl.BlockSpec((SPAN, width), lambda i: (i, 0))
    out = pl.pallas_call(
        functools.partial(states_kernel, shards),
        grid=(blocks,),
        in_specs=[tokens, tokens, pl.BlockSpec((heads, SPAN), lambda i: (0, i))],
        out_specs=[
            pl.BlockSpec((1, width, HEAD_DIM), lambda i: (i, 0, 0)),
            pl.BlockSpec((1, heads, HEAD_DIM), lambda i: (i, 0, 0)),
        ]
        + [whole(piece)] * shards,
        scratch_shapes=[pltpu.VMEM((width, HEAD_DIM), F32), pltpu.VMEM((heads, HEAD_DIM), F32)],
        out_shape=[struct(shape, F32) for shape in shapes],
        compiler_params=params(56),
        cost_estimate=cost(4 * count * width * HEAD_DIM, 4 * count * width),
        name="local_states",
    )(keys, values, log_decay)
    return out[0], out[1], out[2:]


def chain_kernel(shards, *refs):
    mine = lax.axis_index("ctx")
    arrived, refs = refs[:shards], refs[shards + 1 :]
    outs, (ordered, entering) = refs[:shards], refs[shards:]
    rows = outs[0].shape[0]
    for index in range(shards):
        ordered[mine ^ index] = arrived[index][...]
    carried = jnp.zeros((rows, HEAD_DIM), F32)
    for shard in range(shards):
        entering[shard] = carried
        carried = carried * ordered[shard, rows : rows + 1, :] + ordered[shard, :rows, :]
    for index in range(shards):
        outs[index][...] = entering[mine ^ index]


def chain(pieces, after):
    shards = len(pieces)
    rows = pieces[0].shape[0] - 8
    return pl.pallas_call(
        functools.partial(chain_kernel, shards),
        grid=(1,),
        in_specs=[whole((rows + 8, HEAD_DIM))] * shards + [anywhere()],
        out_specs=[whole((rows, HEAD_DIM))] * shards,
        scratch_shapes=[
            pltpu.VMEM((shards, rows + 8, HEAD_DIM), F32),
            pltpu.VMEM((shards, rows, HEAD_DIM), F32),
        ],
        out_shape=[struct((rows, HEAD_DIM), F32)] * shards,
        compiler_params=params(16),
        name="chain",
    )(*pieces, after)


def inner_kernel(q_ref, k_ref, v_ref, decay_ref, raw_ref):
    heads = decay_ref.shape[0]
    cumul = running_sum(decay_ref[...])
    columns = cumul.T
    half = SPAN // 2
    for part in range(2):
        rows = slice(part * half, (part + 1) * half)
        width = (part + 1) * half
        token = lax.broadcasted_iota(jnp.int32, (half, width), 0) + part * half
        earlier = lax.broadcasted_iota(jnp.int32, (half, width), 1)
        for group in range(0, heads, 4):
            members = range(group, min(group + 4, heads))
            scores = [
                lax.dot_general(
                    q_ref[rows, head_columns(head)],
                    k_ref[:width, head_columns(head)],
                    (((1,), (1,)), ((), ())),
                    preferred_element_type=F32,
                )
                for head in members
            ]
            weights = []
            for head, score in zip(members, scores):
                diff = columns[rows, head : head + 1] - cumul[head : head + 1, :width]
                factor = jnp.exp(jnp.where(token >= earlier, diff, -jnp.inf))
                weights.append((score * factor).astype(BF16))
            for head, weight in zip(members, weights):
                cols = head_columns(head)
                raw_ref[rows, cols] = dot(weight, v_ref[:width, cols])


def inner(queries, keys, values, log_decay):
    count, width = keys.shape
    heads = width // HEAD_DIM
    tokens = pl.BlockSpec((SPAN, width), lambda i: (i, 0))
    return pl.pallas_call(
        inner_kernel,
        grid=(count // SPAN,),
        in_specs=[tokens, tokens, tokens, pl.BlockSpec((heads, SPAN), lambda i: (0, i))],
        out_specs=tokens,
        out_shape=struct((count, width), F32),
        compiler_params=params(24),
        cost_estimate=cost(4 * count * width * SPAN, 10 * count * width, count * heads * SPAN),
        name="inner",
    )(queries, keys, values, log_decay)


def finish_kernel(
    shards, q_ref, raw_ref, entering_ref, before_ref, decay_ref, gain_ref, *rest
):
    pieces, (centered_ref, stats_ref, arrived, sums) = rest[:shards], rest[shards:]
    heads = decay_ref.shape[0]
    width = heads * HEAD_DIM
    rows = width // shards
    step = pl.program_id(0)
    blocks = pl.num_programs(0)
    count = centered_ref.shape[0]

    @pl.when(step == 0)
    def _():
        mine = lax.axis_index("ctx")
        for index in range(shards):
            start = pl.multiple_of((mine ^ index) * rows, rows)
            arrived[pl.ds(start, rows), :] = pieces[index][...]
        sums[0:8, :] = jnp.zeros((8, width), F32)
        sums[8:16, :] = jnp.full((8, width), -jnp.inf, F32)
        sums[16:24, :] = jnp.full((8, width), jnp.inf, F32)

    factor = jnp.exp(running_sum(decay_ref[...])).T
    here = pl.ds(pl.multiple_of(step * SPAN, SPAN), SPAN)
    for group in range(0, heads, 4):
        members = range(group, min(group + 4, heads))
        outers = []
        for head in members:
            cols = head_columns(head)
            state = entering_ref[0, cols, :] + before_ref[0, head : head + 1, :] * arrived[cols, :]
            query = q_ref[:, cols]
            outers.append(
                dot(
                    jnp.concatenate([query, query], axis=1),
                    jnp.concatenate(split(state), axis=0),
                )
            )
        for head, outer in zip(members, outers):
            cols = head_columns(head)
            raw = raw_ref[:, cols] + outer * factor[:, head : head + 1]
            power = jnp.mean(raw * raw, axis=1, keepdims=True)
            attended = (raw * lax.rsqrt(power + 1e-06) * gain_ref[:, cols]).astype(BF16)
            centered_ref[here, cols] = attended
            wide = attended.astype(F32).reshape(SPAN // 8, 8, HEAD_DIM)
            sums[8:16, cols] = jnp.maximum(sums[8:16, cols], jnp.max(wide, axis=0))
            sums[16:24, cols] = jnp.minimum(sums[16:24, cols], jnp.min(wide, axis=0))
    sums[0:8, :] += dot(jnp.ones((8, SPAN), BF16), centered_ref[here, :])

    @pl.when(step == blocks - 1)
    def _():
        mean = sums[0:1, :] / count
        first, rest = split(mean)
        rest = mean - first.astype(F32)
        second, third = split(rest)
        top = jnp.max(sums[8:16, :], axis=0, keepdims=True)
        bottom = jnp.min(sums[16:24, :], axis=0, keepdims=True)
        lines = [first.astype(F32), second.astype(F32), third.astype(F32), top, bottom]
        lines.append(jnp.zeros((11, width), F32))
        stats_ref[...] = jnp.concatenate(lines, axis=0).astype(BF16)

        @pl.loop(0, count // 128)
        def _(index):
            part = pl.ds(pl.multiple_of(index * 128, 128), 128)
            centered_ref[part, :] = (centered_ref[part, :].astype(F32) - mean).astype(BF16)


def finish(queries, raw, entering, before, log_decay, gain, pieces):
    count, width = queries.shape
    heads = width // HEAD_DIM
    shards = len(pieces)
    tokens = pl.BlockSpec((SPAN, width), lambda i: (i, 0))
    return pl.pallas_call(
        functools.partial(finish_kernel, shards),
        grid=(count // SPAN,),
        in_specs=[
            tokens,
            tokens,
            pl.BlockSpec((1, width, HEAD_DIM), lambda i: (i, 0, 0)),
            pl.BlockSpec((1, heads, HEAD_DIM), lambda i: (i, 0, 0)),
            pl.BlockSpec((heads, SPAN), lambda i: (0, i)),
            whole((1, width)),
        ]
        + [whole(pieces[0].shape)] * shards,
        out_specs=[whole((count, width)), whole((16, width))],
        scratch_shapes=[pltpu.VMEM((width, HEAD_DIM), F32), pltpu.VMEM((24, width), F32)],
        out_shape=[struct((count, width), BF16), struct((16, width), BF16)],
        compiler_params=params(32),
        cost_estimate=cost(4 * count * width * HEAD_DIM, 10 * count * width),
        name="finish",
    )(queries, raw, entering, before, log_decay, gain, *pieces)


def places(count, inner, bit):
    return [
        (outer * 2 + bit) * inner + index
        for outer in range(count // inner // 2)
        for index in range(inner)
    ]


def gram_kernel(rows, ranges, apart, own_ref, other_ref, *rest):
    keep_ref, send_ref = rest[-2:]
    width = own_ref.shape[1]
    shards = width // rows
    bit = (lax.axis_index("ctx") // apart) % 2
    if len(rest) > 3:
        send_ref[shards // 2 * rows :, :] = rest[0][...]

    def fill(out_ref, blocks):
        for index, block in enumerate(blocks):
            line = slice(index * rows, (index + 1) * rows)
            left = own_ref[:, block * rows : (block + 1) * rows].T
            place = 0
            for begin, end in ranges:
                begin, end = (block + begin) * rows, (block + end) * rows
                for ref, low in ((own_ref, 0), (other_ref, width)):
                    first, last = max(begin - low, 0), min(end - low, width)
                    if first < last:
                        out = dot(left, ref[:, first:last]).astype(out_ref.dtype)
                        out_ref[line, place : place + last - first] = out
                        place += last - first

    for mine in range(2):

        @pl.when(bit == mine)
        def _():
            fill(send_ref, places(shards, apart, 1 - mine))
            fill(keep_ref, places(shards, apart, mine))


def gram_parts(own, other, extra, after, rows, ranges, apart):
    count, width = own.shape
    shards = width // rows
    size = sum(end - begin for begin, end in ranges) * rows
    kept = (shards // 2 * rows, size)
    if rows % 128:
        full = lax.dot_general(
            own,
            jnp.concatenate([own, other], axis=1),
            (((0,), (0,)), ((), ())),
            preferred_element_type=F32,
        )
        parts = []
        for shard in range(shards):
            line = full[shard * rows : (shard + 1) * rows]
            slabs = [line[:, (shard + a) * rows : (shard + b) * rows] for a, b in ranges]
            parts.append(jnp.concatenate(slabs, axis=1))
        bit = (lax.axis_index("ctx") // apart) % 2
        parts = jnp.stack(parts).reshape(-1, 2, apart, rows, size)
        keep = lax.dynamic_index_in_dim(parts, bit, 1, False).reshape(kept)
        send = lax.dynamic_index_in_dim(parts, 1 - bit, 1, False).reshape(kept)
        return keep, jnp.concatenate([send.astype(BF16)] + extra)
    sent = (kept[0] + sum(value.shape[0] for value in extra), size)
    return pl.pallas_call(
        functools.partial(gram_kernel, rows, ranges, apart),
        in_specs=[vmem()] * (2 + len(extra)) + [anywhere()],
        out_specs=[vmem(), vmem()],
        out_shape=[struct(kept, F32), struct(sent, BF16)],
        compiler_params=params(16),
        cost_estimate=cost(2 * count * width * size, 4 * count * width),
        name="gram",
    )(own, other, *extra, after)


def fold_kernel(rows, inner, apart, keep_ref, other_ref, *rest):
    kept_ref, send_ref = rest[-2:]
    count = keep_ref.shape[0] // rows
    bit = (lax.axis_index("ctx") // apart) % 2
    if len(rest) > 2:
        extra = rest[0].shape[0]
        low = kept_ref.shape[0]
        send_ref[low : low + extra, :] = rest[0][...]
        send_ref[low + extra :, :] = other_ref[keep_ref.shape[0] :, :]

    for mine in range(2):

        @pl.when(bit == mine)
        def _():
            for out_ref, side in ((send_ref, 1 - mine), (kept_ref, mine)):
                for index, block in enumerate(places(count, inner, side)):
                    line = slice(block * rows, (block + 1) * rows)
                    total = keep_ref[line, :] + other_ref[line, :].astype(F32)
                    out_ref[index * rows : (index + 1) * rows, :] = total.astype(out_ref.dtype)


def fold(keep, other, extra, rows, inner, apart):
    kept = (keep.shape[0] // 2, keep.shape[1])
    sent = (kept[0] + 2 * sum(value.shape[0] for value in extra), kept[1])
    return pl.pallas_call(
        functools.partial(fold_kernel, rows, inner, apart),
        in_specs=[vmem()] * (2 + len(extra)),
        out_specs=[vmem(), vmem()],
        out_shape=[struct(kept, F32), struct(sent, BF16)],
        compiler_params=params(16),
        name="fold",
    )(keep, other, *extra)


def close_kernel(rows, columns, keep_ref, other_ref, total_ref, *slab_refs):
    total = keep_ref[...] + other_ref[:rows, :].astype(F32)
    total_ref[...] = total
    for column, slab_ref in zip(columns, slab_refs):
        slab_ref[...] = total[:, column * rows : (column + 1) * rows].astype(BF16)


def close(keep, other, rows, columns):
    out = pl.pallas_call(
        functools.partial(close_kernel, rows, columns),
        in_specs=[vmem(), vmem()],
        out_specs=[vmem()] * (1 + len(columns)),
        out_shape=[struct(keep.shape, F32)] + [struct((rows, rows), BF16)] * len(columns),
        compiler_params=params(16),
        name="close",
    )(keep, other)
    return out[0], out[1:]


def cover_kernel(rows, shards, total, order, means_ref, others_ref, *refs):
    chunk_count = len(order)
    chunks = refs[:chunk_count]
    mirrors = refs[chunk_count : chunk_count + shards - 1]
    out_ref, spread = refs[chunk_count + shards - 1 :]
    width = rows * shards
    mine, side = lax.axis_index("ctx"), lax.axis_index("head") & 1
    for ref, place in ((means_ref, side), (others_ref, 1 - side)):
        value = ref[...]
        centre = jnp.sum(value, axis=0, keepdims=True) / shards
        spread[:, pl.ds(pl.multiple_of(place * width, width), width)] = value - centre
    block = side * shards + mine
    left = spread[:, pl.ds(pl.multiple_of(block * rows, rows), rows)].T
    count = total // shards
    out_ref[...] = count * jnp.dot(left, spread[...], precision=HIGHEST, preferred_element_type=F32)

    def put(position, gram):
        position = lax.rem(position + 2 * shards, 2 * shards)
        at = pl.ds(pl.multiple_of(position * rows, rows), rows)
        out_ref[:, at] = (out_ref[:, at] + gram) / total

    for chunk, steps in zip(chunks, order):
        for index, step in enumerate(steps):
            put(block + step, chunk[:, index * rows : (index + 1) * rows])
    for index in range(shards - 1):
        put(block - (index + 1), mirrors[index][...].T.astype(F32))


def cover(means, others, chunks, mirrors, order, rows, shards, total):
    width = rows * shards
    if rows % 128:
        mine, side = lax.axis_index("ctx"), lax.axis_index("head") & 1
        pair = [jnp.where(side == 0, means, others), jnp.where(side == 0, others, means)]
        spread = jnp.concatenate(pair, axis=1)
        spread = spread - jnp.mean(spread, axis=0)
        block = side * shards + mine
        left = lax.dynamic_slice_in_dim(spread, block * rows, rows, 1)
        fix = (total // shards) * jnp.dot(left.T, spread, precision=HIGHEST)
        ahead = {}
        for chunk, steps in zip(chunks, order):
            for index, step in enumerate(steps):
                ahead[step] = chunk[:, index * rows : (index + 1) * rows]
        slabs = [mirrors[step - 1].T.astype(F32) for step in range(shards - 1, 0, -1)]
        slabs += [ahead[step] for step in range(shards + 1)]
        line = jnp.roll(jnp.concatenate(slabs, axis=1), (block - (shards - 1)) * rows, axis=1)
        return (line + fix) / total
    return pl.pallas_call(
        functools.partial(cover_kernel, rows, shards, total, order),
        grid=(1,),
        in_specs=[whole(value.shape) for value in (means, others, *chunks, *mirrors)],
        out_specs=whole((rows, 2 * width)),
        scratch_shapes=[pltpu.VMEM((shards, 2 * width), F32)],
        out_shape=struct((rows, 2 * width), F32),
        compiler_params=params(16),
        name="cover",
    )(means, others, *chunks, *mirrors)


def body(queries, keys, values, log_decay, gain):
    count, width = queries.shape
    shards = lax.axis_size("ctx")
    sides = lax.axis_size("head")
    rows = width // shards
    mine = lax.axis_index("ctx")

    def to_shard(value, apart):
        return lax.ppermute(value, "ctx", [(a, a ^ apart) for a in range(shards)])

    def to_partner(value):
        return lax.ppermute(value, "head", [(a, a ^ 1) for a in range(sides)])

    def everywhere(values):
        return [values[0]] + [to_shard(values[k], k) for k in range(1, shards)]

    def forward(value, steps):
        pairs = []
        for shard in range(shards):
            for side in range(sides):
                block = (side % 2) * shards + shard + steps
                other = (block // shards) % 2
                target = (block % shards) * sides + (side // 2) * 2 + other
                pairs.append((shard * sides + side, target))
        return lax.ppermute(value, ("ctx", "head"), pairs)

    entering, before, pieces = local_states(keys, values, log_decay, shards)
    arrived = everywhere(pieces)
    raw = inner(queries, keys, values, log_decay)
    entry = everywhere(chain(arrived, raw))
    centered, stats = finish(
        queries, raw, entering, before, log_decay, gain.reshape(1, width), entry
    )
    partner = to_partner(centered)

    half = shards // 2
    lines = half * rows
    packed = -(-5 * width // lines)
    padded = packed + -packed % 16
    extra = jnp.pad(stats[:5].reshape(packed, lines), ((0, padded - packed), (0, 0)))
    bits = [1 << place for place in range(shards.bit_length() - 1)]
    plans = [
        (tuple(range(1, half + 1)), ((1, half + 1),), bits),
        ((shards, 0), ((shards, shards + 1), (0, 1)), bits[1:] + bits[:1]),
        (tuple(range(half + 1, shards)), ((half + 1, shards),), bits),
    ]
    order = [steps for steps, _, _ in plans]
    kept, riders, after = [], [extra], stats
    for steps, ranges, turns in plans:
        keep, send = gram_parts(
            centered, partner, riders if not kept else [], after, rows, ranges, turns[0]
        )
        after = keep
        kept.append((keep, to_shard(send, turns[0])))
    chunks, mirrors = [], [None] * (shards - 1)
    for (steps, ranges, turns), (keep, other) in zip(plans, kept):
        first = not chunks
        left = bits[:]
        for done, apart in zip(turns, turns[1:]):
            left.remove(done)
            inner_blocks = 1 << left.index(apart)
            gathered = riders if first else []
            low = keep.shape[0]
            keep, send = fold(keep, other, gathered, rows, inner_blocks, apart)
            if first:
                riders = [jnp.concatenate([riders[0], other[low:]])]
            other = to_shard(send, apart)
        if first:
            gathered = jnp.concatenate([riders[0], other[rows:]])
        columns = [index for index, step in enumerate(steps) if 0 < step < shards]
        total, slabs = close(keep, other, rows, columns)
        chunks.append(total)
        for column, slab in zip(columns, slabs):
            mirrors[steps[column] - 1] = forward(slab, steps[column])
        if first:
            every = gathered

    every = every.reshape(shards, padded, lines)[:, :packed]
    every = every.reshape(shards, 5, width).astype(F32)
    means = every[:, 0] + every[:, 1] + every[:, 2]
    shift = (jnp.max(every[:, 3], axis=0) + jnp.min(every[:, 4], axis=0)) / 2.0
    others = to_partner(means)
    covariance = cover(means, others, chunks, mirrors, order, rows, shards, count * shards)
    return (shift, covariance)


def solution(mesh):
    placed = (P("ctx", "head"), P("ctx", "head"), P("ctx", "head"), P("head", "ctx"), P("head"))
    return jax.shard_map(
        body,
        mesh=mesh,
        in_specs=placed,
        out_specs=(P("head"), P(("head", "ctx"), None)),
        check_vma=False,
    )
```

```python
import functools

import jax
import jax.numpy as jnp
from jax import lax
from jax.experimental import pallas as pl
from jax.experimental.pallas import tpu as pltpu
from jax.sharding import PartitionSpec as P

HEAD_DIM = 128
SPAN = 256
F32 = jnp.float32
BF16 = jnp.bfloat16
HIGHEST = lax.Precision.HIGHEST
MIB = 1 << 20


def params(limit_mib):
    return pltpu.CompilerParams(vmem_limit_bytes=limit_mib * MIB)


def cost(flops, moved, transcendentals=0):
    return pl.CostEstimate(
        flops=int(flops), bytes_accessed=int(moved), transcendentals=int(transcendentals)
    )


def whole(shape):
    return pl.BlockSpec(shape, lambda *_: (0,) * len(shape))


def anywhere():
    return pl.BlockSpec(memory_space=pl.ANY)


def vmem():
    return pl.BlockSpec(memory_space=pltpu.VMEM)


def struct(shape, dtype):
    return jax.ShapeDtypeStruct(shape, dtype)


def dot(a, b):
    return jnp.dot(a, b, preferred_element_type=F32)


def split(value):
    high = value.astype(BF16)
    return high, (value - high.astype(F32)).astype(BF16)


def running_sum(decay):
    rows = lax.broadcasted_iota(jnp.int32, (SPAN, SPAN), 0)
    columns = lax.broadcasted_iota(jnp.int32, (SPAN, SPAN), 1)
    ones = jnp.where(rows <= columns, 1.0, 0.0).astype(F32)
    return jnp.dot(decay, ones, precision=HIGHEST, preferred_element_type=F32)


def head_columns(head):
    return slice(head * HEAD_DIM, (head + 1) * HEAD_DIM)


def states_kernel(near, k_ref, v_ref, decay_ref, entering_ref, before_ref, *rest):
    pieces, (state, total) = rest[:near], rest[near:]
    heads = decay_ref.shape[0]
    step = pl.program_id(0)

    @pl.when(step == 0)
    def _():
        state[...] = jnp.zeros_like(state)
        total[...] = jnp.ones_like(total)

    entering_ref[0] = state[...]
    before_ref[0] = total[...]
    cumul = running_sum(decay_ref[...])
    last = cumul[:, SPAN - 1 :]
    weight = jnp.exp(last - cumul)
    drop = jnp.exp(last)
    for group in range(0, heads, 4):
        members = range(group, min(group + 4, heads))
        turned = [k_ref[:, head_columns(head)].T for head in members]
        parts = []
        for head, key in zip(members, turned):
            high, low = split(key.astype(F32) * weight[head : head + 1, :])
            parts.append(jnp.concatenate([high, low], axis=0))
        updates = [dot(part, v_ref[:, head_columns(head)]) for head, part in zip(members, parts)]
        for head, update in zip(members, updates):
            cols = head_columns(head)
            update = update[:HEAD_DIM] + update[HEAD_DIM:]
            state[cols, :] = state[cols, :] * drop[head : head + 1, :] + update
    total[...] = total[...] * drop

    @pl.when(step == pl.num_programs(0) - 1)
    def _():
        mine = lax.axis_index("ctx") % near
        rows = heads * HEAD_DIM // near
        for apart in range(near):
            start = pl.multiple_of((mine ^ apart) * rows, rows)
            pieces[apart][:rows, :] = state[pl.ds(start, rows), :]
            pieces[apart][rows:, :] = jnp.zeros((8, HEAD_DIM), F32)
            for head in range(rows // HEAD_DIM):
                line = total[pl.ds(start // HEAD_DIM + head, 1), :]
                pieces[apart][rows + head : rows + head + 1, :] = line


def local_states(keys, values, log_decay, near):
    count, width = keys.shape
    heads = width // HEAD_DIM
    blocks = count // SPAN
    rows = width // near
    piece = (rows + 8, HEAD_DIM)
    shapes = [(blocks, width, HEAD_DIM), (blocks, heads, HEAD_DIM)] + [piece] * near
    tokens = pl.BlockSpec((SPAN, width), lambda i: (i, 0))
    out = pl.pallas_call(
        functools.partial(states_kernel, near),
        grid=(blocks,),
        in_specs=[tokens, tokens, pl.BlockSpec((heads, SPAN), lambda i: (0, i))],
        out_specs=[
            pl.BlockSpec((1, width, HEAD_DIM), lambda i: (i, 0, 0)),
            pl.BlockSpec((1, heads, HEAD_DIM), lambda i: (i, 0, 0)),
        ]
        + [whole(piece)] * near,
        scratch_shapes=[pltpu.VMEM((width, HEAD_DIM), F32), pltpu.VMEM((heads, HEAD_DIM), F32)],
        out_shape=[struct(shape, F32) for shape in shapes],
        compiler_params=params(56),
        cost_estimate=cost(4 * count * width * HEAD_DIM, 4 * count * width),
        name="local_states",
    )(keys, values, log_decay)
    return out[0], out[1], out[2:]


def chain_kernel(near, *refs):
    arrived, (inside_ref, left_ref, leaving_ref, ordered) = refs[:near], refs[near:]
    mine = lax.axis_index("ctx") % near
    rows = leaving_ref.shape[0]
    heads = rows // HEAD_DIM
    for apart in range(near):
        ordered[mine ^ apart] = arrived[apart][...]
    left_ref[...] = jnp.zeros_like(left_ref)
    for head in range(heads):
        cols = head_columns(head)
        carried = jnp.zeros((HEAD_DIM, HEAD_DIM), F32)
        left = jnp.ones((1, HEAD_DIM), F32)
        for shard in range(near):
            inside_ref[shard, cols, :] = carried
            left_ref[shard, head : head + 1, :] = left
            drop = ordered[shard, rows + head : rows + head + 1, :]
            carried = carried * drop + ordered[shard, cols, :]
            left = left * drop
        leaving_ref[cols, :] = carried


def chain(pieces):
    near = len(pieces)
    rows = pieces[0].shape[0] - 8
    shapes = [(near, rows, HEAD_DIM), (near, 8, HEAD_DIM), (rows, HEAD_DIM)]
    return pl.pallas_call(
        functools.partial(chain_kernel, near),
        in_specs=[vmem()] * near,
        out_specs=[vmem()] * 3,
        out_shape=[struct(shape, F32) for shape in shapes],
        scratch_shapes=[pltpu.VMEM((near, rows + 8, HEAD_DIM), F32)],
        compiler_params=params(16),
        name="chain",
    )(*pieces)


def spread_kernel(inside_ref, left_ref, entered_ref, _, *outs):
    near, rows, _ = inside_ref.shape
    mine = lax.axis_index("ctx") % near
    for apart, out_ref in enumerate(outs):
        shard = mine ^ apart
        left = left_ref[shard]
        for head in range(rows // HEAD_DIM):
            cols = head_columns(head)
            part = entered_ref[cols, :] * left[head : head + 1, :]
            out_ref[cols, :] = inside_ref[shard, cols, :] + part


def spread_states(inside, left, entered, after):
    near, rows, _ = inside.shape
    return pl.pallas_call(
        spread_kernel,
        in_specs=[vmem()] * 3 + [anywhere()],
        out_specs=[vmem()] * near,
        out_shape=[struct((rows, HEAD_DIM), F32)] * near,
        compiler_params=params(16),
        name="spread_states",
    )(inside, left, entered, after)


def inner_kernel(q_ref, k_ref, v_ref, decay_ref, raw_ref):
    heads = decay_ref.shape[0]
    cumul = running_sum(decay_ref[...])
    columns = cumul.T
    half = SPAN // 2
    for part in range(2):
        rows = slice(part * half, (part + 1) * half)
        width = (part + 1) * half
        token = lax.broadcasted_iota(jnp.int32, (half, width), 0) + part * half
        earlier = lax.broadcasted_iota(jnp.int32, (half, width), 1)
        for group in range(0, heads, 4):
            members = range(group, min(group + 4, heads))
            scores = [
                lax.dot_general(
                    q_ref[rows, head_columns(head)],
                    k_ref[:width, head_columns(head)],
                    (((1,), (1,)), ((), ())),
                    preferred_element_type=F32,
                )
                for head in members
            ]
            weights = []
            for head, score in zip(members, scores):
                diff = columns[rows, head : head + 1] - cumul[head : head + 1, :width]
                factor = jnp.exp(jnp.where(token >= earlier, diff, -jnp.inf))
                weights.append((score * factor).astype(BF16))
            for head, weight in zip(members, weights):
                cols = head_columns(head)
                raw_ref[rows, cols] = dot(weight, v_ref[:width, cols])


def inner(queries, keys, values, log_decay):
    count, width = keys.shape
    heads = width // HEAD_DIM
    tokens = pl.BlockSpec((SPAN, width), lambda i: (i, 0))
    return pl.pallas_call(
        inner_kernel,
        grid=(count // SPAN,),
        in_specs=[tokens, tokens, tokens, pl.BlockSpec((heads, SPAN), lambda i: (0, i))],
        out_specs=tokens,
        out_shape=struct((count, width), F32),
        compiler_params=params(24),
        cost_estimate=cost(4 * count * width * SPAN, 10 * count * width, count * heads * SPAN),
        name="inner",
    )(queries, keys, values, log_decay)


def finish_kernel(
    near, q_ref, raw_ref, entering_ref, before_ref, decay_ref, gain_ref, *rest
):
    pieces, (centered_ref, stats_ref, arrived, sums) = rest[:near], rest[near:]
    heads = decay_ref.shape[0]
    width = heads * HEAD_DIM
    rows = width // near
    step = pl.program_id(0)
    blocks = pl.num_programs(0)
    count = centered_ref.shape[0]

    @pl.when(step == 0)
    def _():
        mine = lax.axis_index("ctx") % near
        for apart in range(near):
            start = pl.multiple_of((mine ^ apart) * rows, rows)
            arrived[pl.ds(start, rows), :] = pieces[apart][...]
        sums[0:8, :] = jnp.zeros((8, width), F32)
        sums[8:16, :] = jnp.full((8, width), -jnp.inf, F32)
        sums[16:24, :] = jnp.full((8, width), jnp.inf, F32)

    factor = jnp.exp(running_sum(decay_ref[...])).T
    here = pl.ds(pl.multiple_of(step * SPAN, SPAN), SPAN)
    for group in range(0, heads, 4):
        members = range(group, min(group + 4, heads))
        outers = []
        for head in members:
            cols = head_columns(head)
            state = entering_ref[0, cols, :] + before_ref[0, head : head + 1, :] * arrived[cols, :]
            query = q_ref[:, cols]
            outers.append(
                dot(
                    jnp.concatenate([query, query], axis=1),
                    jnp.concatenate(split(state), axis=0),
                )
            )
        for head, outer in zip(members, outers):
            cols = head_columns(head)
            raw = raw_ref[:, cols] + outer * factor[:, head : head + 1]
            power = jnp.mean(raw * raw, axis=1, keepdims=True)
            attended = (raw * lax.rsqrt(power + 1e-06) * gain_ref[:, cols]).astype(BF16)
            centered_ref[here, cols] = attended
            wide = attended.astype(F32).reshape(SPAN // 8, 8, HEAD_DIM)
            sums[8:16, cols] = jnp.maximum(sums[8:16, cols], jnp.max(wide, axis=0))
            sums[16:24, cols] = jnp.minimum(sums[16:24, cols], jnp.min(wide, axis=0))
    sums[0:8, :] += dot(jnp.ones((8, SPAN), BF16), centered_ref[here, :])

    @pl.when(step == blocks - 1)
    def _():
        mean = sums[0:1, :] / count
        first, rest = split(mean)
        rest = mean - first.astype(F32)
        second, third = split(rest)
        top = jnp.max(sums[8:16, :], axis=0, keepdims=True)
        bottom = jnp.min(sums[16:24, :], axis=0, keepdims=True)
        lines = [first.astype(F32), second.astype(F32), third.astype(F32), top, bottom]
        lines.append(jnp.zeros((11, width), F32))
        stats_ref[...] = jnp.concatenate(lines, axis=0).astype(BF16)

        @pl.loop(0, count // 128)
        def _(index):
            part = pl.ds(pl.multiple_of(index * 128, 128), 128)
            centered_ref[part, :] = (centered_ref[part, :].astype(F32) - mean).astype(BF16)


def finish(queries, raw, entering, before, log_decay, gain, pieces):
    count, width = queries.shape
    heads = width // HEAD_DIM
    near = len(pieces)
    tokens = pl.BlockSpec((SPAN, width), lambda i: (i, 0))
    return pl.pallas_call(
        functools.partial(finish_kernel, near),
        grid=(count // SPAN,),
        in_specs=[
            tokens,
            tokens,
            pl.BlockSpec((1, width, HEAD_DIM), lambda i: (i, 0, 0)),
            pl.BlockSpec((1, heads, HEAD_DIM), lambda i: (i, 0, 0)),
            pl.BlockSpec((heads, SPAN), lambda i: (0, i)),
            whole((1, width)),
        ]
        + [whole(pieces[0].shape)] * near,
        out_specs=[whole((count, width)), whole((16, width))],
        scratch_shapes=[pltpu.VMEM((width, HEAD_DIM), F32), pltpu.VMEM((24, width), F32)],
        out_shape=[struct((count, width), BF16), struct((16, width), BF16)],
        compiler_params=params(32),
        cost_estimate=cost(4 * count * width * HEAD_DIM, 10 * count * width),
        name="finish",
    )(queries, raw, entering, before, log_decay, gain, *pieces)


def places(count, inner, bit):
    return [
        (outer * 2 + bit) * inner + index
        for outer in range(count // inner // 2)
        for index in range(inner)
    ]


def side_of(side, block, shards):
    return side if side < 2 else (0 if block < shards // 2 else 1)


def gram_kernel(rows, blocks, apart, own_ref, other_ref, *rest):
    keep_ref, send_ref, turned = rest[-3:]
    width = own_ref.shape[1]
    shards = width // rows
    steps = sorted({step for step, _ in blocks})
    bit = (lax.axis_index("ctx") // apart) % 2
    if len(rest) > 4:
        send_ref[shards // 2 * rows :, :] = rest[0][...]
    for start in range(0, turned.shape[0], HEAD_DIM):
        here = start % width
        turned[start : start + HEAD_DIM, :] = own_ref[:, here : here + HEAD_DIM].T

    def fill(out_ref, row_blocks):
        for index, block in enumerate(row_blocks):
            line = slice(index * rows, (index + 1) * rows)
            here = slice(block * rows, (block + 1) * rows)
            left = turned[(block + steps[0]) * rows : (block + steps[-1] + 1) * rows, :]
            right = jnp.concatenate([own_ref[:, here], other_ref[:, here]], axis=1)
            out = dot(left, right).astype(out_ref.dtype)
            for place, (step, side) in enumerate(blocks):
                low = (step - steps[0]) * rows
                first = side_of(side, block, shards) * rows
                target = slice(place * rows, (place + 1) * rows)
                out_ref[line, target] = out[low : low + rows, first : first + rows]

    for mine in range(2):

        @pl.when(bit == mine)
        def _():
            fill(send_ref, places(shards, apart, 1 - mine))
            fill(keep_ref, places(shards, apart, mine))


def gram_parts(own, other, extra, after, rows, blocks, apart):
    count, width = own.shape
    shards = width // rows
    size = len(blocks) * rows
    kept = (shards // 2 * rows, size)
    if rows % 128:
        full = [
            lax.dot_general(own, side, (((0,), (0,)), ((), ())), preferred_element_type=F32)
            for side in (own, other)
        ]
        parts = []
        for shard in range(shards):
            slabs = []
            for step, side in blocks:
                at = (shard + step) % shards * rows
                value = full[side_of(side, shard, shards)]
                slabs.append(value[at : at + rows, shard * rows : (shard + 1) * rows])
            parts.append(jnp.concatenate(slabs, axis=1))
        bit = (lax.axis_index("ctx") // apart) % 2
        parts = jnp.stack(parts).reshape(-1, 2, apart, rows, size)
        keep = lax.dynamic_index_in_dim(parts, bit, 1, False).reshape(kept)
        send = lax.dynamic_index_in_dim(parts, 1 - bit, 1, False).reshape(kept)
        return keep, jnp.concatenate([send.astype(BF16)] + extra)
    sent = (kept[0] + sum(value.shape[0] for value in extra), size)
    return pl.pallas_call(
        functools.partial(gram_kernel, rows, blocks, apart),
        in_specs=[vmem()] * (2 + len(extra)) + [anywhere()],
        out_specs=[vmem(), vmem()],
        scratch_shapes=[pltpu.VMEM((width + max(step for step, _ in blocks) * rows, count), BF16)],
        out_shape=[struct(kept, F32), struct(sent, BF16)],
        compiler_params=params(16),
        cost_estimate=cost(2 * count * width * size, 4 * count * width),
        name="gram",
    )(own, other, *extra, after)


def merge(first, second, means):
    a, b = first.astype(F32), second.astype(F32)
    top, bottom = slice(means, means + 2), slice(means + 2, means + 4)
    lines = [a[:means], b[:means], jnp.maximum(a[top], b[top]), jnp.minimum(a[bottom], b[bottom])]
    spare = -(2 * means + 4) % 16
    if spare:
        lines.append(jnp.zeros((spare, a.shape[1]), F32))
    return jnp.concatenate(lines, axis=0).astype(BF16)


def fold_kernel(rows, inner, apart, means, keep_ref, other_ref, _, *rest):
    count = keep_ref.shape[0] // rows
    bit = (lax.axis_index("ctx") // apart) % 2
    if means:
        riders_ref, kept_ref, send_ref, merged_ref = rest
        merged = merge(riders_ref[...], other_ref[keep_ref.shape[0] :, :], means)
        send_ref[kept_ref.shape[0] :, :] = merged
        merged_ref[...] = merged
    else:
        kept_ref, send_ref = rest

    for mine in range(2):

        @pl.when(bit == mine)
        def _():
            for out_ref, side in ((send_ref, 1 - mine), (kept_ref, mine)):
                for index, block in enumerate(places(count, inner, side)):
                    line = slice(block * rows, (block + 1) * rows)
                    total = keep_ref[line, :] + other_ref[line, :].astype(F32)
                    out_ref[index * rows : (index + 1) * rows, :] = total.astype(out_ref.dtype)


def fold(keep, other, after, riders, means, rows, inner, apart):
    kept = (keep.shape[0] // 2, keep.shape[1])
    shapes = [struct(kept, F32), struct(kept, BF16)]
    if riders:
        merged = (2 * means + 4 + -(2 * means + 4) % 16, kept[1])
        shapes = [struct(kept, F32), struct((kept[0] + merged[0], kept[1]), BF16)]
        shapes.append(struct(merged, BF16))
    return pl.pallas_call(
        functools.partial(fold_kernel, rows, inner, apart, means if riders else 0),
        in_specs=[vmem()] * 2 + [anywhere()] + [vmem()] * len(riders),
        out_specs=[vmem()] * len(shapes),
        out_shape=shapes,
        compiler_params=params(16),
        name="fold",
    )(keep, other, after, *riders)


def close_kernel(rows, runs, waits, keep_ref, other_ref, *rest):
    total_ref, slab_refs = rest[waits], rest[waits + 1 :]
    total = keep_ref[...] + other_ref[:rows, :].astype(F32)
    total_ref[...] = total
    for run, slab_ref in zip(runs, slab_refs):
        for place, column in enumerate(run):
            slab = total[:, column * rows : (column + 1) * rows].astype(BF16)
            slab_ref[:, place * rows : (place + 1) * rows] = slab


def close(keep, other, after, rows, runs):
    out = pl.pallas_call(
        functools.partial(close_kernel, rows, runs, len(after)),
        in_specs=[vmem(), vmem()] + [anywhere()] * len(after),
        out_specs=[vmem()] * (1 + len(runs)),
        out_shape=[struct(keep.shape, F32)] + [struct((rows, len(run) * rows), BF16) for run in runs],
        compiler_params=params(16),
        name="close",
    )(keep, other, *after)
    return out[0], out[1:]


def assemble(put, upper, shards, chunks, mirrors, crossed):
    half = shards // 2
    put(0, 0, chunks[(0, 0)])
    put(0, 1, chunks[(0, 1)])
    for step in range(1, half):
        put(step, 0, chunks[(step, 0)].T)
        put(step, 1, crossed[step].T)
        put(-step, 0, mirrors[(step, 0)])
        put(-step, 1, mirrors[(step, 1)])
    last = jnp.where(upper, crossed[half].astype(F32), chunks[(half, 2)])
    put(half, upper, last.T)
    put(half, 1 - upper, mirrors[(half, 2)])


def pick(rows, names, values):
    out = {}
    for blocks, value in zip(names, values):
        for place, name in enumerate(blocks):
            out[name] = value[:, place * rows : (place + 1) * rows]
    return out


def cover_kernel(rows, shards, total, names, means_ref, others_ref, *refs):
    out_ref, spread = refs[-2:]
    width = rows * shards
    mine, side = lax.axis_index("ctx"), lax.axis_index("head") & 1
    for ref, place in ((means_ref, side), (others_ref, 1 - side)):
        value = ref[...]
        centre = jnp.sum(value, axis=0, keepdims=True) / shards
        spread[:, pl.ds(pl.multiple_of(place * width, width), width)] = value - centre
    own = pl.multiple_of((side * shards + mine) * rows, rows)
    left = spread[:, pl.ds(own, rows)].T
    count = total // shards
    out_ref[...] = count * jnp.dot(left, spread[...], precision=HIGHEST, preferred_element_type=F32)

    def put(step, flip, gram):
        shard = lax.rem(mine + step + shards, shards)
        at = pl.ds(pl.multiple_of(((side ^ flip) * shards + shard) * rows, rows), rows)
        out_ref[:, at] = (out_ref[:, at] + gram.astype(F32)) / total

    values = iter(refs[:-2])
    parts = [pick(rows, group, [next(values) for _ in group]) for group in names]
    assemble(put, jnp.where(mine >= shards // 2, 1, 0), shards, *parts)


def cover(means, others, groups, names, rows, shards, total):
    width = rows * shards
    values = [value for group in groups for value in group]
    if rows % 128:
        mine, side = lax.axis_index("ctx"), lax.axis_index("head") & 1
        pair = [jnp.where(side == 0, means, others), jnp.where(side == 0, others, means)]
        spread = jnp.concatenate(pair, axis=1)
        spread = spread - jnp.mean(spread, axis=0)
        left = lax.dynamic_slice_in_dim(spread, (side * shards + mine) * rows, rows, 1)
        out = [(total // shards) * jnp.dot(left.T, spread, precision=HIGHEST)]

        def put(step, flip, gram):
            shard = lax.rem(mine + step + shards, shards)
            at = ((side ^ flip) * shards + shard) * rows
            old = lax.dynamic_slice_in_dim(out[0], at, rows, 1)
            new = (old + gram.astype(F32)) / total
            out[0] = lax.dynamic_update_slice_in_dim(out[0], new, at, 1)

        parts = [pick(rows, *pair) for pair in zip(names, groups)]
        assemble(put, jnp.where(mine >= shards // 2, 1, 0), shards, *parts)
        return out[0]
    return pl.pallas_call(
        functools.partial(cover_kernel, rows, shards, total, names),
        in_specs=[vmem()] * (2 + len(values)),
        out_specs=vmem(),
        scratch_shapes=[pltpu.VMEM((shards, 2 * width), F32)],
        out_shape=struct((rows, 2 * width), F32),
        compiler_params=params(16),
        name="cover",
    )(means, others, *values)


def body(queries, keys, values, log_decay, gain):
    count, width = queries.shape
    shards = lax.axis_size("ctx")
    sides = lax.axis_size("head")
    rows = width // shards
    mine = lax.axis_index("ctx")

    def to_shard(value, apart):
        return lax.ppermute(value, "ctx", [(a, a ^ apart) for a in range(shards)])

    def to_partner(value):
        return lax.ppermute(value, "head", [(a, a ^ 1) for a in range(sides)])

    near = shards // 2

    def nearby(values):
        return [values[0]] + [to_shard(values[apart], apart) for apart in range(1, near)]

    def forward(value, step):
        return lax.ppermute(value, "ctx", [(a, (a + step) % shards) for a in range(shards)])

    entering, before, pieces = local_states(keys, values, log_decay, near)
    inside, left, leaving = chain(nearby(pieces))
    entered = lax.ppermute(leaving, "ctx", [(a, a + near) for a in range(near)])
    raw = inner(queries, keys, values, log_decay)
    entry = nearby(spread_states(inside, left, entered, raw))
    centered, stats = finish(
        queries, raw, entering, before, log_decay, gain.reshape(1, width), entry
    )
    partner = to_partner(centered)

    half = shards // 2
    lines = half * rows
    mean_rows = 3 * width // lines
    extra = stats[:5].reshape(mean_rows + 4, lines)
    extra = jnp.pad(extra, ((0, -extra.shape[0] % 16), (0, 0)))
    bits = [1 << place for place in range(shards.bit_length() - 1)]
    near = range(1, half // 2 + 1)
    far = range(half // 2 + 1, half)
    plans = [
        ([(step, side) for step in near for side in (0, 1)], bits),
        ([(0, 0), (0, 1)], bits[1:] + bits[:1]),
        ([(step, side) for step in far for side in (0, 1)] + [(half, 2)], bits),
    ]
    kept, riders, after = [], [extra], stats
    for blocks, turns in plans:
        keep, send = gram_parts(
            centered, partner, [] if kept else riders, after, rows, blocks, turns[0]
        )
        after = keep
        kept.append((keep, to_shard(send, turns[0])))
    def split_on(index, after):
        keep, other = kept[index]
        turns = plans[index][1]
        stage = stages[index]
        left = [bit for bit in bits if bit not in turns[:stage]]
        inner_blocks = 1 << left.index(turns[stage])
        carried = riders if index == 0 else []
        keep, send, *merged = fold(
            keep, other, after, carried, mean_rows << (stage - 1), rows, inner_blocks, turns[stage]
        )
        riders[:] = merged or riders
        kept[index] = (keep, to_shard(send, turns[stage]))
        stages[index] += 1
        return keep

    stages = [1] * len(plans)
    after = kept[0][0]
    for stage in range(1, len(bits)):
        for index in (1, 0, 2):
            after = split_on(index, after)

    chunks, mirrors, mirror_names, crossed, crossed_names = [None] * len(plans), [], [], [], []
    for index in (0, 1, 2):
        blocks, (keep, other) = plans[index][0], kept[index]
        if index == 0:
            every = merge(riders[0], other[rows:], mean_rows * half)
        steps = sorted({step for step, _ in blocks} - {0})
        runs = [[i for i, block in enumerate(blocks) if block[0] == step] for step in steps]
        crossing = [i for i, (step, side) in enumerate(blocks) if step and side]
        earlier = mirrors + crossed if index == 2 else []
        total, slabs = close(keep, other, earlier, rows, runs + [crossing] * bool(crossing))
        chunks[index] = total
        for step, run, slab in zip(steps, runs, slabs):
            mirrors.append(forward(slab, step))
            mirror_names.append([blocks[i] for i in run])
        if crossing:
            crossed.append(to_partner(slabs[-1]))
            crossed_names.append([blocks[i][0] for i in crossing])

    every = every.astype(F32)
    means = jnp.sum(every[: mean_rows * shards].reshape(shards, 3, width), axis=1)
    extremes = every[mean_rows * shards :][:4].reshape(2, width)
    shift = (extremes[0] + extremes[1]) / 2.0
    others = to_partner(means)
    covariance = cover(
        means,
        others,
        (chunks, mirrors, crossed),
        ([blocks for blocks, _ in plans], mirror_names, crossed_names),
        rows,
        shards,
        count * shards,
    )
    return (shift, covariance)


def solution(mesh):
    placed = (P("ctx", "head"), P("ctx", "head"), P("ctx", "head"), P("head", "ctx"), P("head"))
    return jax.shard_map(
        body,
        mesh=mesh,
        in_specs=placed,
        out_specs=(P("head"), P(("head", "ctx"), None)),
        check_vma=False,
    )
```

```python
import functools
import math

import jax
import jax.numpy as jnp
from jax import lax
from jax.experimental import pallas as pl
from jax.experimental.pallas import tpu as pltpu
from jax.sharding import PartitionSpec as P

HEAD_DIM = 128
SPAN = 256
F32 = jnp.float32
BF16 = jnp.bfloat16
HIGHEST = lax.Precision.HIGHEST
MIB = 1 << 20


def params(limit_mib):
    return pltpu.CompilerParams(vmem_limit_bytes=limit_mib * MIB)


def cost(flops, moved, transcendentals=0):
    return pl.CostEstimate(
        flops=int(flops), bytes_accessed=int(moved), transcendentals=int(transcendentals)
    )


def whole(shape):
    return pl.BlockSpec(shape, lambda *_: (0,) * len(shape))


def anywhere():
    return pl.BlockSpec(memory_space=pl.ANY)


def vmem():
    return pl.BlockSpec(memory_space=pltpu.VMEM)


def hbm():
    return pl.BlockSpec(memory_space=pltpu.HBM)


def struct(shape, dtype):
    return jax.ShapeDtypeStruct(shape, dtype)


def dot(a, b):
    return jnp.dot(a, b, preferred_element_type=F32)


def split(value):
    high = value.astype(BF16)
    return high, (value - high.astype(F32)).astype(BF16)


def running_sum(decay):
    rows = lax.broadcasted_iota(jnp.int32, (SPAN, SPAN), 0)
    columns = lax.broadcasted_iota(jnp.int32, (SPAN, SPAN), 1)
    ones = jnp.where(rows <= columns, 1.0, 0.0).astype(F32)
    return jnp.dot(decay, ones, precision=HIGHEST, preferred_element_type=F32)


def span_at(first, start=0, size=SPAN):
    if isinstance(first, int):
        return slice(first + start, first + start + size)
    return pl.ds(pl.multiple_of(first + start, math.gcd(start, SPAN)), size)


def lines_at(ref, index, blocks):
    heads = ref.shape[0] // blocks
    return pl.ds(pl.multiple_of(index * heads, heads), heads)


def fits(count, width):
    return count * width <= 1 << 20


def widen(value):
    heads = value.shape[0]
    first, rest = split(value)
    second, third = split(value - first.astype(F32))
    rows = lax.broadcasted_iota(jnp.int32, (heads, heads * HEAD_DIM), 0)
    columns = lax.broadcasted_iota(jnp.int32, (heads, heads * HEAD_DIM), 1)
    ones = jnp.where(columns // HEAD_DIM == rows, 1.0, 0.0)
    pieces = [first.astype(F32), second.astype(F32), third.astype(F32)]
    return lax.dot_general(
        jnp.concatenate(pieces, axis=0).astype(BF16),
        jnp.concatenate([ones] * 3, axis=0).astype(BF16),
        (((0,), (0,)), ((), ())),
        preferred_element_type=F32,
    )


def head_columns(head):
    return slice(head * HEAD_DIM, (head + 1) * HEAD_DIM)


def states_block(k_ref, v_ref, first, cumul, state, total):
    heads = cumul.shape[0]
    last = cumul[:, SPAN - 1 :]
    weight = jnp.exp(last - cumul)
    drop = jnp.exp(last)
    rows = span_at(first)
    for group in range(0, heads, 4):
        members = range(group, min(group + 4, heads))
        turned = [k_ref[rows, head_columns(head)].T for head in members]
        parts = []
        for head, key in zip(members, turned):
            high, low = split(key.astype(F32) * weight[head : head + 1, :])
            parts.append(jnp.concatenate([high, low], axis=0))
        updates = [dot(part, v_ref[rows, head_columns(head)]) for head, part in zip(members, parts)]
        for head, update in zip(members, updates):
            cols = head_columns(head)
            update = update[:HEAD_DIM] + update[HEAD_DIM:]
            state[cols, :] = state[cols, :] * drop[head : head + 1, :] + update
    total[...] = total[...] * drop


def states_out(near, state, total, pieces):
    mine = lax.axis_index("ctx") % near
    rows = state.shape[0] // near
    for apart in range(near):
        start = pl.multiple_of((mine ^ apart) * rows, rows)
        pieces[apart][:rows, :] = state[pl.ds(start, rows), :]
        pieces[apart][rows:, :] = jnp.zeros((8, HEAD_DIM), F32)
        for head in range(rows // HEAD_DIM):
            line = total[pl.ds(start // HEAD_DIM + head, 1), :]
            pieces[apart][rows + head : rows + head + 1, :] = line


def states_kernel(near, k_ref, v_ref, decay_ref, entering_ref, before_ref, cumul_ref, *rest):
    pieces, (state, total) = rest[:near], rest[near:]
    step = pl.program_id(0)

    @pl.when(step == 0)
    def _():
        state[...] = jnp.zeros_like(state)
        total[...] = jnp.ones_like(total)

    entering_ref[0] = state[...]
    before_ref[0] = total[...]
    cumul_ref[...] = running_sum(decay_ref[...])
    states_block(k_ref, v_ref, 0, cumul_ref[...], state, total)

    @pl.when(step == pl.num_programs(0) - 1)
    def _():
        states_out(near, state, total, pieces)


def states_fetch_kernel(near, k_any, v_any, decay_any, entering_ref, before_ref, cumul, *rest):
    pieces, (k_ref, v_ref, decay_ref, state, total, sems) = rest[:near], rest[near:]
    count = k_any.shape[0]
    blocks = count // SPAN
    heads = decay_ref.shape[0]

    def fetch(source, target, index, which):
        rows = span_at(index * SPAN)
        return pltpu.make_async_copy(source.at[rows, :], target.at[rows, :], sems.at[which, index])

    decays = pltpu.make_async_copy(decay_any, decay_ref, sems.at[2, 0])
    decays.start()
    for index in range(blocks):
        fetch(k_any, k_ref, index, 0).start()
        fetch(v_any, v_ref, index, 1).start()
    state[...] = jnp.zeros_like(state)
    total[...] = jnp.ones_like(total)
    decays.wait()
    lines = [decay_ref[:, index * SPAN : (index + 1) * SPAN] for index in range(blocks)]
    cumul[...] = running_sum(jnp.concatenate(lines, axis=0))

    @pl.loop(0, blocks)
    def _(index):
        fetch(k_any, k_ref, index, 0).wait()
        fetch(v_any, v_ref, index, 1).wait()
        entering_ref[index] = state[...]
        before_ref[index] = total[...]
        lines = cumul[pl.ds(pl.multiple_of(index * heads, heads), heads), :]
        states_block(k_ref, v_ref, index * SPAN, lines, state, total)

    states_out(near, state, total, pieces)


def local_states(keys, values, log_decay, near):
    count, width = keys.shape
    heads = width // HEAD_DIM
    blocks = count // SPAN
    rows = width // near
    piece = (rows + 8, HEAD_DIM)
    shapes = [(blocks, width, HEAD_DIM), (blocks, heads, HEAD_DIM), (blocks * heads, SPAN)]
    shapes += [piece] * near
    scratch = [pltpu.VMEM((width, HEAD_DIM), F32), pltpu.VMEM((heads, HEAD_DIM), F32)]
    if fits(count, width):
        kept = [struct(value.shape, value.dtype) for value in (keys, values)]
        out = pl.pallas_call(
            functools.partial(states_fetch_kernel, near),
            in_specs=[hbm()] * 3,
            out_specs=[vmem()] * (len(shapes) + 2),
            out_shape=[struct(shape, F32) for shape in shapes] + kept,
            scratch_shapes=[pltpu.VMEM((heads, count), F32)]
            + scratch
            + [pltpu.SemaphoreType.DMA((3, blocks))],
            compiler_params=params(48),
            cost_estimate=cost(4 * count * width * HEAD_DIM, 4 * count * width),
            name="local_states",
        )(keys, values, log_decay)
        return out[:3], out[3:-2], out[-2:]
    tokens = pl.BlockSpec((SPAN, width), lambda i: (i, 0))
    out = pl.pallas_call(
        functools.partial(states_kernel, near),
        grid=(blocks,),
        in_specs=[tokens, tokens, pl.BlockSpec((heads, SPAN), lambda i: (0, i))],
        out_specs=[
            pl.BlockSpec((1, width, HEAD_DIM), lambda i: (i, 0, 0)),
            pl.BlockSpec((1, heads, HEAD_DIM), lambda i: (i, 0, 0)),
            pl.BlockSpec((heads, SPAN), lambda i: (i, 0)),
        ]
        + [whole(piece)] * near,
        scratch_shapes=scratch,
        out_shape=[struct(shape, F32) for shape in shapes],
        compiler_params=params(56),
        cost_estimate=cost(4 * count * width * HEAD_DIM, 4 * count * width),
        name="local_states",
    )(keys, values, log_decay)
    return out[:3], out[3:], (keys, values)


def chain_kernel(near, *refs):
    arrived, (inside_ref, left_ref, leaving_ref, ordered) = refs[:near], refs[near + 1 :]
    mine = lax.axis_index("ctx") % near
    rows = leaving_ref.shape[0]
    heads = rows // HEAD_DIM
    for apart in range(near):
        ordered[mine ^ apart] = arrived[apart][...]
    left_ref[...] = jnp.zeros_like(left_ref)
    for head in range(heads):
        cols = head_columns(head)
        carried = jnp.zeros((HEAD_DIM, HEAD_DIM), F32)
        left = jnp.ones((1, HEAD_DIM), F32)
        for shard in range(near):
            inside_ref[shard, cols, :] = carried
            left_ref[shard, head : head + 1, :] = left
            drop = ordered[shard, rows + head : rows + head + 1, :]
            carried = carried * drop + ordered[shard, cols, :]
            left = left * drop
        leaving_ref[cols, :] = carried


def chain(pieces, after):
    near = len(pieces)
    rows = pieces[0].shape[0] - 8
    shapes = [(near, rows, HEAD_DIM), (near, 8, HEAD_DIM), (rows, HEAD_DIM)]
    return pl.pallas_call(
        functools.partial(chain_kernel, near),
        in_specs=[vmem()] * near + [anywhere()],
        out_specs=[vmem()] * 3,
        out_shape=[struct(shape, F32) for shape in shapes],
        scratch_shapes=[pltpu.VMEM((near, rows + 8, HEAD_DIM), F32)],
        compiler_params=params(16),
        name="chain",
    )(*pieces, after)


def spread_kernel(inside_ref, left_ref, entered_ref, *outs):
    near, rows, _ = inside_ref.shape
    mine = lax.axis_index("ctx") % near
    for apart, out_ref in enumerate(outs):
        shard = mine ^ apart
        left = left_ref[shard]
        for head in range(rows // HEAD_DIM):
            cols = head_columns(head)
            part = entered_ref[cols, :] * left[head : head + 1, :]
            out_ref[cols, :] = inside_ref[shard, cols, :] + part


def spread_states(inside, left, entered):
    near, rows, _ = inside.shape
    return pl.pallas_call(
        spread_kernel,
        in_specs=[vmem()] * 3,
        out_specs=[vmem()] * near,
        out_shape=[struct((rows, HEAD_DIM), F32)] * near,
        compiler_params=params(16),
        name="spread_states",
    )(inside, left, entered)


def inner_block(q_ref, k_ref, v_ref, first, cumul, raw_ref):
    heads = cumul.shape[0]
    columns = cumul.T
    half = SPAN // 2
    for part in range(2):
        rows = span_at(first, part * half, half)
        width = (part + 1) * half
        seen = span_at(first, 0, width)
        token = lax.broadcasted_iota(jnp.int32, (half, width), 0) + part * half
        earlier = lax.broadcasted_iota(jnp.int32, (half, width), 1)
        for group in range(0, heads, 4):
            members = range(group, min(group + 4, heads))
            scores = [
                lax.dot_general(
                    q_ref[rows, head_columns(head)],
                    k_ref[seen, head_columns(head)],
                    (((1,), (1,)), ((), ())),
                    preferred_element_type=F32,
                )
                for head in members
            ]
            weights = []
            for head, score in zip(members, scores):
                column = columns[part * half : (part + 1) * half, head : head + 1]
                diff = column - cumul[head : head + 1, :width]
                factor = jnp.exp(jnp.where(token >= earlier, diff, -jnp.inf))
                weights.append((score * factor).astype(BF16))
            for head, weight in zip(members, weights):
                cols = head_columns(head)
                raw_ref[rows, cols] = dot(weight, v_ref[seen, cols])


def inner_kernel(q_ref, k_ref, v_ref, cumul_ref, raw_ref):
    inner_block(q_ref, k_ref, v_ref, 0, cumul_ref[...], raw_ref)


def inner_loop_kernel(q_ref, k_ref, v_ref, cumul_ref, raw_ref):
    @pl.loop(0, q_ref.shape[0] // SPAN)
    def _(index):
        cumul = cumul_ref[lines_at(cumul_ref, index, q_ref.shape[0] // SPAN), :]
        inner_block(q_ref, k_ref, v_ref, index * SPAN, cumul, raw_ref)


def inner(queries, keys, values, cumul):
    count, width = keys.shape
    heads = width // HEAD_DIM
    work = cost(4 * count * width * SPAN, 10 * count * width, count * heads * SPAN)
    if fits(count, width):
        return pl.pallas_call(
            inner_loop_kernel,
            in_specs=[vmem()] * 4,
            out_specs=vmem(),
            out_shape=struct((count, width), F32),
            compiler_params=params(16),
            cost_estimate=work,
            name="inner",
        )(queries, keys, values, cumul)
    tokens = pl.BlockSpec((SPAN, width), lambda i: (i, 0))
    return pl.pallas_call(
        inner_kernel,
        grid=(count // SPAN,),
        in_specs=[tokens, tokens, tokens, pl.BlockSpec((heads, SPAN), lambda i: (i, 0))],
        out_specs=tokens,
        out_shape=struct((count, width), F32),
        compiler_params=params(24),
        cost_estimate=work,
        name="inner",
    )(queries, keys, values, cumul)


def finish_start(near, pieces, arrived, sums):
    mine = lax.axis_index("ctx") % near
    rows = arrived.shape[0] // near
    width = sums.shape[1]
    for apart in range(near):
        start = pl.multiple_of((mine ^ apart) * rows, rows)
        arrived[pl.ds(start, rows), :] = pieces[apart][...]
    sums[0:8, :] = jnp.zeros((8, width), F32)
    sums[8:16, :] = jnp.full((8, width), -jnp.inf, F32)
    sums[16:24, :] = jnp.full((8, width), jnp.inf, F32)


def finish_block(
    q_ref, raw_ref, first, entering_ref, before_ref, cumul, gain_ref, centered_ref, here, arrived, sums
):
    heads = cumul.shape[0]
    rows = span_at(first)
    block = 0 if isinstance(first, int) else first // SPAN
    factor = widen(jnp.exp(cumul))
    for group in range(0, heads, 4):
        members = range(group, min(group + 4, heads))
        outers = []
        for head in members:
            cols = head_columns(head)
            left = before_ref[block, head : head + 1, :]
            state = entering_ref[block, cols, :] + left * arrived[cols, :]
            query = q_ref[rows, cols]
            outers.append(
                dot(
                    jnp.concatenate([query, query], axis=1),
                    jnp.concatenate(split(state), axis=0),
                )
            )
        for head, outer in zip(members, outers):
            cols = head_columns(head)
            raw = raw_ref[rows, cols] + outer * factor[:, cols]
            power = jnp.mean(raw * raw, axis=1, keepdims=True)
            attended = (raw * lax.rsqrt(power + 1e-06) * gain_ref[:, cols]).astype(BF16)
            centered_ref[here, cols] = attended
            wide = attended.astype(F32).reshape(SPAN // 8, 8, HEAD_DIM)
            sums[0:8, cols] += jnp.sum(wide, axis=0)
            sums[8:16, cols] = jnp.maximum(sums[8:16, cols], jnp.max(wide, axis=0))
            sums[16:24, cols] = jnp.minimum(sums[16:24, cols], jnp.min(wide, axis=0))


def finish_end(centered_ref, stats_ref, sums):
    count, width = centered_ref.shape
    mean = jnp.sum(sums[0:8, :], axis=0, keepdims=True) / count
    first, rest = split(mean)
    rest = mean - first.astype(F32)
    second, third = split(rest)
    top = jnp.max(sums[8:16, :], axis=0, keepdims=True)
    bottom = jnp.min(sums[16:24, :], axis=0, keepdims=True)
    lines = [first.astype(F32), second.astype(F32), third.astype(F32), top, bottom]
    lines.append(jnp.zeros((11, width), F32))
    stats_ref[...] = jnp.concatenate(lines, axis=0).astype(BF16)

    @pl.loop(0, count // 128)
    def _(index):
        part = pl.ds(pl.multiple_of(index * 128, 128), 128)
        centered_ref[part, :] = (centered_ref[part, :].astype(F32) - mean).astype(BF16)


def finish_kernel(
    near, q_ref, raw_ref, entering_ref, before_ref, cumul_ref, gain_ref, *rest
):
    pieces, (centered_ref, stats_ref, arrived, sums) = rest[:near], rest[near:]
    step = pl.program_id(0)

    @pl.when(step == 0)
    def _():
        finish_start(near, pieces, arrived, sums)

    finish_block(
        q_ref,
        raw_ref,
        0,
        entering_ref,
        before_ref,
        cumul_ref[...],
        gain_ref,
        centered_ref,
        span_at(step * SPAN),
        arrived,
        sums,
    )

    @pl.when(step == pl.num_programs(0) - 1)
    def _():
        finish_end(centered_ref, stats_ref, sums)


def finish_loop_kernel(
    near, q_ref, raw_ref, entering_ref, before_ref, cumul_ref, gain_ref, *rest
):
    pieces, (centered_ref, stats_ref, arrived, sums) = rest[:near], rest[near:]
    finish_start(near, pieces, arrived, sums)

    @pl.loop(0, q_ref.shape[0] // SPAN)
    def _(index):
        here = span_at(index * SPAN)
        finish_block(
            q_ref,
            raw_ref,
            index * SPAN,
            entering_ref,
            before_ref,
            cumul_ref[lines_at(cumul_ref, index, q_ref.shape[0] // SPAN), :],
            gain_ref,
            centered_ref,
            here,
            arrived,
            sums,
        )

    finish_end(centered_ref, stats_ref, sums)


def finish(queries, raw, entering, before, cumul, gain, pieces):
    count, width = queries.shape
    heads = width // HEAD_DIM
    near = len(pieces)
    shapes = [struct((count, width), BF16), struct((16, width), BF16)]
    scratch = [pltpu.VMEM((width, HEAD_DIM), F32), pltpu.VMEM((24, width), F32)]
    work = cost(4 * count * width * HEAD_DIM, 10 * count * width)
    operands = (queries, raw, entering, before, cumul, gain, *pieces)
    if fits(count, width):
        return pl.pallas_call(
            functools.partial(finish_loop_kernel, near),
            in_specs=[vmem()] * len(operands),
            out_specs=[vmem()] * 2,
            scratch_shapes=scratch,
            out_shape=shapes,
            compiler_params=params(16),
            cost_estimate=work,
            name="finish",
        )(*operands)
    tokens = pl.BlockSpec((SPAN, width), lambda i: (i, 0))
    return pl.pallas_call(
        functools.partial(finish_kernel, near),
        grid=(count // SPAN,),
        in_specs=[
            tokens,
            tokens,
            pl.BlockSpec((1, width, HEAD_DIM), lambda i: (i, 0, 0)),
            pl.BlockSpec((1, heads, HEAD_DIM), lambda i: (i, 0, 0)),
            pl.BlockSpec((heads, SPAN), lambda i: (i, 0)),
            whole((1, width)),
        ]
        + [whole(pieces[0].shape)] * near,
        out_specs=[whole((count, width)), whole((16, width))],
        scratch_shapes=scratch,
        out_shape=shapes,
        compiler_params=params(32),
        cost_estimate=work,
        name="finish",
    )(*operands)


def places(count, inner, bit):
    return [
        (outer * 2 + bit) * inner + index
        for outer in range(count // inner // 2)
        for index in range(inner)
    ]


def side_of(side, block, shards):
    return side if side < 2 else (0 if block < shards // 2 else 1)


def gram_kernel(rows, blocks, apart, own_ref, other_ref, *rest):
    keep_ref, send_ref, turned = rest[-3:]
    width = own_ref.shape[1]
    shards = width // rows
    steps = sorted({step for step, _ in blocks})
    bit = (lax.axis_index("ctx") // apart) % 2
    if len(rest) > 4:
        send_ref[shards // 2 * rows :, :] = rest[0][...]
    for start in range(0, turned.shape[0], HEAD_DIM):
        here = start % width
        turned[start : start + HEAD_DIM, :] = own_ref[:, here : here + HEAD_DIM].T

    def fill(out_ref, row_blocks):
        for index, block in enumerate(row_blocks):
            line = slice(index * rows, (index + 1) * rows)
            here = slice(block * rows, (block + 1) * rows)
            left = turned[(block + steps[0]) * rows : (block + steps[-1] + 1) * rows, :]
            right = jnp.concatenate([own_ref[:, here], other_ref[:, here]], axis=1)
            out = dot(left, right).astype(out_ref.dtype)
            for place, (step, side) in enumerate(blocks):
                low = (step - steps[0]) * rows
                first = side_of(side, block, shards) * rows
                target = slice(place * rows, (place + 1) * rows)
                out_ref[line, target] = out[low : low + rows, first : first + rows]

    for mine in range(2):

        @pl.when(bit == mine)
        def _():
            fill(send_ref, places(shards, apart, 1 - mine))
            fill(keep_ref, places(shards, apart, mine))


def gram_parts(own, other, extra, after, rows, blocks, apart):
    count, width = own.shape
    shards = width // rows
    size = len(blocks) * rows
    kept = (shards // 2 * rows, size)
    if rows % 128:
        full = [
            lax.dot_general(own, side, (((0,), (0,)), ((), ())), preferred_element_type=F32)
            for side in (own, other)
        ]
        parts = []
        for shard in range(shards):
            slabs = []
            for step, side in blocks:
                at = (shard + step) % shards * rows
                value = full[side_of(side, shard, shards)]
                slabs.append(value[at : at + rows, shard * rows : (shard + 1) * rows])
            parts.append(jnp.concatenate(slabs, axis=1))
        bit = (lax.axis_index("ctx") // apart) % 2
        parts = jnp.stack(parts).reshape(-1, 2, apart, rows, size)
        keep = lax.dynamic_index_in_dim(parts, bit, 1, False).reshape(kept)
        send = lax.dynamic_index_in_dim(parts, 1 - bit, 1, False).reshape(kept)
        return keep, jnp.concatenate([send.astype(BF16)] + extra)
    sent = (kept[0] + sum(value.shape[0] for value in extra), size)
    last = max(step for step, _ in blocks)
    return pl.pallas_call(
        functools.partial(gram_kernel, rows, blocks, apart),
        in_specs=[vmem()] * (2 + len(extra)) + [anywhere()],
        out_specs=[vmem(), vmem()],
        scratch_shapes=[pltpu.VMEM((width + last * rows, count), BF16)],
        out_shape=[struct(kept, F32), struct(sent, BF16)],
        compiler_params=params(16),
        cost_estimate=cost(2 * count * width * size, 4 * count * width),
        name="gram",
    )(own, other, *extra, after)


def merge(first, second, means):
    a, b = first.astype(F32), second.astype(F32)
    top, bottom = slice(means, means + 2), slice(means + 2, means + 4)
    lines = [a[:means], b[:means], jnp.maximum(a[top], b[top]), jnp.minimum(a[bottom], b[bottom])]
    spare = -(2 * means + 4) % 16
    if spare:
        lines.append(jnp.zeros((spare, a.shape[1]), F32))
    return jnp.concatenate(lines, axis=0).astype(BF16)


def fold_kernel(rows, inner, apart, means, keep_ref, other_ref, _, *rest):
    count = keep_ref.shape[0] // rows
    bit = (lax.axis_index("ctx") // apart) % 2
    if means:
        riders_ref, kept_ref, send_ref, merged_ref = rest
        merged = merge(riders_ref[...], other_ref[keep_ref.shape[0] :, :], means)
        send_ref[kept_ref.shape[0] :, :] = merged
        merged_ref[...] = merged
    else:
        kept_ref, send_ref = rest

    for mine in range(2):

        @pl.when(bit == mine)
        def _():
            for out_ref, side in ((send_ref, 1 - mine), (kept_ref, mine)):
                for index, block in enumerate(places(count, inner, side)):
                    line = slice(block * rows, (block + 1) * rows)
                    total = keep_ref[line, :] + other_ref[line, :].astype(F32)
                    out_ref[index * rows : (index + 1) * rows, :] = total.astype(out_ref.dtype)


def fold(keep, other, after, riders, means, rows, inner, apart):
    kept = (keep.shape[0] // 2, keep.shape[1])
    shapes = [struct(kept, F32), struct(kept, BF16)]
    if riders:
        merged = (2 * means + 4 + -(2 * means + 4) % 16, kept[1])
        shapes = [struct(kept, F32), struct((kept[0] + merged[0], kept[1]), BF16)]
        shapes.append(struct(merged, BF16))
    return pl.pallas_call(
        functools.partial(fold_kernel, rows, inner, apart, means if riders else 0),
        in_specs=[vmem()] * 2 + [anywhere()] + [vmem()] * len(riders),
        out_specs=[vmem()] * len(shapes),
        out_shape=shapes,
        compiler_params=params(16),
        name="fold",
    )(keep, other, after, *riders)


def close_kernel(rows, runs, waits, keep_ref, other_ref, *rest):
    total_ref, slab_refs = rest[waits], rest[waits + 1 :]
    total = keep_ref[...] + other_ref[:rows, :].astype(F32)
    total_ref[...] = total
    for run, slab_ref in zip(runs, slab_refs):
        for place, column in enumerate(run):
            slab = total[:, column * rows : (column + 1) * rows].astype(BF16)
            slab_ref[:, place * rows : (place + 1) * rows] = slab


def close(keep, other, after, rows, runs):
    out = pl.pallas_call(
        functools.partial(close_kernel, rows, runs, len(after)),
        in_specs=[vmem(), vmem()] + [anywhere()] * len(after),
        out_specs=[vmem()] * (1 + len(runs)),
        out_shape=[struct(keep.shape, F32)] + [struct((rows, len(run) * rows), BF16) for run in runs],
        compiler_params=params(16),
        name="close",
    )(keep, other, *after)
    return out[0], out[1:]


def assemble(put, upper, shards, chunks, mirrors, crossed):
    half = shards // 2
    put(0, 0, chunks[(0, 0)])
    put(0, 1, chunks[(0, 1)])
    for step in range(1, half):
        put(step, 0, chunks[(step, 0)].T)
        put(step, 1, crossed[step].T)
        put(-step, 0, mirrors[(step, 0)])
        put(-step, 1, mirrors[(step, 1)])
    last = jnp.where(upper, crossed[half].astype(F32), chunks[(half, 2)])
    put(half, upper, last.T)
    put(half, 1 - upper, mirrors[(half, 2)])


def pick(rows, names, values):
    out = {}
    for blocks, value in zip(names, values):
        for place, name in enumerate(blocks):
            out[name] = value[:, place * rows : (place + 1) * rows]
    return out


def cover_kernel(rows, shards, total, names, means_ref, others_ref, *refs):
    out_ref, spread = refs[-2:]
    width = rows * shards
    mine, side = lax.axis_index("ctx"), lax.axis_index("head") & 1
    for ref, place in ((means_ref, side), (others_ref, 1 - side)):
        value = ref[...]
        centre = jnp.sum(value, axis=0, keepdims=True) / shards
        spread[:, pl.ds(pl.multiple_of(place * width, width), width)] = value - centre
    own = pl.multiple_of((side * shards + mine) * rows, rows)
    left = spread[:, pl.ds(own, rows)].T
    count = total // shards
    out_ref[...] = count * jnp.dot(left, spread[...], precision=HIGHEST, preferred_element_type=F32)

    def put(step, flip, gram):
        shard = lax.rem(mine + step + shards, shards)
        at = pl.ds(pl.multiple_of(((side ^ flip) * shards + shard) * rows, rows), rows)
        out_ref[:, at] = (out_ref[:, at] + gram.astype(F32)) / total

    values = iter(refs[:-2])
    parts = [pick(rows, group, [next(values) for _ in group]) for group in names]
    assemble(put, jnp.where(mine >= shards // 2, 1, 0), shards, *parts)


def cover(means, others, groups, names, rows, shards, total):
    width = rows * shards
    values = [value for group in groups for value in group]
    if rows % 128:
        mine, side = lax.axis_index("ctx"), lax.axis_index("head") & 1
        pair = [jnp.where(side == 0, means, others), jnp.where(side == 0, others, means)]
        spread = jnp.concatenate(pair, axis=1)
        spread = spread - jnp.mean(spread, axis=0)
        left = lax.dynamic_slice_in_dim(spread, (side * shards + mine) * rows, rows, 1)
        out = [(total // shards) * jnp.dot(left.T, spread, precision=HIGHEST)]

        def put(step, flip, gram):
            shard = lax.rem(mine + step + shards, shards)
            at = ((side ^ flip) * shards + shard) * rows
            old = lax.dynamic_slice_in_dim(out[0], at, rows, 1)
            new = (old + gram.astype(F32)) / total
            out[0] = lax.dynamic_update_slice_in_dim(out[0], new, at, 1)

        parts = [pick(rows, *pair) for pair in zip(names, groups)]
        assemble(put, jnp.where(mine >= shards // 2, 1, 0), shards, *parts)
        return out[0]
    return pl.pallas_call(
        functools.partial(cover_kernel, rows, shards, total, names),
        in_specs=[vmem()] * (2 + len(values)),
        out_specs=vmem(),
        scratch_shapes=[pltpu.VMEM((shards, 2 * width), F32)],
        out_shape=struct((rows, 2 * width), F32),
        compiler_params=params(16),
        name="cover",
    )(means, others, *values)


def body(queries, keys, values, log_decay, gain):
    count, width = queries.shape
    shards = lax.axis_size("ctx")
    sides = lax.axis_size("head")
    rows = width // shards
    mine = lax.axis_index("ctx")

    def to_shard(value, apart):
        return lax.ppermute(value, "ctx", [(a, a ^ apart) for a in range(shards)])

    def to_partner(value):
        return lax.ppermute(value, "head", [(a, a ^ 1) for a in range(sides)])

    near = shards // 2

    def nearby(values):
        return [values[0]] + [to_shard(values[apart], apart) for apart in range(1, near)]

    def forward(value, step):
        return lax.ppermute(value, "ctx", [(a, (a + step) % shards) for a in range(shards)])

    (entering, before, cumul), pieces, (keys, values) = local_states(
        keys, values, log_decay, near
    )
    raw = inner(queries, keys, values, cumul)
    inside, left, leaving = chain(nearby(pieces), raw)
    entered = lax.ppermute(leaving, "ctx", [(a, a + near) for a in range(near)])
    entry = nearby(spread_states(inside, left, entered))
    centered, stats = finish(
        queries, raw, entering, before, cumul, gain.reshape(1, width), entry
    )
    partner = to_partner(centered)

    half = shards // 2
    lines = half * rows
    mean_rows = 3 * width // lines
    extra = stats[:5].reshape(mean_rows + 4, lines)
    extra = jnp.pad(extra, ((0, -extra.shape[0] % 16), (0, 0)))
    bits = [1 << place for place in range(shards.bit_length() - 1)]
    near_steps = range(1, half // 2 + 1)
    far_steps = range(half // 2 + 1, half)
    bits = [1 << place for place in range(shards.bit_length() - 1)]
    plans = [
        ([(step, side) for step in near_steps for side in (0, 1)], bits),
        ([(0, 0), (0, 1)], bits[1:] + bits[:1]),
        ([(step, side) for step in far_steps for side in (0, 1)] + [(half, 2)], bits),
    ]
    kept, riders, after = [], [extra], stats
    for blocks, turns in plans:
        carried = [] if kept else riders
        keep, send = gram_parts(centered, partner, carried, after, rows, blocks, turns[0])
        after = keep
        kept.append((keep, to_shard(send, turns[0])))

    def split_on(index, stage, after):
        keep, other = kept[index]
        turns = plans[index][1]
        left = [bit for bit in bits if bit not in turns[:stage]]
        carried = riders if index == 0 else []
        keep, send, *merged = fold(
            keep,
            other,
            after,
            carried,
            mean_rows << (stage - 1),
            rows,
            1 << left.index(turns[stage]),
            turns[stage],
        )
        riders[:] = merged or riders
        kept[index] = (keep, to_shard(send, turns[stage]))
        return keep

    after = kept[0][0]
    for stage in range(1, len(bits)):
        for index in (1, 0, 2):
            after = split_on(index, stage, after)

    chunks, mirrors, mirror_names, crossed, crossed_names = [None] * len(plans), [], [], [], []
    for index in (0, 1, 2):
        blocks, (keep, other) = plans[index][0], kept[index]
        if index == 0:
            every = merge(riders[0], other[rows:], mean_rows * half)
        steps = sorted({step for step, _ in blocks} - {0})
        runs = [[i for i, block in enumerate(blocks) if block[0] == step] for step in steps]
        crossing = [i for i, (step, side) in enumerate(blocks) if step and side]
        earlier = mirrors + crossed if index == 2 else []
        total, slabs = close(keep, other, earlier, rows, runs + [crossing] * bool(crossing))
        chunks[index] = total
        for step, run, slab in zip(steps, runs, slabs):
            mirrors.append(forward(slab, step))
            mirror_names.append([blocks[i] for i in run])
        if crossing:
            crossed.append(to_partner(slabs[-1]))
            crossed_names.append([blocks[i][0] for i in crossing])

    every = every.astype(F32)
    means = jnp.sum(every[: mean_rows * shards].reshape(shards, 3, width), axis=1)
    extremes = every[mean_rows * shards :][:4].reshape(2, width)
    shift = (extremes[0] + extremes[1]) / 2.0
    others = to_partner(means)
    covariance = cover(
        means,
        others,
        (chunks, mirrors, crossed),
        ([blocks for blocks, _ in plans], mirror_names, crossed_names),
        rows,
        shards,
        count * shards,
    )
    return (shift, covariance)


def solution(mesh):
    placed = (P("ctx", "head"), P("ctx", "head"), P("ctx", "head"), P("head", "ctx"), P("head"))
    return jax.shard_map(
        body,
        mesh=mesh,
        in_specs=placed,
        out_specs=(P("head"), P(("head", "ctx"), None)),
        check_vma=False,
    )
```

```python
import functools
import math

import jax
import jax.numpy as jnp
from jax import lax
from jax.experimental import pallas as pl
from jax.experimental.pallas import tpu as pltpu
from jax.sharding import PartitionSpec as P

HEAD_DIM = 128
SPAN = 256
F32 = jnp.float32
BF16 = jnp.bfloat16
HIGHEST = lax.Precision.HIGHEST
MIB = 1 << 20
RIDER_ROWS = 4


def params(limit_mib):
    return pltpu.CompilerParams(vmem_limit_bytes=limit_mib * MIB)


def cost(flops, moved, transcendentals=0):
    return pl.CostEstimate(
        flops=1, bytes_accessed=1, transcendentals=0
    )


def whole(shape):
    return pl.BlockSpec(shape, lambda *_: (0,) * len(shape))


def anywhere():
    return pl.BlockSpec(memory_space=pl.ANY)


def vmem():
    return pl.BlockSpec(memory_space=pltpu.VMEM)


def hbm():
    return pl.BlockSpec(memory_space=pltpu.HBM)


def struct(shape, dtype):
    return jax.ShapeDtypeStruct(shape, dtype)


def dot(a, b):
    return jnp.dot(a, b, preferred_element_type=F32)


def split(value):
    high = value.astype(BF16)
    return high, (value - high.astype(F32)).astype(BF16)


def running_sum(decay):
    rows = lax.broadcasted_iota(jnp.int32, (SPAN, SPAN), 0)
    columns = lax.broadcasted_iota(jnp.int32, (SPAN, SPAN), 1)
    ones = jnp.where(rows <= columns, 1.0, 0.0).astype(F32)
    return jnp.dot(decay, ones, precision=HIGHEST, preferred_element_type=F32)


def span_at(first, start=0, size=SPAN):
    if isinstance(first, int):
        return slice(first + start, first + start + size)
    return pl.ds(pl.multiple_of(first + start, math.gcd(start, SPAN)), size)


def lines_at(ref, index, blocks):
    heads = ref.shape[0] // blocks
    return pl.ds(pl.multiple_of(index * heads, heads), heads)


def fits(count, width):
    return count * width <= 1 << 20


def widen(value):
    heads = value.shape[0]
    first, rest = split(value)
    second, third = split(value - first.astype(F32))
    rows = lax.broadcasted_iota(jnp.int32, (heads, heads * HEAD_DIM), 0)
    columns = lax.broadcasted_iota(jnp.int32, (heads, heads * HEAD_DIM), 1)
    ones = jnp.where(columns // HEAD_DIM == rows, 1.0, 0.0)
    pieces = [first.astype(F32), second.astype(F32), third.astype(F32)]
    return lax.dot_general(
        jnp.concatenate(pieces, axis=0).astype(BF16),
        jnp.concatenate([ones] * 3, axis=0).astype(BF16),
        (((0,), (0,)), ((), ())),
        preferred_element_type=F32,
    )


def head_columns(head):
    return slice(head * HEAD_DIM, (head + 1) * HEAD_DIM)


def states_block(k_ref, v_ref, first, cumul, state, total):
    heads = cumul.shape[0]
    last = cumul[:, SPAN - 1 :]
    weight = jnp.exp(last - cumul)
    drop = jnp.exp(last)
    rows = span_at(first)
    for group in range(0, heads, 4):
        members = range(group, min(group + 4, heads))
        turned = [k_ref[rows, head_columns(head)].T for head in members]
        parts = []
        for head, key in zip(members, turned):
            high, low = split(key.astype(F32) * weight[head : head + 1, :])
            parts.append(jnp.concatenate([high, low], axis=0))
        updates = [dot(part, v_ref[rows, head_columns(head)]) for head, part in zip(members, parts)]
        for head, update in zip(members, updates):
            cols = head_columns(head)
            update = update[:HEAD_DIM] + update[HEAD_DIM:]
            state[cols, :] = state[cols, :] * drop[head : head + 1, :] + update
    total[...] = total[...] * drop


def states_out(near, state, total, pieces):
    mine = lax.axis_index("ctx") % near
    rows = state.shape[0] // near
    for apart in range(near):
        start = pl.multiple_of((mine ^ apart) * rows, rows)
        pieces[apart][:rows, :] = state[pl.ds(start, rows), :]
        pieces[apart][rows:, :] = jnp.zeros((8, HEAD_DIM), F32)
        for head in range(rows // HEAD_DIM):
            line = total[pl.ds(start // HEAD_DIM + head, 1), :]
            pieces[apart][rows + head : rows + head + 1, :] = line


def states_kernel(near, k_ref, v_ref, decay_ref, entering_ref, before_ref, cumul_ref, *rest):
    pieces, (state, total) = rest[:near], rest[near:]
    step = pl.program_id(0)

    @pl.when(step == 0)
    def _():
        state[...] = jnp.zeros_like(state)
        total[...] = jnp.ones_like(total)

    entering_ref[0] = state[...]
    before_ref[0] = total[...]
    cumul_ref[...] = running_sum(decay_ref[...])
    states_block(k_ref, v_ref, 0, cumul_ref[...], state, total)

    @pl.when(step == pl.num_programs(0) - 1)
    def _():
        states_out(near, state, total, pieces)


def states_fetch_kernel(near, k_any, v_any, decay_any, entering_ref, before_ref, cumul, *rest):
    pieces, (k_ref, v_ref, decay_ref, state, total, sems) = rest[:near], rest[near:]
    count = k_any.shape[0]
    blocks = count // SPAN
    heads = decay_ref.shape[0]

    def fetch(source, target, index, which):
        rows = span_at(index * SPAN)
        return pltpu.make_async_copy(source.at[rows, :], target.at[rows, :], sems.at[which, index])

    decays = pltpu.make_async_copy(decay_any, decay_ref, sems.at[2, 0])
    decays.start()
    for index in range(blocks):
        fetch(k_any, k_ref, index, 0).start()
        fetch(v_any, v_ref, index, 1).start()
    state[...] = jnp.zeros_like(state)
    total[...] = jnp.ones_like(total)
    decays.wait()
    lines = [decay_ref[:, index * SPAN : (index + 1) * SPAN] for index in range(blocks)]
    cumul[...] = running_sum(jnp.concatenate(lines, axis=0))

    @pl.loop(0, blocks)
    def _(index):
        fetch(k_any, k_ref, index, 0).wait()
        fetch(v_any, v_ref, index, 1).wait()
        entering_ref[index] = state[...]
        before_ref[index] = total[...]
        lines = cumul[pl.ds(pl.multiple_of(index * heads, heads), heads), :]
        states_block(k_ref, v_ref, index * SPAN, lines, state, total)

    states_out(near, state, total, pieces)


def local_states(keys, values, log_decay, near):
    count, width = keys.shape
    heads = width // HEAD_DIM
    blocks = count // SPAN
    rows = width // near
    piece = (rows + 8, HEAD_DIM)
    shapes = [(blocks, width, HEAD_DIM), (blocks, heads, HEAD_DIM), (blocks * heads, SPAN)]
    shapes += [piece] * near
    scratch = [pltpu.VMEM((width, HEAD_DIM), F32), pltpu.VMEM((heads, HEAD_DIM), F32)]
    if fits(count, width):
        kept = [struct(value.shape, value.dtype) for value in (keys, values)]
        out = pl.pallas_call(
            functools.partial(states_fetch_kernel, near),
            in_specs=[hbm()] * 3,
            out_specs=[vmem()] * (len(shapes) + 2),
            out_shape=[struct(shape, F32) for shape in shapes] + kept,
            scratch_shapes=[pltpu.VMEM((heads, count), F32)]
            + scratch
            + [pltpu.SemaphoreType.DMA((3, blocks))],
            compiler_params=params(48),
            cost_estimate=cost(4 * count * width * HEAD_DIM, 4 * count * width),
            name="local_states",
        )(keys, values, log_decay)
        return out[:3], out[3:-2], out[-2:]
    tokens = pl.BlockSpec((SPAN, width), lambda i: (i, 0))
    out = pl.pallas_call(
        functools.partial(states_kernel, near),
        grid=(blocks,),
        in_specs=[tokens, tokens, pl.BlockSpec((heads, SPAN), lambda i: (0, i))],
        out_specs=[
            pl.BlockSpec((1, width, HEAD_DIM), lambda i: (i, 0, 0)),
            pl.BlockSpec((1, heads, HEAD_DIM), lambda i: (i, 0, 0)),
            pl.BlockSpec((heads, SPAN), lambda i: (i, 0)),
        ]
        + [whole(piece)] * near,
        scratch_shapes=scratch,
        out_shape=[struct(shape, F32) for shape in shapes],
        compiler_params=params(56),
        cost_estimate=cost(4 * count * width * HEAD_DIM, 4 * count * width),
        name="local_states",
    )(keys, values, log_decay)
    return out[:3], out[3:], (keys, values)


def chain_kernel(near, *refs):
    arrived, (inside_ref, left_ref, leaving_ref, ordered) = refs[:near], refs[near + 1 :]
    mine = lax.axis_index("ctx") % near
    rows = leaving_ref.shape[0]
    heads = rows // HEAD_DIM
    for apart in range(near):
        ordered[mine ^ apart] = arrived[apart][...]
    left_ref[...] = jnp.zeros_like(left_ref)
    for head in range(heads):
        cols = head_columns(head)
        carried = jnp.zeros((HEAD_DIM, HEAD_DIM), F32)
        left = jnp.ones((1, HEAD_DIM), F32)
        for shard in range(near):
            inside_ref[shard, cols, :] = carried
            left_ref[shard, head : head + 1, :] = left
            drop = ordered[shard, rows + head : rows + head + 1, :]
            carried = carried * drop + ordered[shard, cols, :]
            left = left * drop
        leaving_ref[cols, :] = carried


def chain(pieces, after):
    near = len(pieces)
    rows = pieces[0].shape[0] - 8
    shapes = [(near, rows, HEAD_DIM), (near, 8, HEAD_DIM), (rows, HEAD_DIM)]
    return pl.pallas_call(
        functools.partial(chain_kernel, near),
        in_specs=[vmem()] * near + [anywhere()],
        out_specs=[vmem()] * 3,
        out_shape=[struct(shape, F32) for shape in shapes],
        scratch_shapes=[pltpu.VMEM((near, rows + 8, HEAD_DIM), F32)],
        compiler_params=params(16),
        name="chain",
    )(*pieces, after)


def spread_kernel(inside_ref, left_ref, entered_ref, *outs):
    near, rows, _ = inside_ref.shape
    mine = lax.axis_index("ctx") % near
    for apart, out_ref in enumerate(outs):
        shard = mine ^ apart
        left = left_ref[shard]
        for head in range(rows // HEAD_DIM):
            cols = head_columns(head)
            part = entered_ref[cols, :] * left[head : head + 1, :]
            out_ref[cols, :] = inside_ref[shard, cols, :] + part


def spread_states(inside, left, entered):
    near, rows, _ = inside.shape
    return pl.pallas_call(
        spread_kernel,
        in_specs=[vmem()] * 3,
        out_specs=[vmem()] * near,
        out_shape=[struct((rows, HEAD_DIM), F32)] * near,
        compiler_params=params(16),
        name="spread_states",
    )(inside, left, entered)


def inner_block(q_ref, k_ref, v_ref, first, cumul, raw_ref):
    heads = cumul.shape[0]
    columns = cumul.T
    half = SPAN // 2
    for part in range(2):
        rows = span_at(first, part * half, half)
        width = (part + 1) * half
        seen = span_at(first, 0, width)
        token = lax.broadcasted_iota(jnp.int32, (half, width), 0) + part * half
        earlier = lax.broadcasted_iota(jnp.int32, (half, width), 1)
        for group in range(0, heads, 4):
            members = range(group, min(group + 4, heads))
            scores = [
                lax.dot_general(
                    q_ref[rows, head_columns(head)],
                    k_ref[seen, head_columns(head)],
                    (((1,), (1,)), ((), ())),
                    preferred_element_type=F32,
                )
                for head in members
            ]
            weights = []
            for head, score in zip(members, scores):
                column = columns[part * half : (part + 1) * half, head : head + 1]
                diff = column - cumul[head : head + 1, :width]
                factor = jnp.exp(jnp.where(token >= earlier, diff, -jnp.inf))
                weights.append((score * factor).astype(BF16))
            for head, weight in zip(members, weights):
                cols = head_columns(head)
                raw_ref[rows, cols] = dot(weight, v_ref[seen, cols])


def inner_kernel(q_ref, k_ref, v_ref, cumul_ref, raw_ref):
    inner_block(q_ref, k_ref, v_ref, 0, cumul_ref[...], raw_ref)


def inner_loop_kernel(q_ref, k_ref, v_ref, cumul_ref, raw_ref):
    @pl.loop(0, q_ref.shape[0] // SPAN)
    def _(index):
        cumul = cumul_ref[lines_at(cumul_ref, index, q_ref.shape[0] // SPAN), :]
        inner_block(q_ref, k_ref, v_ref, index * SPAN, cumul, raw_ref)


def inner(queries, keys, values, cumul):
    count, width = keys.shape
    heads = width // HEAD_DIM
    work = cost(4 * count * width * SPAN, 10 * count * width, count * heads * SPAN)
    if fits(count, width):
        return pl.pallas_call(
            inner_loop_kernel,
            in_specs=[vmem()] * 4,
            out_specs=vmem(),
            out_shape=struct((count, width), F32),
            compiler_params=params(16),
            cost_estimate=work,
            name="inner",
        )(queries, keys, values, cumul)
    tokens = pl.BlockSpec((SPAN, width), lambda i: (i, 0))
    return pl.pallas_call(
        inner_kernel,
        grid=(count // SPAN,),
        in_specs=[tokens, tokens, tokens, pl.BlockSpec((heads, SPAN), lambda i: (i, 0))],
        out_specs=tokens,
        out_shape=struct((count, width), F32),
        compiler_params=params(24),
        cost_estimate=work,
        name="inner",
    )(queries, keys, values, cumul)


def finish_start(near, pieces, arrived, sums):
    mine = lax.axis_index("ctx") % near
    rows = arrived.shape[0] // near
    width = sums.shape[1]
    for apart in range(near):
        start = pl.multiple_of((mine ^ apart) * rows, rows)
        arrived[pl.ds(start, rows), :] = pieces[apart][...]
    sums[0:8, :] = jnp.zeros((8, width), F32)
    sums[8:16, :] = jnp.full((8, width), -jnp.inf, F32)
    sums[16:24, :] = jnp.full((8, width), jnp.inf, F32)


def finish_block(
    q_ref, raw_ref, first, entering_ref, before_ref, cumul, gain_ref, centered_ref, here, arrived, sums
):
    heads = cumul.shape[0]
    rows = span_at(first)
    block = 0 if isinstance(first, int) else first // SPAN
    factor = widen(jnp.exp(cumul))
    for group in range(0, heads, 4):
        members = range(group, min(group + 4, heads))
        outers = []
        for head in members:
            cols = head_columns(head)
            left = before_ref[block, head : head + 1, :]
            state = entering_ref[block, cols, :] + left * arrived[cols, :]
            query = q_ref[rows, cols]
            outers.append(
                dot(
                    jnp.concatenate([query, query], axis=1),
                    jnp.concatenate(split(state), axis=0),
                )
            )
        for head, outer in zip(members, outers):
            cols = head_columns(head)
            raw = raw_ref[rows, cols] + outer * factor[:, cols]
            power = jnp.mean(raw * raw, axis=1, keepdims=True)
            attended = (raw * lax.rsqrt(power + 1e-06) * gain_ref[:, cols]).astype(BF16)
            centered_ref[here, cols] = attended
            wide = attended.astype(F32).reshape(SPAN // 8, 8, HEAD_DIM)
            sums[0:8, cols] += jnp.sum(wide, axis=0)
            sums[8:16, cols] = jnp.maximum(sums[8:16, cols], jnp.max(wide, axis=0))
            sums[16:24, cols] = jnp.minimum(sums[16:24, cols], jnp.min(wide, axis=0))


def finish_end(centered_ref, stats_ref, sums):
    count, width = centered_ref.shape
    mean = jnp.sum(sums[0:8, :], axis=0, keepdims=True) / count
    first, rest = split(mean)
    rest = mean - first.astype(F32)
    second, third = split(rest)
    top = jnp.max(sums[8:16, :], axis=0, keepdims=True)
    bottom = jnp.min(sums[16:24, :], axis=0, keepdims=True)
    lines = [first.astype(F32), second.astype(F32), third.astype(F32), top, bottom]
    lines.append(jnp.zeros((11, width), F32))
    stats_ref[...] = jnp.concatenate(lines, axis=0).astype(BF16)

    @pl.loop(0, count // 128)
    def _(index):
        part = pl.ds(pl.multiple_of(index * 128, 128), 128)
        centered_ref[part, :] = (centered_ref[part, :].astype(F32) - mean).astype(BF16)


def finish_kernel(
    near, q_ref, raw_ref, entering_ref, before_ref, cumul_ref, gain_ref, *rest
):
    pieces, (centered_ref, stats_ref, arrived, sums) = rest[:near], rest[near:]
    step = pl.program_id(0)

    @pl.when(step == 0)
    def _():
        finish_start(near, pieces, arrived, sums)

    finish_block(
        q_ref,
        raw_ref,
        0,
        entering_ref,
        before_ref,
        cumul_ref[...],
        gain_ref,
        centered_ref,
        span_at(step * SPAN),
        arrived,
        sums,
    )

    @pl.when(step == pl.num_programs(0) - 1)
    def _():
        finish_end(centered_ref, stats_ref, sums)


def finish_loop_kernel(
    near, q_ref, raw_ref, entering_ref, before_ref, cumul_ref, gain_ref, *rest
):
    pieces, (centered_ref, stats_ref, arrived, sums) = rest[:near], rest[near:]
    finish_start(near, pieces, arrived, sums)

    @pl.loop(0, q_ref.shape[0] // SPAN)
    def _(index):
        here = span_at(index * SPAN)
        finish_block(
            q_ref,
            raw_ref,
            index * SPAN,
            entering_ref,
            before_ref,
            cumul_ref[lines_at(cumul_ref, index, q_ref.shape[0] // SPAN), :],
            gain_ref,
            centered_ref,
            here,
            arrived,
            sums,
        )

    finish_end(centered_ref, stats_ref, sums)


def finish(queries, raw, entering, before, cumul, gain, pieces):
    count, width = queries.shape
    heads = width // HEAD_DIM
    near = len(pieces)
    shapes = [struct((count, width), BF16), struct((16, width), BF16)]
    scratch = [pltpu.VMEM((width, HEAD_DIM), F32), pltpu.VMEM((24, width), F32)]
    work = cost(4 * count * width * HEAD_DIM, 10 * count * width)
    operands = (queries, raw, entering, before, cumul, gain, *pieces)
    if fits(count, width):
        return pl.pallas_call(
            functools.partial(finish_loop_kernel, near),
            in_specs=[vmem()] * len(operands),
            out_specs=[vmem()] * 2,
            scratch_shapes=scratch,
            out_shape=shapes,
            compiler_params=params(16),
            cost_estimate=work,
            name="finish",
        )(*operands)
    tokens = pl.BlockSpec((SPAN, width), lambda i: (i, 0))
    return pl.pallas_call(
        functools.partial(finish_kernel, near),
        grid=(count // SPAN,),
        in_specs=[
            tokens,
            tokens,
            pl.BlockSpec((1, width, HEAD_DIM), lambda i: (i, 0, 0)),
            pl.BlockSpec((1, heads, HEAD_DIM), lambda i: (i, 0, 0)),
            pl.BlockSpec((heads, SPAN), lambda i: (i, 0)),
            whole((1, width)),
        ]
        + [whole(pieces[0].shape)] * near,
        out_specs=[whole((count, width)), whole((16, width))],
        scratch_shapes=scratch,
        out_shape=shapes,
        compiler_params=params(32),
        cost_estimate=work,
        name="finish",
    )(*operands)


def places(count, inner, bit):
    return [
        (outer * 2 + bit) * inner + index
        for outer in range(count // inner // 2)
        for index in range(inner)
    ]


def side_of(side, block, shards):
    return side if side < 2 else (0 if block < shards // 2 else 1)


def gram_kernel(rows, blocks, apart, own_ref, other_ref, *rest):
    keep_ref, send_ref, turned = rest[-3:]
    width = own_ref.shape[1]
    shards = width // rows
    steps = sorted({step for step, _ in blocks})
    sides = {side for _, side in blocks}
    refs = [own_ref] if sides == {0} else [other_ref] if sides == {1} else [own_ref, other_ref]
    bit = (lax.axis_index("ctx") // apart) % 2
    if len(rest) > 4:
        send_ref[shards // 2 * rows :, :] = rest[0][...]
    for start in range(0, turned.shape[0], HEAD_DIM):
        here = start % width
        turned[start : start + HEAD_DIM, :] = own_ref[:, here : here + HEAD_DIM].T

    def fill(out_ref, row_blocks):
        for index, block in enumerate(row_blocks):
            line = slice(index * rows, (index + 1) * rows)
            here = slice(block * rows, (block + 1) * rows)
            left = turned[(block + steps[0]) * rows : (block + steps[-1] + 1) * rows, :]
            right = [ref[:, here] for ref in refs]
            right = right[0] if len(right) == 1 else jnp.concatenate(right, axis=1)
            out = dot(left, right).astype(out_ref.dtype)
            for place, (step, side) in enumerate(blocks):
                low = (step - steps[0]) * rows
                first = (side_of(side, block, shards) if len(refs) > 1 else 0) * rows
                target = slice(place * rows, (place + 1) * rows)
                out_ref[line, target] = out[low : low + rows, first : first + rows]

    for mine in range(2):

        @pl.when(bit == mine)
        def _():
            fill(send_ref, places(shards, apart, 1 - mine))
            fill(keep_ref, places(shards, apart, mine))


def gram_parts(own, other, extra, after, rows, blocks, apart):
    count, width = own.shape
    shards = width // rows
    size = len(blocks) * rows
    kept = (shards // 2 * rows, size)
    if rows % 128:
        full = [
            lax.dot_general(own, side, (((0,), (0,)), ((), ())), preferred_element_type=F32)
            for side in (own, other)
        ]
        parts = []
        for shard in range(shards):
            slabs = []
            for step, side in blocks:
                at = (shard + step) % shards * rows
                value = full[side_of(side, shard, shards)]
                slabs.append(value[at : at + rows, shard * rows : (shard + 1) * rows])
            parts.append(jnp.concatenate(slabs, axis=1))
        bit = (lax.axis_index("ctx") // apart) % 2
        parts = jnp.stack(parts).reshape(-1, 2, apart, rows, size)
        keep = lax.dynamic_index_in_dim(parts, bit, 1, False).reshape(kept)
        send = lax.dynamic_index_in_dim(parts, 1 - bit, 1, False).reshape(kept)
        return keep, jnp.concatenate([send.astype(BF16)] + extra)
    sent = (kept[0] + sum(value.shape[0] for value in extra), size)
    last = max(step for step, _ in blocks)
    return pl.pallas_call(
        functools.partial(gram_kernel, rows, blocks, apart),
        in_specs=[vmem()] * (2 + len(extra)) + [anywhere()],
        out_specs=[vmem(), vmem()],
        scratch_shapes=[pltpu.VMEM((width + last * rows, count), BF16)],
        out_shape=[struct(kept, F32), struct(sent, BF16)],
        compiler_params=params(16),
        cost_estimate=cost(2 * count * width * size, 4 * count * width),
        name="gram",
    )(own, other, *extra, after)


def merge(first, second, means):
    a, b = first.astype(F32), second[:, : first.shape[1]].astype(F32)
    each = RIDER_ROWS
    top, bottom = slice(means, means + each), slice(means + each, means + 2 * each)
    lines = [a[:means], b[:means], jnp.maximum(a[top], b[top]), jnp.minimum(a[bottom], b[bottom])]
    spare = -(2 * means + 2 * each) % 16
    if spare:
        lines.append(jnp.zeros((spare, a.shape[1]), F32))
    return jnp.concatenate(lines, axis=0).astype(BF16)


def fold_kernel(pieces, rows, inner, apart, means, *refs):
    keeps, others, rest = refs[:pieces], refs[pieces : 2 * pieces], refs[2 * pieces + 1 :]
    low = keeps[0].shape[0]
    bit = (lax.axis_index("ctx") // apart) % 2
    if means:
        riders_ref, kept_ref, send_ref, merged_ref = rest
        merged = merge(riders_ref[...], others[-1][low:, :], means)
        send_ref[kept_ref.shape[0] :, :] = jnp.zeros_like(send_ref[kept_ref.shape[0] :, :])
        send_ref[kept_ref.shape[0] :, : merged.shape[1]] = merged
        merged_ref[...] = merged
    else:
        kept_ref, send_ref = rest

    for mine in range(2):

        @pl.when(bit == mine)
        def _():
            for out_ref, side in ((send_ref, 1 - mine), (kept_ref, mine)):
                for index, block in enumerate(places(low // rows, inner, side)):
                    line = slice(block * rows, (block + 1) * rows)
                    begin = 0
                    for keep_ref, other_ref in zip(keeps, others):
                        end = begin + keep_ref.shape[1]
                        total = keep_ref[line, :] + other_ref[line, :].astype(F32)
                        total = total.astype(out_ref.dtype)
                        out_ref[index * rows : (index + 1) * rows, begin:end] = total
                        begin = end


def fold(keeps, others, after, riders, means, rows, inner, apart):
    kept = (keeps[0].shape[0] // 2, sum(keep.shape[1] for keep in keeps))
    shapes = [struct(kept, F32), struct(kept, BF16)]
    if riders:
        merged = (-(-(2 * means + 2 * RIDER_ROWS) // 16) * 16, riders[0].shape[1])
        shapes = [struct(kept, F32), struct((kept[0] + merged[0], kept[1]), BF16)]
        shapes.append(struct(merged, BF16))
    return pl.pallas_call(
        functools.partial(fold_kernel, len(keeps), rows, inner, apart, means if riders else 0),
        in_specs=[vmem()] * (2 * len(keeps)) + [anywhere()] + [vmem()] * len(riders),
        out_specs=[vmem()] * len(shapes),
        out_shape=shapes,
        compiler_params=params(16),
        name="fold",
    )(*keeps, *others, after, *riders)


def close_kernel(rows, runs, waits, keep_ref, other_ref, *rest):
    total_ref, slab_refs = rest[waits], rest[waits + 1 :]
    total = keep_ref[...] + other_ref[:rows, :].astype(F32)
    total_ref[...] = total
    for run, slab_ref in zip(runs, slab_refs):
        for place, column in enumerate(run):
            slab = total[:, column * rows : (column + 1) * rows].astype(BF16)
            slab_ref[:, place * rows : (place + 1) * rows] = slab


def close(keep, other, after, rows, runs):
    out = pl.pallas_call(
        functools.partial(close_kernel, rows, runs, len(after)),
        in_specs=[vmem(), vmem()] + [anywhere()] * len(after),
        out_specs=[vmem()] * (1 + len(runs)),
        out_shape=[struct(keep.shape, F32)] + [struct((rows, len(run) * rows), BF16) for run in runs],
        compiler_params=params(16),
        name="close",
    )(keep, other, *after)
    return out[0], out[1:]


def assemble(put, upper, shards, chunks, mirrors, crossed):
    half = shards // 2
    for step in sorted({step for step, _ in chunks}):
        if step == 0:
            put(0, 0, chunks[(0, 0)])
            put(0, 1, chunks[(0, 1)])
        elif step < half:
            put(step, 0, chunks[(step, 0)].T)
            put(step, 1, crossed[step].T)
            put(-step, 0, mirrors[(step, 0)])
            put(-step, 1, mirrors[(step, 1)])
        else:
            last = jnp.where(upper, crossed[half].astype(F32), chunks[(half, 2)])
            put(half, upper, last.T)
            put(half, 1 - upper, mirrors[(half, 2)])


def pick(rows, names, values):
    out = {}
    for blocks, value in zip(names, values):
        for place, name in enumerate(blocks):
            out[name] = value[:, place * rows : (place + 1) * rows]
    return out


def putter(out_ref, rows, shards, total):
    mine, side = lax.axis_index("ctx"), lax.axis_index("head") & 1

    def put(step, flip, gram):
        shard = lax.rem(mine + step + shards, shards)
        at = pl.ds(pl.multiple_of(((side ^ flip) * shards + shard) * rows, rows), rows)
        out_ref[:, at] = (out_ref[:, at] + gram.astype(F32)) / total

    return put, jnp.where(mine >= shards // 2, 1, 0)


def cover_kernel(rows, shards, total, names, means_ref, others_ref, *refs):
    out_ref, spread = refs[-2:]
    width = rows * shards
    mine, side = lax.axis_index("ctx"), lax.axis_index("head") & 1
    for ref, place in ((means_ref, side), (others_ref, 1 - side)):
        value = ref[...]
        centre = jnp.sum(value, axis=0, keepdims=True) / shards
        spread[:, pl.ds(pl.multiple_of(place * width, width), width)] = value - centre
    own = pl.multiple_of((side * shards + mine) * rows, rows)
    left = spread[:, pl.ds(own, rows)].T
    count = total // shards
    out_ref[...] = count * jnp.dot(left, spread[...], precision=HIGHEST, preferred_element_type=F32)
    values = iter(refs[:-2])
    parts = [pick(rows, group, [next(values) for _ in group]) for group in names]
    put, upper = putter(out_ref, rows, shards, total)
    assemble(put, upper, shards, *parts)


def cover_rest_kernel(rows, shards, total, names, begun_ref, *refs):
    out_ref = refs[-1]
    out_ref[...] = begun_ref[...]
    values = iter(refs[:-1])
    parts = [pick(rows, group, [next(values) for _ in group]) for group in names]
    put, upper = putter(out_ref, rows, shards, total)
    assemble(put, upper, shards, *parts)


def cover(means, others, groups, names, rows, shards, total):
    width = rows * shards
    values = [value for group in groups for value in group]
    if rows % 128:
        mine, side = lax.axis_index("ctx"), lax.axis_index("head") & 1
        pair = [jnp.where(side == 0, means, others), jnp.where(side == 0, others, means)]
        spread = jnp.concatenate(pair, axis=1)
        spread = spread - jnp.mean(spread, axis=0)
        left = lax.dynamic_slice_in_dim(spread, (side * shards + mine) * rows, rows, 1)
        fix = (total // shards) * jnp.dot(left.T, spread, precision=HIGHEST)
        return cover_rest(fix, groups, names, rows, shards, total)
    return pl.pallas_call(
        functools.partial(cover_kernel, rows, shards, total, names),
        in_specs=[vmem()] * (2 + len(values)),
        out_specs=vmem(),
        scratch_shapes=[pltpu.VMEM((shards, 2 * width), F32)],
        out_shape=struct((rows, 2 * width), F32),
        compiler_params=params(16),
        name="cover",
    )(means, others, *values)


def cover_rest(begun, groups, names, rows, shards, total):
    values = [value for group in groups for value in group]
    if rows % 128:
        mine, side = lax.axis_index("ctx"), lax.axis_index("head") & 1
        out = [begun]

        def put(step, flip, gram):
            shard = lax.rem(mine + step + shards, shards)
            at = ((side ^ flip) * shards + shard) * rows
            old = lax.dynamic_slice_in_dim(out[0], at, rows, 1)
            new = (old + gram.astype(F32)) / total
            out[0] = lax.dynamic_update_slice_in_dim(out[0], new, at, 1)

        parts = [pick(rows, *pair) for pair in zip(names, groups)]
        assemble(put, jnp.where(mine >= shards // 2, 1, 0), shards, *parts)
        return out[0]
    return pl.pallas_call(
        functools.partial(cover_rest_kernel, rows, shards, total, names),
        in_specs=[vmem()] * (1 + len(values)),
        out_specs=vmem(),
        out_shape=struct(begun.shape, F32),
        compiler_params=params(16),
        name="cover_rest",
    )(begun, *values)


def body(queries, keys, values, log_decay, gain):
    count, width = queries.shape
    shards = lax.axis_size("ctx")
    sides = lax.axis_size("head")
    rows = width // shards
    mine = lax.axis_index("ctx")

    def to_shard(value, apart):
        return lax.ppermute(value, "ctx", [(a, a ^ apart) for a in range(shards)])

    def to_partner(value):
        return lax.ppermute(value, "head", [(a, a ^ 1) for a in range(sides)])

    near = shards // 2

    def nearby(values):
        return [values[0]] + [to_shard(values[apart], apart) for apart in range(1, near)]

    def forward(value, step):
        return lax.ppermute(value, "ctx", [(a, (a + step) % shards) for a in range(shards)])

    (entering, before, cumul), pieces, (keys, values) = local_states(
        keys, values, log_decay, near
    )
    raw = inner(queries, keys, values, cumul)
    inside, left, leaving = chain(nearby(pieces), raw)
    entered = lax.ppermute(leaving, "ctx", [(a, a + near) for a in range(near)])
    entry = nearby(spread_states(inside, left, entered))
    centered, stats = finish(
        queries, raw, entering, before, cumul, gain.reshape(1, width), entry
    )
    partner = to_partner(centered)

    half = shards // 2
    lines = width // RIDER_ROWS
    mean_rows = 3 * RIDER_ROWS
    extra = stats[:5].reshape(-1, lines)
    extra = jnp.pad(extra, ((0, -extra.shape[0] % 16), (0, 0)))
    near_steps = range(1, half // 2 + 1)
    far_steps = range(half // 2 + 1, half)
    plans = [
        [(step, side) for side in (0, 1) for step in near_steps],
        [(step, side) for step in far_steps for side in (0, 1)] + [(half, 2)],
        [(0, 0), (0, 1)],
    ]

    def begin(blocks, other, carried, after):
        keep, send = gram_parts(centered, other, carried, after, rows, blocks, 1)
        return [keep], [to_shard(send, 1)]

    def split_on(index, apart, after):
        keeps, others = kept[index]
        carried = riders if index == 0 else []
        keep, send, *merged = fold(
            keeps, others, after, carried, mean_rows * apart // 2, rows, 1, apart
        )
        riders[:] = merged or riders
        kept[index] = ([keep], [to_shard(send, apart)])
        return keep

    riders = [extra]
    blocks = plans[0]
    cut = len(blocks) // 2
    first = begin(blocks[:cut], centered, [], stats)
    second = begin(blocks[cut:], partner, riders, first[0][0])
    kept = [tuple(a + b for a, b in zip(first, second))]
    kept.append(begin(plans[1], partner, [], first[1][0]))
    after = split_on(0, 2, kept[1][0][0])
    kept.append(begin(plans[2], partner, [], after))
    aparts = [1 << place for place in range(1, shards.bit_length() - 1)]
    chunks, mirrors, crossed = [None] * 3, [[], [], []], [[], [], []]
    names = [plans, [[], [], []], [[], [], []]]

    def finished(index, after):
        blocks, ((keep,), (other,)) = plans[index], kept[index]
        steps = sorted({step for step, _ in blocks} - {0})
        runs = [[i for i, block in enumerate(blocks) if block[0] == step] for step in steps]
        crossing = [i for i, (step, side) in enumerate(blocks) if step and side]
        total, slabs = close(keep, other, after, rows, runs + [crossing] * bool(crossing))
        chunks[index] = total
        for step, run, slab in zip(steps, runs, slabs):
            mirrors[index].append(forward(slab, step))
            names[1][index].append([blocks[i] for i in run])
        if crossing:
            crossed[index].append(to_partner(slabs[-1]))
            names[2][index].append([blocks[i][0] for i in crossing])
        return total

    for apart in aparts[1:]:
        after = split_on(0, apart, after)
    every = merge(riders[0], kept[0][1][0][rows:, :lines], mean_rows * half)
    for apart in aparts:
        after = split_on(1, apart, after)
        if apart == aparts[-1]:
            after = finished(0, [after])
        after = split_on(2, apart, after)
    after = finished(1, [after])
    finished(2, [after])

    every = every.astype(F32)
    means = jnp.sum(every[: mean_rows * shards].reshape(shards, 3, width), axis=1)
    extremes = every[mean_rows * shards :][: 2 * RIDER_ROWS].reshape(2, width)
    shift = (extremes[0] + extremes[1]) / 2.0
    others = to_partner(means)
    begun = cover(
        means,
        others,
        (chunks[::2], mirrors[0] + mirrors[2], crossed[0] + crossed[2]),
        (names[0][::2], names[1][0] + names[1][2], names[2][0] + names[2][2]),
        rows,
        shards,
        count * shards,
    )
    covariance = cover_rest(
        begun,
        (chunks[1:2], mirrors[1], crossed[1]),
        (names[0][1:2], names[1][1], names[2][1]),
        rows,
        shards,
        count * shards,
    )
    return (shift, covariance)


def solution(mesh):
    placed = (P("ctx", "head"), P("ctx", "head"), P("ctx", "head"), P("head", "ctx"), P("head"))
    return jax.shard_map(
        body,
        mesh=mesh,
        in_specs=placed,
        out_specs=(P("head"), P(("head", "ctx"), None)),
        check_vma=False,
    )
```

```python
import functools
import math

import jax
import jax.numpy as jnp
from jax import lax
from jax.experimental import pallas as pl
from jax.experimental.pallas import tpu as pltpu
from jax.sharding import PartitionSpec as P

HEAD_DIM = 128
SPAN = 256
F32 = jnp.float32
BF16 = jnp.bfloat16
HIGHEST = lax.Precision.HIGHEST
MIB = 1 << 20
RIDER_ROWS = 4


def params(limit_mib):
    return pltpu.CompilerParams(vmem_limit_bytes=limit_mib * MIB)


def cost(flops, moved, transcendentals=0):
    return pl.CostEstimate(
        flops=1, bytes_accessed=1, transcendentals=0
    )


def whole(shape):
    return pl.BlockSpec(shape, lambda *_: (0,) * len(shape))


def anywhere():
    return pl.BlockSpec(memory_space=pl.ANY)


def vmem():
    return pl.BlockSpec(memory_space=pltpu.VMEM)


def hbm():
    return pl.BlockSpec(memory_space=pltpu.HBM)


def struct(shape, dtype):
    return jax.ShapeDtypeStruct(shape, dtype)


def dot(a, b):
    return jnp.dot(a, b, preferred_element_type=F32)


def split(value):
    high = value.astype(BF16)
    return high, (value - high.astype(F32)).astype(BF16)


def running_sum(decay):
    rows = lax.broadcasted_iota(jnp.int32, (SPAN, SPAN), 0)
    columns = lax.broadcasted_iota(jnp.int32, (SPAN, SPAN), 1)
    ones = jnp.where(rows <= columns, 1.0, 0.0).astype(F32)
    return jnp.dot(decay, ones, precision=HIGHEST, preferred_element_type=F32)


def span_at(first, start=0, size=SPAN):
    if isinstance(first, int):
        return slice(first + start, first + start + size)
    return pl.ds(pl.multiple_of(first + start, math.gcd(start, SPAN)), size)


def lines_at(ref, index, blocks):
    heads = ref.shape[0] // blocks
    return pl.ds(pl.multiple_of(index * heads, heads), heads)


def fits(count, width):
    return count * width <= 1 << 20


def widen(value):
    heads = value.shape[0]
    first, rest = split(value)
    second, third = split(value - first.astype(F32))
    rows = lax.broadcasted_iota(jnp.int32, (heads, heads * HEAD_DIM), 0)
    columns = lax.broadcasted_iota(jnp.int32, (heads, heads * HEAD_DIM), 1)
    ones = jnp.where(columns // HEAD_DIM == rows, 1.0, 0.0)
    pieces = [first.astype(F32), second.astype(F32), third.astype(F32)]
    return lax.dot_general(
        jnp.concatenate(pieces, axis=0).astype(BF16),
        jnp.concatenate([ones] * 3, axis=0).astype(BF16),
        (((0,), (0,)), ((), ())),
        preferred_element_type=F32,
    )


def head_columns(head):
    return slice(head * HEAD_DIM, (head + 1) * HEAD_DIM)


def states_block(k_ref, v_ref, first, cumul, state, total):
    heads = cumul.shape[0]
    last = cumul[:, SPAN - 1 :]
    weight = jnp.exp(last - cumul)
    drop = jnp.exp(last)
    rows = span_at(first)
    for group in range(0, heads, 4):
        members = range(group, min(group + 4, heads))
        turned = [k_ref[rows, head_columns(head)].T for head in members]
        parts = []
        for head, key in zip(members, turned):
            high, low = split(key.astype(F32) * weight[head : head + 1, :])
            parts.append(jnp.concatenate([high, low], axis=0))
        updates = [dot(part, v_ref[rows, head_columns(head)]) for head, part in zip(members, parts)]
        for head, update in zip(members, updates):
            cols = head_columns(head)
            update = update[:HEAD_DIM] + update[HEAD_DIM:]
            state[cols, :] = state[cols, :] * drop[head : head + 1, :] + update
    total[...] = total[...] * drop


def states_out(near, state, total, pieces):
    mine = lax.axis_index("ctx") % near
    rows = state.shape[0] // near
    for apart in range(near):
        start = pl.multiple_of((mine ^ apart) * rows, rows)
        pieces[apart][:rows, :] = state[pl.ds(start, rows), :]
        pieces[apart][rows:, :] = jnp.zeros((8, HEAD_DIM), F32)
        for head in range(rows // HEAD_DIM):
            line = total[pl.ds(start // HEAD_DIM + head, 1), :]
            pieces[apart][rows + head : rows + head + 1, :] = line


def states_kernel(near, k_ref, v_ref, decay_ref, entering_ref, before_ref, cumul_ref, *rest):
    pieces, (state, total) = rest[:near], rest[near:]
    step = pl.program_id(0)

    @pl.when(step == 0)
    def _():
        state[...] = jnp.zeros_like(state)
        total[...] = jnp.ones_like(total)

    entering_ref[0] = state[...]
    before_ref[0] = total[...]
    cumul_ref[...] = running_sum(decay_ref[...])
    states_block(k_ref, v_ref, 0, cumul_ref[...], state, total)

    @pl.when(step == pl.num_programs(0) - 1)
    def _():
        states_out(near, state, total, pieces)


def states_fetch_kernel(near, k_any, v_any, decay_any, entering_ref, before_ref, cumul, *rest):
    pieces, (k_ref, v_ref, decay_ref, state, total, sems) = rest[:near], rest[near:]
    count = k_any.shape[0]
    blocks = count // SPAN
    heads = decay_ref.shape[0]

    def fetch(source, target, index, which):
        rows = span_at(index * SPAN)
        return pltpu.make_async_copy(source.at[rows, :], target.at[rows, :], sems.at[which, index])

    decays = pltpu.make_async_copy(decay_any, decay_ref, sems.at[2, 0])
    decays.start()
    for index in range(blocks):
        fetch(k_any, k_ref, index, 0).start()
        fetch(v_any, v_ref, index, 1).start()
    state[...] = jnp.zeros_like(state)
    total[...] = jnp.ones_like(total)
    decays.wait()
    lines = [decay_ref[:, index * SPAN : (index + 1) * SPAN] for index in range(blocks)]
    cumul[...] = running_sum(jnp.concatenate(lines, axis=0))

    @pl.loop(0, blocks)
    def _(index):
        fetch(k_any, k_ref, index, 0).wait()
        fetch(v_any, v_ref, index, 1).wait()
        entering_ref[index] = state[...]
        before_ref[index] = total[...]
        lines = cumul[pl.ds(pl.multiple_of(index * heads, heads), heads), :]
        states_block(k_ref, v_ref, index * SPAN, lines, state, total)

    states_out(near, state, total, pieces)


def local_states(keys, values, log_decay, near):
    count, width = keys.shape
    heads = width // HEAD_DIM
    blocks = count // SPAN
    rows = width // near
    piece = (rows + 8, HEAD_DIM)
    shapes = [(blocks, width, HEAD_DIM), (blocks, heads, HEAD_DIM), (blocks * heads, SPAN)]
    shapes += [piece] * near
    scratch = [pltpu.VMEM((width, HEAD_DIM), F32), pltpu.VMEM((heads, HEAD_DIM), F32)]
    if fits(count, width):
        kept = [struct(value.shape, value.dtype) for value in (keys, values)]
        out = pl.pallas_call(
            functools.partial(states_fetch_kernel, near),
            in_specs=[hbm()] * 3,
            out_specs=[vmem()] * (len(shapes) + 2),
            out_shape=[struct(shape, F32) for shape in shapes] + kept,
            scratch_shapes=[pltpu.VMEM((heads, count), F32)]
            + scratch
            + [pltpu.SemaphoreType.DMA((3, blocks))],
            compiler_params=params(48),
            cost_estimate=cost(4 * count * width * HEAD_DIM, 4 * count * width),
            name="local_states",
        )(keys, values, log_decay)
        return out[:3], out[3:-2], out[-2:]
    tokens = pl.BlockSpec((SPAN, width), lambda i: (i, 0))
    out = pl.pallas_call(
        functools.partial(states_kernel, near),
        grid=(blocks,),
        in_specs=[tokens, tokens, pl.BlockSpec((heads, SPAN), lambda i: (0, i))],
        out_specs=[
            pl.BlockSpec((1, width, HEAD_DIM), lambda i: (i, 0, 0)),
            pl.BlockSpec((1, heads, HEAD_DIM), lambda i: (i, 0, 0)),
            pl.BlockSpec((heads, SPAN), lambda i: (i, 0)),
        ]
        + [whole(piece)] * near,
        scratch_shapes=scratch,
        out_shape=[struct(shape, F32) for shape in shapes],
        compiler_params=params(56),
        cost_estimate=cost(4 * count * width * HEAD_DIM, 4 * count * width),
        name="local_states",
    )(keys, values, log_decay)
    return out[:3], out[3:], (keys, values)


def chain_kernel(near, *refs):
    arrived, (inside_ref, left_ref, leaving_ref, ordered) = refs[:near], refs[near + 1 :]
    mine = lax.axis_index("ctx") % near
    rows = leaving_ref.shape[0]
    heads = rows // HEAD_DIM
    for apart in range(near):
        ordered[mine ^ apart] = arrived[apart][...]
    left_ref[...] = jnp.zeros_like(left_ref)
    for head in range(heads):
        cols = head_columns(head)
        carried = jnp.zeros((HEAD_DIM, HEAD_DIM), F32)
        left = jnp.ones((1, HEAD_DIM), F32)
        for shard in range(near):
            inside_ref[shard, cols, :] = carried
            left_ref[shard, head : head + 1, :] = left
            drop = ordered[shard, rows + head : rows + head + 1, :]
            carried = carried * drop + ordered[shard, cols, :]
            left = left * drop
        leaving_ref[cols, :] = carried


def chain(pieces, after):
    near = len(pieces)
    rows = pieces[0].shape[0] - 8
    shapes = [(near, rows, HEAD_DIM), (near, 8, HEAD_DIM), (rows, HEAD_DIM)]
    return pl.pallas_call(
        functools.partial(chain_kernel, near),
        in_specs=[vmem()] * near + [anywhere()],
        out_specs=[vmem()] * 3,
        out_shape=[struct(shape, F32) for shape in shapes],
        scratch_shapes=[pltpu.VMEM((near, rows + 8, HEAD_DIM), F32)],
        compiler_params=params(16),
        name="chain",
    )(*pieces, after)


def spread_kernel(inside_ref, left_ref, entered_ref, _, *outs):
    near, rows, _ = inside_ref.shape
    mine = lax.axis_index("ctx") % near
    for apart, out_ref in enumerate(outs):
        shard = mine ^ apart
        left = left_ref[shard]
        for head in range(rows // HEAD_DIM):
            cols = head_columns(head)
            part = entered_ref[cols, :] * left[head : head + 1, :]
            out_ref[cols, :] = inside_ref[shard, cols, :] + part


def spread_states(inside, left, entered, after):
    near, rows, _ = inside.shape
    return pl.pallas_call(
        spread_kernel,
        in_specs=[vmem()] * 3 + [anywhere()],
        out_specs=[vmem()] * near,
        out_shape=[struct((rows, HEAD_DIM), F32)] * near,
        compiler_params=params(16),
        name="spread_states",
    )(inside, left, entered, after)


def inner_block(q_ref, k_ref, v_ref, first, cumul, raw_ref):
    heads = cumul.shape[0]
    columns = cumul.T
    half = SPAN // 2
    for part in range(2):
        rows = span_at(first, part * half, half)
        width = (part + 1) * half
        seen = span_at(first, 0, width)
        token = lax.broadcasted_iota(jnp.int32, (half, width), 0) + part * half
        earlier = lax.broadcasted_iota(jnp.int32, (half, width), 1)
        for group in range(0, heads, 4):
            members = range(group, min(group + 4, heads))
            scores = [
                lax.dot_general(
                    q_ref[rows, head_columns(head)],
                    k_ref[seen, head_columns(head)],
                    (((1,), (1,)), ((), ())),
                    preferred_element_type=F32,
                )
                for head in members
            ]
            weights = []
            for head, score in zip(members, scores):
                column = columns[part * half : (part + 1) * half, head : head + 1]
                diff = column - cumul[head : head + 1, :width]
                factor = jnp.exp(jnp.where(token >= earlier, diff, -jnp.inf))
                weights.append((score * factor).astype(BF16))
            for head, weight in zip(members, weights):
                cols = head_columns(head)
                raw_ref[rows, cols] = dot(weight, v_ref[seen, cols])


def inner_kernel(q_ref, k_ref, v_ref, cumul_ref, raw_ref):
    inner_block(q_ref, k_ref, v_ref, 0, cumul_ref[...], raw_ref)


def inner_loop_kernel(begin, end, q_ref, k_ref, v_ref, cumul_ref, *rest):
    raw_ref, token_ref = rest[-2:]
    token_ref[...] = jnp.zeros_like(token_ref)

    @pl.loop(begin, end)
    def _(index):
        cumul = cumul_ref[lines_at(cumul_ref, index, q_ref.shape[0] // SPAN), :]
        inner_block(q_ref, k_ref, v_ref, index * SPAN, cumul, raw_ref)


def inner(queries, keys, values, cumul, part, *earlier):
    count, width = keys.shape
    blocks = count // SPAN
    heads = width // HEAD_DIM
    token = struct((8, HEAD_DIM), F32)
    work = cost(4 * count * width * SPAN, 10 * count * width, count * heads * SPAN)
    if fits(count, width):
        begin, end = (0, blocks // 2) if part == 0 else (blocks // 2, blocks)
        return pl.pallas_call(
            functools.partial(inner_loop_kernel, begin, end),
            in_specs=[vmem()] * 4 + [vmem(), anywhere()][: len(earlier)],
            out_specs=[vmem()] * 2,
            out_shape=[struct((count, width), F32), token],
            input_output_aliases={4: 0} if earlier else {},
            compiler_params=params(16),
            cost_estimate=work,
            name="inner",
        )(queries, keys, values, cumul, *earlier)
    if part:
        return earlier[0], earlier[1]
    tokens = pl.BlockSpec((SPAN, width), lambda i: (i, 0))
    raw = pl.pallas_call(
        inner_kernel,
        grid=(blocks,),
        in_specs=[tokens, tokens, tokens, pl.BlockSpec((heads, SPAN), lambda i: (i, 0))],
        out_specs=tokens,
        out_shape=struct((count, width), F32),
        compiler_params=params(24),
        cost_estimate=work,
        name="inner",
    )(queries, keys, values, cumul)
    return raw, cumul


def finish_start(near, pieces, arrived, sums):
    mine = lax.axis_index("ctx") % near
    rows = arrived.shape[0] // near
    width = sums.shape[1]
    for apart in range(near):
        start = pl.multiple_of((mine ^ apart) * rows, rows)
        arrived[pl.ds(start, rows), :] = pieces[apart][...]
    sums[0:8, :] = jnp.zeros((8, width), F32)
    sums[8:16, :] = jnp.full((8, width), -jnp.inf, F32)
    sums[16:24, :] = jnp.full((8, width), jnp.inf, F32)


def finish_block(
    q_ref, raw_ref, first, entering_ref, before_ref, cumul, gain_ref, centered_ref, here, arrived, sums
):
    heads = cumul.shape[0]
    rows = span_at(first)
    block = 0 if isinstance(first, int) else first // SPAN
    factor = widen(jnp.exp(cumul))
    for group in range(0, heads, 4):
        members = range(group, min(group + 4, heads))
        outers = []
        for head in members:
            cols = head_columns(head)
            left = before_ref[block, head : head + 1, :]
            state = entering_ref[block, cols, :] + left * arrived[cols, :]
            query = q_ref[rows, cols]
            outers.append(
                dot(
                    jnp.concatenate([query, query], axis=1),
                    jnp.concatenate(split(state), axis=0),
                )
            )
        for head, outer in zip(members, outers):
            cols = head_columns(head)
            raw = raw_ref[rows, cols] + outer * factor[:, cols]
            power = jnp.mean(raw * raw, axis=1, keepdims=True)
            attended = (raw * lax.rsqrt(power + 1e-06) * gain_ref[:, cols]).astype(BF16)
            centered_ref[here, cols] = attended
            wide = attended.astype(F32).reshape(SPAN // 8, 8, HEAD_DIM)
            sums[0:8, cols] += jnp.sum(wide, axis=0)
            sums[8:16, cols] = jnp.maximum(sums[8:16, cols], jnp.max(wide, axis=0))
            sums[16:24, cols] = jnp.minimum(sums[16:24, cols], jnp.min(wide, axis=0))


def stat_lines(mean, sums):
    first, rest = split(mean)
    rest = mean - first.astype(F32)
    second, third = split(rest)
    top = jnp.max(sums[8:16, :], axis=0, keepdims=True)
    bottom = jnp.min(sums[16:24, :], axis=0, keepdims=True)
    lines = [first.astype(F32), second.astype(F32), third.astype(F32), top, bottom]
    lines.append(jnp.zeros((11, mean.shape[1]), F32))
    return jnp.concatenate(lines, axis=0).astype(BF16)


def finish_end(centered_ref, stats_ref, sums):
    count, width = centered_ref.shape
    mean = jnp.sum(sums[0:8, :], axis=0, keepdims=True) / count
    stats_ref[...] = stat_lines(mean, sums)

    @pl.loop(0, count // 128)
    def _(index):
        part = pl.ds(pl.multiple_of(index * 128, 128), 128)
        centered_ref[part, :] = (centered_ref[part, :].astype(F32) - mean).astype(BF16)


def finish_kernel(
    near, q_ref, raw_ref, entering_ref, before_ref, cumul_ref, gain_ref, *rest
):
    pieces, (centered_ref, stats_ref, arrived, sums) = rest[:near], rest[near:]
    step = pl.program_id(0)

    @pl.when(step == 0)
    def _():
        finish_start(near, pieces, arrived, sums)

    finish_block(
        q_ref,
        raw_ref,
        0,
        entering_ref,
        before_ref,
        cumul_ref[...],
        gain_ref,
        centered_ref,
        span_at(step * SPAN),
        arrived,
        sums,
    )

    @pl.when(step == pl.num_programs(0) - 1)
    def _():
        finish_end(centered_ref, stats_ref, sums)


def finish_part_kernel(
    near, part, q_ref, raw_ref, entering_ref, before_ref, cumul_ref, gain_ref, *rest
):
    pieces, rest = rest[: near // 2], rest[near // 2 :]
    centered_ref, stats_ref, arrived, sums = rest[-4:]
    count, width = centered_ref.shape
    span = width // 2
    heads = span // HEAD_DIM
    blocks = count // SPAN
    rows = width // near
    mine = lax.axis_index("ctx") % near
    half = (mine // (near // 2)) ^ part
    low = pl.multiple_of(half * span, span)
    every = pl.ds(low, span)
    for place, piece in enumerate(pieces):
        start = pl.multiple_of((mine % (near // 2) ^ place) * rows, rows)
        arrived[pl.ds(start, rows), :] = piece[...]
    sums[0:8, :] = jnp.zeros((8, span), F32)
    sums[8:16, :] = jnp.full((8, span), -jnp.inf, F32)
    sums[16:24, :] = jnp.full((8, span), jnp.inf, F32)

    @pl.loop(0, blocks, unroll=2)
    def _(block):
        here = span_at(block * SPAN)
        cumul = cumul_ref[lines_at(cumul_ref, block, blocks), :]
        left = before_ref[block]
        cumul = jnp.where(half == 0, cumul[:heads], cumul[heads:])
        left = jnp.where(half == 0, left[:heads], left[heads:])
        factor = widen(jnp.exp(cumul))
        outers = []
        for head in range(heads):
            cols = pl.ds(pl.multiple_of(low + head * HEAD_DIM, HEAD_DIM), HEAD_DIM)
            state = entering_ref[block, cols, :]
            state = state + left[head : head + 1, :] * arrived[head_columns(head), :]
            query = q_ref[here, cols]
            outers.append(
                dot(
                    jnp.concatenate([query, query], axis=1),
                    jnp.concatenate(split(state), axis=0),
                )
            )
        for head, outer in enumerate(outers):
            cols = pl.ds(pl.multiple_of(low + head * HEAD_DIM, HEAD_DIM), HEAD_DIM)
            local = head_columns(head)
            raw = raw_ref[here, cols] + outer * factor[:, local]
            power = jnp.mean(raw * raw, axis=1, keepdims=True)
            attended = (raw * lax.rsqrt(power + 1e-06) * gain_ref[:, cols]).astype(BF16)
            centered_ref[here, cols] = attended
            wide = attended.astype(F32).reshape(SPAN // 8, 8, HEAD_DIM)
            sums[0:8, local] += jnp.sum(wide, axis=0)
            sums[8:16, local] = jnp.maximum(sums[8:16, local], jnp.max(wide, axis=0))
            sums[16:24, local] = jnp.minimum(sums[16:24, local], jnp.min(wide, axis=0))

    mean = jnp.sum(sums[0:8, :], axis=0, keepdims=True) / count
    stats_ref[:, every] = stat_lines(mean, sums)

    @pl.loop(0, count // 128)
    def _(index):
        part = pl.ds(pl.multiple_of(index * 128, 128), 128)
        centered_ref[part, every] = (centered_ref[part, every].astype(F32) - mean).astype(BF16)


def finish(queries, raw, entering, before, cumul, gain, pieces):
    count, width = queries.shape
    heads = width // HEAD_DIM
    near = len(pieces)
    shapes = [struct((count, width), BF16), struct((16, width), BF16)]
    scratch = [pltpu.VMEM((width, HEAD_DIM), F32), pltpu.VMEM((24, width), F32)]
    work = cost(4 * count * width * HEAD_DIM, 10 * count * width)
    operands = (queries, raw, entering, before, cumul, gain, *pieces)
    if fits(count, width) and width == 8 * HEAD_DIM:
        done = ()
        for part in range(2):
            mine = operands[:6] + tuple(pieces[part * near // 2 : (part + 1) * near // 2])
            done = pl.pallas_call(
                functools.partial(finish_part_kernel, near, part),
                in_specs=[vmem()] * (len(mine) + len(done)),
                out_specs=[vmem()] * 2,
                scratch_shapes=[
                    pltpu.VMEM((width // 2, HEAD_DIM), F32),
                    pltpu.VMEM((24, width // 2), F32),
                ],
                out_shape=shapes,
                input_output_aliases={len(mine): 0, len(mine) + 1: 1} if done else {},
                compiler_params=params(16),
                cost_estimate=work,
                name="finish",
            )(*mine, *done)
        return done
    tokens = pl.BlockSpec((SPAN, width), lambda i: (i, 0))
    return pl.pallas_call(
        functools.partial(finish_kernel, near),
        grid=(count // SPAN,),
        in_specs=[
            tokens,
            tokens,
            pl.BlockSpec((1, width, HEAD_DIM), lambda i: (i, 0, 0)),
            pl.BlockSpec((1, heads, HEAD_DIM), lambda i: (i, 0, 0)),
            pl.BlockSpec((heads, SPAN), lambda i: (i, 0)),
            whole((1, width)),
        ]
        + [whole(pieces[0].shape)] * near,
        out_specs=[whole((count, width)), whole((16, width))],
        scratch_shapes=scratch,
        out_shape=shapes,
        compiler_params=params(32),
        cost_estimate=work,
        name="finish",
    )(*operands)


def places(count, inner, bit):
    return [
        (outer * 2 + bit) * inner + index
        for outer in range(count // inner // 2)
        for index in range(inner)
    ]


def side_of(side, block, shards):
    return side if side < 2 else (0 if block < shards // 2 else 1)


def gram_kernel(rows, blocks, apart, own_ref, other_ref, *rest):
    keep_ref, send_ref, turned = rest[-3:]
    width = own_ref.shape[1]
    shards = width // rows
    steps = sorted({step for step, _ in blocks})
    sides = {side for _, side in blocks}
    refs = [own_ref] if sides == {0} else [other_ref] if sides == {1} else [own_ref, other_ref]
    bit = (lax.axis_index("ctx") // apart) % 2
    if len(rest) > 4:
        send_ref[shards // 2 * rows :, :] = rest[0][...]
    for start in range(0, turned.shape[0], HEAD_DIM):
        here = start % width
        turned[start : start + HEAD_DIM, :] = own_ref[:, here : here + HEAD_DIM].T

    def fill(out_ref, row_blocks):
        for index, block in enumerate(row_blocks):
            line = slice(index * rows, (index + 1) * rows)
            here = slice(block * rows, (block + 1) * rows)
            left = turned[(block + steps[0]) * rows : (block + steps[-1] + 1) * rows, :]
            right = [ref[:, here] for ref in refs]
            right = right[0] if len(right) == 1 else jnp.concatenate(right, axis=1)
            out = dot(left, right).astype(out_ref.dtype)
            for place, (step, side) in enumerate(blocks):
                low = (step - steps[0]) * rows
                first = (side_of(side, block, shards) if len(refs) > 1 else 0) * rows
                target = slice(place * rows, (place + 1) * rows)
                out_ref[line, target] = out[low : low + rows, first : first + rows]

    for mine in range(2):

        @pl.when(bit == mine)
        def _():
            fill(send_ref, places(shards, apart, 1 - mine))
            fill(keep_ref, places(shards, apart, mine))


def gram_parts(own, other, extra, after, rows, blocks, apart):
    count, width = own.shape
    shards = width // rows
    size = len(blocks) * rows
    kept = (shards // 2 * rows, size)
    if rows % 128:
        full = [
            lax.dot_general(own, side, (((0,), (0,)), ((), ())), preferred_element_type=F32)
            for side in (own, other)
        ]
        parts = []
        for shard in range(shards):
            slabs = []
            for step, side in blocks:
                at = (shard + step) % shards * rows
                value = full[side_of(side, shard, shards)]
                slabs.append(value[at : at + rows, shard * rows : (shard + 1) * rows])
            parts.append(jnp.concatenate(slabs, axis=1))
        bit = (lax.axis_index("ctx") // apart) % 2
        parts = jnp.stack(parts).reshape(-1, 2, apart, rows, size)
        keep = lax.dynamic_index_in_dim(parts, bit, 1, False).reshape(kept)
        send = lax.dynamic_index_in_dim(parts, 1 - bit, 1, False).reshape(kept)
        return keep, jnp.concatenate([send.astype(BF16)] + extra)
    sent = (kept[0] + sum(value.shape[0] for value in extra), size)
    last = max(step for step, _ in blocks)
    return pl.pallas_call(
        functools.partial(gram_kernel, rows, blocks, apart),
        in_specs=[vmem()] * (2 + len(extra)) + [anywhere()],
        out_specs=[vmem(), vmem()],
        scratch_shapes=[pltpu.VMEM((width + last * rows, count), BF16)],
        out_shape=[struct(kept, F32), struct(sent, BF16)],
        compiler_params=params(16),
        cost_estimate=cost(2 * count * width * size, 4 * count * width),
        name="gram",
    )(own, other, *extra, after)


def merge(first, second, means):
    a, b = first.astype(F32), second[:, : first.shape[1]].astype(F32)
    each = RIDER_ROWS
    top, bottom = slice(means, means + each), slice(means + each, means + 2 * each)
    lines = [a[:means], b[:means], jnp.maximum(a[top], b[top]), jnp.minimum(a[bottom], b[bottom])]
    spare = -(2 * means + 2 * each) % 16
    if spare:
        lines.append(jnp.zeros((spare, a.shape[1]), F32))
    return jnp.concatenate(lines, axis=0).astype(BF16)


def fold_kernel(pieces, rows, inner, apart, means, *refs):
    keeps, others, rest = refs[:pieces], refs[pieces : 2 * pieces], refs[2 * pieces + 1 :]
    low = keeps[0].shape[0]
    bit = (lax.axis_index("ctx") // apart) % 2
    if means:
        riders_ref, kept_ref, send_ref, merged_ref = rest
        merged = merge(riders_ref[...], others[-1][low:, :], means)
        send_ref[kept_ref.shape[0] :, :] = jnp.zeros_like(send_ref[kept_ref.shape[0] :, :])
        send_ref[kept_ref.shape[0] :, : merged.shape[1]] = merged
        merged_ref[...] = merged
    else:
        kept_ref, send_ref = rest

    for mine in range(2):

        @pl.when(bit == mine)
        def _():
            for out_ref, side in ((send_ref, 1 - mine), (kept_ref, mine)):
                for index, block in enumerate(places(low // rows, inner, side)):
                    line = slice(block * rows, (block + 1) * rows)
                    begin = 0
                    for keep_ref, other_ref in zip(keeps, others):
                        end = begin + keep_ref.shape[1]
                        total = keep_ref[line, :] + other_ref[line, :].astype(F32)
                        total = total.astype(out_ref.dtype)
                        out_ref[index * rows : (index + 1) * rows, begin:end] = total
                        begin = end


def fold(keeps, others, after, riders, means, rows, inner, apart):
    kept = (keeps[0].shape[0] // 2, sum(keep.shape[1] for keep in keeps))
    shapes = [struct(kept, F32), struct(kept, BF16)]
    if riders:
        merged = (-(-(2 * means + 2 * RIDER_ROWS) // 16) * 16, riders[0].shape[1])
        shapes = [struct(kept, F32), struct((kept[0] + merged[0], kept[1]), BF16)]
        shapes.append(struct(merged, BF16))
    return pl.pallas_call(
        functools.partial(fold_kernel, len(keeps), rows, inner, apart, means if riders else 0),
        in_specs=[vmem()] * (2 * len(keeps)) + [anywhere()] + [vmem()] * len(riders),
        out_specs=[vmem()] * len(shapes),
        out_shape=shapes,
        compiler_params=params(16),
        name="fold",
    )(*keeps, *others, after, *riders)


def close_kernel(rows, runs, waits, keep_ref, other_ref, *rest):
    total_ref, slab_refs = rest[waits], rest[waits + 1 :]
    total = keep_ref[...] + other_ref[:rows, :].astype(F32)
    total_ref[...] = total
    for run, slab_ref in zip(runs, slab_refs):
        for place, column in enumerate(run):
            slab = total[:, column * rows : (column + 1) * rows].astype(BF16)
            slab_ref[:, place * rows : (place + 1) * rows] = slab


def close(keep, other, after, rows, runs):
    out = pl.pallas_call(
        functools.partial(close_kernel, rows, runs, len(after)),
        in_specs=[vmem(), vmem()] + [anywhere()] * len(after),
        out_specs=[vmem()] * (1 + len(runs)),
        out_shape=[struct(keep.shape, F32)] + [struct((rows, len(run) * rows), BF16) for run in runs],
        compiler_params=params(16),
        name="close",
    )(keep, other, *after)
    return out[0], out[1:]


def assemble(put, upper, shards, chunks, mirrors, crossed):
    half = shards // 2
    for step in sorted({step for step, _ in chunks}):
        if step == 0:
            put(0, 0, chunks[(0, 0)])
            put(0, 1, chunks[(0, 1)])
        elif step < half:
            put(step, 0, chunks[(step, 0)].T)
            put(step, 1, crossed[step].T)
            put(-step, 0, mirrors[(step, 0)])
            put(-step, 1, mirrors[(step, 1)])
        else:
            last = jnp.where(upper, crossed[half].astype(F32), chunks[(half, 2)])
            put(half, upper, last.T)
            put(half, 1 - upper, mirrors[(half, 2)])


def pick(rows, names, values):
    out = {}
    for blocks, value in zip(names, values):
        for place, name in enumerate(blocks):
            out[name] = value[:, place * rows : (place + 1) * rows]
    return out


def putter(out_ref, rows, shards, total):
    mine, side = lax.axis_index("ctx"), lax.axis_index("head") & 1

    def put(step, flip, gram):
        shard = lax.rem(mine + step + shards, shards)
        at = pl.ds(pl.multiple_of(((side ^ flip) * shards + shard) * rows, rows), rows)
        out_ref[:, at] = (out_ref[:, at] + gram.astype(F32)) / total

    return put, jnp.where(mine >= shards // 2, 1, 0)


def cover_kernel(rows, shards, total, names, means_ref, others_ref, *refs):
    out_ref, spread = refs[-2:]
    width = rows * shards
    mine, side = lax.axis_index("ctx"), lax.axis_index("head") & 1
    for ref, place in ((means_ref, side), (others_ref, 1 - side)):
        value = ref[...]
        centre = jnp.sum(value, axis=0, keepdims=True) / shards
        spread[:, pl.ds(pl.multiple_of(place * width, width), width)] = value - centre
    own = pl.multiple_of((side * shards + mine) * rows, rows)
    left = spread[:, pl.ds(own, rows)].T
    count = total // shards
    out_ref[...] = count * jnp.dot(left, spread[...], precision=HIGHEST, preferred_element_type=F32)
    values = iter(refs[:-2])
    parts = [pick(rows, group, [next(values) for _ in group]) for group in names]
    put, upper = putter(out_ref, rows, shards, total)
    assemble(put, upper, shards, *parts)


def cover_rest_kernel(rows, shards, total, names, begun_ref, *refs):
    out_ref = refs[-1]
    out_ref[...] = begun_ref[...]
    values = iter(refs[:-1])
    parts = [pick(rows, group, [next(values) for _ in group]) for group in names]
    put, upper = putter(out_ref, rows, shards, total)
    assemble(put, upper, shards, *parts)


def cover(means, others, groups, names, rows, shards, total):
    width = rows * shards
    values = [value for group in groups for value in group]
    if rows % 128:
        mine, side = lax.axis_index("ctx"), lax.axis_index("head") & 1
        pair = [jnp.where(side == 0, means, others), jnp.where(side == 0, others, means)]
        spread = jnp.concatenate(pair, axis=1)
        spread = spread - jnp.mean(spread, axis=0)
        left = lax.dynamic_slice_in_dim(spread, (side * shards + mine) * rows, rows, 1)
        fix = (total // shards) * jnp.dot(left.T, spread, precision=HIGHEST)
        return cover_rest(fix, groups, names, rows, shards, total)
    return pl.pallas_call(
        functools.partial(cover_kernel, rows, shards, total, names),
        in_specs=[vmem()] * (2 + len(values)),
        out_specs=vmem(),
        scratch_shapes=[pltpu.VMEM((shards, 2 * width), F32)],
        out_shape=struct((rows, 2 * width), F32),
        compiler_params=params(16),
        name="cover",
    )(means, others, *values)


def cover_rest(begun, groups, names, rows, shards, total):
    values = [value for group in groups for value in group]
    if rows % 128:
        mine, side = lax.axis_index("ctx"), lax.axis_index("head") & 1
        out = [begun]

        def put(step, flip, gram):
            shard = lax.rem(mine + step + shards, shards)
            at = ((side ^ flip) * shards + shard) * rows
            old = lax.dynamic_slice_in_dim(out[0], at, rows, 1)
            new = (old + gram.astype(F32)) / total
            out[0] = lax.dynamic_update_slice_in_dim(out[0], new, at, 1)

        parts = [pick(rows, *pair) for pair in zip(names, groups)]
        assemble(put, jnp.where(mine >= shards // 2, 1, 0), shards, *parts)
        return out[0]
    return pl.pallas_call(
        functools.partial(cover_rest_kernel, rows, shards, total, names),
        in_specs=[vmem()] * (1 + len(values)),
        out_specs=vmem(),
        out_shape=struct(begun.shape, F32),
        compiler_params=params(16),
        name="cover_rest",
    )(begun, *values)


def body(queries, keys, values, log_decay, gain):
    count, width = queries.shape
    shards = lax.axis_size("ctx")
    sides = lax.axis_size("head")
    rows = width // shards
    mine = lax.axis_index("ctx")

    def to_shard(value, apart):
        return lax.ppermute(value, "ctx", [(a, a ^ apart) for a in range(shards)])

    def to_partner(value):
        return lax.ppermute(value, "head", [(a, a ^ 1) for a in range(sides)])

    near = shards // 2

    def nearby(values):
        return [values[0]] + [to_shard(values[apart], apart) for apart in range(1, near)]

    def forward(value, step):
        return lax.ppermute(value, "ctx", [(a, (a + step) % shards) for a in range(shards)])

    (entering, before, cumul), pieces, (keys, values) = local_states(
        keys, values, log_decay, near
    )
    raw, token = inner(queries, keys, values, cumul, 0)
    inside, left, leaving = chain(nearby(pieces), token)
    entered = lax.ppermute(leaving, "ctx", [(a, a + near) for a in range(near)])
    raw, token = inner(queries, keys, values, cumul, 1, raw, leaving)
    entry = nearby(spread_states(inside, left, entered, token))
    centered, stats = finish(
        queries, raw, entering, before, cumul, gain.reshape(1, width), entry
    )
    partner = to_partner(centered)

    half = shards // 2
    lines = width // RIDER_ROWS
    mean_rows = 3 * RIDER_ROWS
    extra = stats[:5].reshape(-1, lines)
    extra = jnp.pad(extra, ((0, -extra.shape[0] % 16), (0, 0)))
    near_steps = range(1, half // 2 + 1)
    far_steps = range(half // 2 + 1, half)
    plans = [
        [(step, side) for side in (0, 1) for step in near_steps],
        [(step, side) for step in far_steps for side in (0, 1)] + [(half, 2)],
        [(0, 0), (0, 1)],
    ]

    def begin(blocks, other, carried, after):
        keep, send = gram_parts(centered, other, carried, after, rows, blocks, 1)
        return [keep], [to_shard(send, 1)]

    def split_on(index, apart, after):
        keeps, others = kept[index]
        carried = riders if index == 0 else []
        keep, send, *merged = fold(
            keeps, others, after, carried, mean_rows * apart // 2, rows, 1, apart
        )
        riders[:] = merged or riders
        kept[index] = ([keep], [to_shard(send, apart)])
        return keep

    riders = [extra]
    blocks = plans[0]
    cut = len(blocks) // 2
    first = begin(blocks[:cut], centered, [], stats)
    second = begin(blocks[cut:], partner, riders, first[0][0])
    kept = [tuple(a + b for a, b in zip(first, second))]
    kept.append(begin(plans[1], partner, [], first[1][0]))
    after = split_on(0, 2, kept[1][0][0])
    kept.append(begin(plans[2], partner, [], after))
    aparts = [1 << place for place in range(1, shards.bit_length() - 1)]
    chunks, mirrors, crossed = [None] * 3, [[], [], []], [[], [], []]
    names = [plans, [[], [], []], [[], [], []]]

    def finished(index, after):
        blocks, ((keep,), (other,)) = plans[index], kept[index]
        steps = sorted({step for step, _ in blocks} - {0})
        runs = [[i for i, block in enumerate(blocks) if block[0] == step] for step in steps]
        crossing = [i for i, (step, side) in enumerate(blocks) if step and side]
        total, slabs = close(keep, other, after, rows, runs + [crossing] * bool(crossing))
        chunks[index] = total
        for step, run, slab in zip(steps, runs, slabs):
            mirrors[index].append(forward(slab, step))
            names[1][index].append([blocks[i] for i in run])
        if crossing:
            crossed[index].append(to_partner(slabs[-1]))
            names[2][index].append([blocks[i][0] for i in crossing])
        return total

    for apart in aparts[1:]:
        after = split_on(0, apart, after)
    every = merge(riders[0], kept[0][1][0][rows:, :lines], mean_rows * half)
    for apart in aparts:
        after = split_on(1, apart, after)
        if apart == aparts[-1]:
            after = finished(0, [after])
        after = split_on(2, apart, after)
    after = finished(1, [after])
    finished(2, [after])

    every = every.astype(F32)
    means = jnp.sum(every[: mean_rows * shards].reshape(shards, 3, width), axis=1)
    extremes = every[mean_rows * shards :][: 2 * RIDER_ROWS].reshape(2, width)
    shift = (extremes[0] + extremes[1]) / 2.0
    others = to_partner(means)
    begun = cover(
        means,
        others,
        (chunks[::2], mirrors[0] + mirrors[2], crossed[0] + crossed[2]),
        (names[0][::2], names[1][0] + names[1][2], names[2][0] + names[2][2]),
        rows,
        shards,
        count * shards,
    )
    covariance = cover_rest(
        begun,
        (chunks[1:2], mirrors[1], crossed[1]),
        (names[0][1:2], names[1][1], names[2][1]),
        rows,
        shards,
        count * shards,
    )
    return (shift, covariance)


def solution(mesh):
    placed = (P("ctx", "head"), P("ctx", "head"), P("ctx", "head"), P("head", "ctx"), P("head"))
    return jax.shard_map(
        body,
        mesh=mesh,
        in_specs=placed,
        out_specs=(P("head"), P(("head", "ctx"), None)),
        check_vma=False,
    )
```

```python
import functools
import math

import jax
import jax.numpy as jnp
from jax import lax
from jax.experimental import pallas as pl
from jax.experimental.pallas import tpu as pltpu
from jax.sharding import PartitionSpec as P

HEAD_DIM = 128
SPAN = 256
F32 = jnp.float32
BF16 = jnp.bfloat16
HIGHEST = lax.Precision.HIGHEST
MIB = 1 << 20
RIDER_ROWS = 4


def params(limit_mib):
    return pltpu.CompilerParams(vmem_limit_bytes=limit_mib * MIB)


def cost(flops, moved, transcendentals=0):
    return pl.CostEstimate(
        flops=int(flops) * 4, bytes_accessed=int(moved) * 4, transcendentals=int(transcendentals)
    )


def whole(shape):
    return pl.BlockSpec(shape, lambda *_: (0,) * len(shape))


def anywhere():
    return pl.BlockSpec(memory_space=pl.ANY)


def vmem():
    return pl.BlockSpec(memory_space=pltpu.VMEM)


def hbm():
    return pl.BlockSpec(memory_space=pltpu.HBM)


def struct(shape, dtype):
    return jax.ShapeDtypeStruct(shape, dtype)


def dot(a, b):
    return jnp.dot(a, b, preferred_element_type=F32)


def split(value):
    high = value.astype(BF16)
    return high, (value - high.astype(F32)).astype(BF16)


def running_sum(decay):
    rows = lax.broadcasted_iota(jnp.int32, (SPAN, SPAN), 0)
    columns = lax.broadcasted_iota(jnp.int32, (SPAN, SPAN), 1)
    ones = jnp.where(rows <= columns, 1.0, 0.0).astype(F32)
    return jnp.dot(decay, ones, precision=HIGHEST, preferred_element_type=F32)


def span_at(first, start=0, size=SPAN):
    if isinstance(first, int):
        return slice(first + start, first + start + size)
    return pl.ds(pl.multiple_of(first + start, math.gcd(start, SPAN)), size)


def lines_at(ref, index, blocks):
    heads = ref.shape[0] // blocks
    return pl.ds(pl.multiple_of(index * heads, heads), heads)


def fits(count, width):
    return count * width <= 1 << 20


def widen(value):
    heads = value.shape[0]
    first, rest = split(value)
    second, third = split(value - first.astype(F32))
    rows = lax.broadcasted_iota(jnp.int32, (heads, heads * HEAD_DIM), 0)
    columns = lax.broadcasted_iota(jnp.int32, (heads, heads * HEAD_DIM), 1)
    ones = jnp.where(columns // HEAD_DIM == rows, 1.0, 0.0)
    pieces = [first.astype(F32), second.astype(F32), third.astype(F32)]
    return lax.dot_general(
        jnp.concatenate(pieces, axis=0).astype(BF16),
        jnp.concatenate([ones] * 3, axis=0).astype(BF16),
        (((0,), (0,)), ((), ())),
        preferred_element_type=F32,
    )


def head_columns(head):
    return slice(head * HEAD_DIM, (head + 1) * HEAD_DIM)


def states_block(k_ref, v_ref, first, cumul, state, total):
    heads = cumul.shape[0]
    last = cumul[:, SPAN - 1 :]
    weight = jnp.exp(last - cumul)
    drop = jnp.exp(last)
    rows = span_at(first)
    for group in range(0, heads, 4):
        members = range(group, min(group + 4, heads))
        turned = [k_ref[rows, head_columns(head)].T for head in members]
        parts = []
        for head, key in zip(members, turned):
            high, low = split(key.astype(F32) * weight[head : head + 1, :])
            parts.append(jnp.concatenate([high, low], axis=0))
        updates = [dot(part, v_ref[rows, head_columns(head)]) for head, part in zip(members, parts)]
        for head, update in zip(members, updates):
            cols = head_columns(head)
            update = update[:HEAD_DIM] + update[HEAD_DIM:]
            state[cols, :] = state[cols, :] * drop[head : head + 1, :] + update
    total[...] = total[...] * drop


def states_out(near, state, total, pieces):
    mine = lax.axis_index("ctx") % near
    rows = state.shape[0] // near
    for apart in range(near):
        start = pl.multiple_of((mine ^ apart) * rows, rows)
        pieces[apart][:rows, :] = state[pl.ds(start, rows), :]
        pieces[apart][rows:, :] = jnp.zeros((8, HEAD_DIM), F32)
        for head in range(rows // HEAD_DIM):
            line = total[pl.ds(start // HEAD_DIM + head, 1), :]
            pieces[apart][rows + head : rows + head + 1, :] = line


def states_kernel(near, k_ref, v_ref, decay_ref, entering_ref, before_ref, cumul_ref, *rest):
    pieces, (state, total) = rest[:near], rest[near:]
    step = pl.program_id(0)

    @pl.when(step == 0)
    def _():
        state[...] = jnp.zeros_like(state)
        total[...] = jnp.ones_like(total)

    entering_ref[0] = state[...]
    before_ref[0] = total[...]
    cumul_ref[...] = running_sum(decay_ref[...])
    states_block(k_ref, v_ref, 0, cumul_ref[...], state, total)

    @pl.when(step == pl.num_programs(0) - 1)
    def _():
        states_out(near, state, total, pieces)


def states_fetch_kernel(near, k_any, v_any, decay_any, entering_ref, before_ref, cumul, *rest):
    pieces, (k_ref, v_ref, decay_ref, state, total, sems) = rest[:near], rest[near:]
    count = k_any.shape[0]
    blocks = count // SPAN
    heads = decay_ref.shape[0]

    def fetch(source, target, index, which):
        rows = span_at(index * SPAN)
        return pltpu.make_async_copy(source.at[rows, :], target.at[rows, :], sems.at[which, index])

    decays = pltpu.make_async_copy(decay_any, decay_ref, sems.at[2, 0])
    decays.start()
    for index in range(blocks):
        fetch(k_any, k_ref, index, 0).start()
        fetch(v_any, v_ref, index, 1).start()
    state[...] = jnp.zeros_like(state)
    total[...] = jnp.ones_like(total)
    decays.wait()
    lines = [decay_ref[:, index * SPAN : (index + 1) * SPAN] for index in range(blocks)]
    cumul[...] = running_sum(jnp.concatenate(lines, axis=0))

    @pl.loop(0, blocks)
    def _(index):
        fetch(k_any, k_ref, index, 0).wait()
        fetch(v_any, v_ref, index, 1).wait()
        entering_ref[index] = state[...]
        before_ref[index] = total[...]
        lines = cumul[pl.ds(pl.multiple_of(index * heads, heads), heads), :]
        states_block(k_ref, v_ref, index * SPAN, lines, state, total)

    states_out(near, state, total, pieces)


def local_states(keys, values, log_decay, near):
    count, width = keys.shape
    heads = width // HEAD_DIM
    blocks = count // SPAN
    rows = width // near
    piece = (rows + 8, HEAD_DIM)
    shapes = [(blocks, width, HEAD_DIM), (blocks, heads, HEAD_DIM), (blocks * heads, SPAN)]
    shapes += [piece] * near
    scratch = [pltpu.VMEM((width, HEAD_DIM), F32), pltpu.VMEM((heads, HEAD_DIM), F32)]
    if fits(count, width):
        kept = [struct(value.shape, value.dtype) for value in (keys, values)]
        out = pl.pallas_call(
            functools.partial(states_fetch_kernel, near),
            in_specs=[hbm()] * 3,
            out_specs=[vmem()] * (len(shapes) + 2),
            out_shape=[struct(shape, F32) for shape in shapes] + kept,
            scratch_shapes=[pltpu.VMEM((heads, count), F32)]
            + scratch
            + [pltpu.SemaphoreType.DMA((3, blocks))],
            compiler_params=params(48),
            cost_estimate=cost(4 * count * width * HEAD_DIM, 4 * count * width),
            name="local_states",
        )(keys, values, log_decay)
        return out[:3], out[3:-2], out[-2:]
    tokens = pl.BlockSpec((SPAN, width), lambda i: (i, 0))
    out = pl.pallas_call(
        functools.partial(states_kernel, near),
        grid=(blocks,),
        in_specs=[tokens, tokens, pl.BlockSpec((heads, SPAN), lambda i: (0, i))],
        out_specs=[
            pl.BlockSpec((1, width, HEAD_DIM), lambda i: (i, 0, 0)),
            pl.BlockSpec((1, heads, HEAD_DIM), lambda i: (i, 0, 0)),
            pl.BlockSpec((heads, SPAN), lambda i: (i, 0)),
        ]
        + [whole(piece)] * near,
        scratch_shapes=scratch,
        out_shape=[struct(shape, F32) for shape in shapes],
        compiler_params=params(56),
        cost_estimate=cost(4 * count * width * HEAD_DIM, 4 * count * width),
        name="local_states",
    )(keys, values, log_decay)
    return out[:3], out[3:], (keys, values)


def chain_kernel(near, *refs):
    arrived, (inside_ref, left_ref, leaving_ref, ordered) = refs[:near], refs[near + 1 :]
    mine = lax.axis_index("ctx") % near
    rows = leaving_ref.shape[0]
    heads = rows // HEAD_DIM
    for apart in range(near):
        ordered[mine ^ apart] = arrived[apart][...]
    left_ref[...] = jnp.zeros_like(left_ref)
    for head in range(heads):
        cols = head_columns(head)
        carried = jnp.zeros((HEAD_DIM, HEAD_DIM), F32)
        left = jnp.ones((1, HEAD_DIM), F32)
        for shard in range(near):
            inside_ref[shard, cols, :] = carried
            left_ref[shard, head : head + 1, :] = left
            drop = ordered[shard, rows + head : rows + head + 1, :]
            carried = carried * drop + ordered[shard, cols, :]
            left = left * drop
        leaving_ref[cols, :] = carried


def chain(pieces, after):
    near = len(pieces)
    rows = pieces[0].shape[0] - 8
    shapes = [(near, rows, HEAD_DIM), (near, 8, HEAD_DIM), (rows, HEAD_DIM)]
    return pl.pallas_call(
        functools.partial(chain_kernel, near),
        in_specs=[vmem()] * near + [anywhere()],
        out_specs=[vmem()] * 3,
        out_shape=[struct(shape, F32) for shape in shapes],
        scratch_shapes=[pltpu.VMEM((near, rows + 8, HEAD_DIM), F32)],
        compiler_params=params(16),
        name="chain",
    )(*pieces, after)


def spread_kernel(inside_ref, left_ref, entered_ref, _, *outs):
    near, rows, _ = inside_ref.shape
    mine = lax.axis_index("ctx") % near
    for apart, out_ref in enumerate(outs):
        shard = mine ^ apart
        left = left_ref[shard]
        for head in range(rows // HEAD_DIM):
            cols = head_columns(head)
            part = entered_ref[cols, :] * left[head : head + 1, :]
            out_ref[cols, :] = inside_ref[shard, cols, :] + part


def spread_states(inside, left, entered, after):
    near, rows, _ = inside.shape
    return pl.pallas_call(
        spread_kernel,
        in_specs=[vmem()] * 3 + [anywhere()],
        out_specs=[vmem()] * near,
        out_shape=[struct((rows, HEAD_DIM), F32)] * near,
        compiler_params=params(16),
        name="spread_states",
    )(inside, left, entered, after)


def inner_block(q_ref, k_ref, v_ref, first, cumul, raw_ref):
    heads = cumul.shape[0]
    columns = cumul.T
    half = SPAN // 2
    for part in range(2):
        rows = span_at(first, part * half, half)
        width = (part + 1) * half
        seen = span_at(first, 0, width)
        token = lax.broadcasted_iota(jnp.int32, (half, width), 0) + part * half
        earlier = lax.broadcasted_iota(jnp.int32, (half, width), 1)
        for group in range(0, heads, 4):
            members = range(group, min(group + 4, heads))
            scores = [
                lax.dot_general(
                    q_ref[rows, head_columns(head)],
                    k_ref[seen, head_columns(head)],
                    (((1,), (1,)), ((), ())),
                    preferred_element_type=F32,
                )
                for head in members
            ]
            weights = []
            for head, score in zip(members, scores):
                column = columns[part * half : (part + 1) * half, head : head + 1]
                diff = column - cumul[head : head + 1, :width]
                factor = jnp.exp(jnp.where(token >= earlier, diff, -jnp.inf))
                weights.append((score * factor).astype(BF16))
            for head, weight in zip(members, weights):
                cols = head_columns(head)
                raw_ref[rows, cols] = dot(weight, v_ref[seen, cols])


def inner_kernel(q_ref, k_ref, v_ref, cumul_ref, raw_ref):
    inner_block(q_ref, k_ref, v_ref, 0, cumul_ref[...], raw_ref)


def inner_loop_kernel(begin, end, q_ref, k_ref, v_ref, cumul_ref, *rest):
    raw_ref, token_ref = rest[-2:]
    token_ref[...] = jnp.zeros_like(token_ref)
    if begin:
        raw_ref[: begin * SPAN, :] = rest[0][: begin * SPAN, :]

    @pl.loop(begin, end)
    def _(index):
        cumul = cumul_ref[lines_at(cumul_ref, index, q_ref.shape[0] // SPAN), :]
        inner_block(q_ref, k_ref, v_ref, index * SPAN, cumul, raw_ref)


def inner(queries, keys, values, cumul, part, *earlier):
    count, width = keys.shape
    blocks = count // SPAN
    heads = width // HEAD_DIM
    token = struct((8, HEAD_DIM), F32)
    work = cost(4 * count * width * SPAN, 10 * count * width, count * heads * SPAN)
    if fits(count, width):
        begin, end = (0, blocks // 2) if part == 0 else (blocks // 2, blocks)
        return pl.pallas_call(
            functools.partial(inner_loop_kernel, begin, end),
            in_specs=[vmem()] * 4 + [vmem(), anywhere()][: len(earlier)],
            out_specs=[vmem()] * 2,
            out_shape=[struct((count, width), F32), token],
            compiler_params=params(16),
            cost_estimate=work,
            name="inner",
        )(queries, keys, values, cumul, *earlier)
    if part:
        return earlier[0], earlier[1]
    tokens = pl.BlockSpec((SPAN, width), lambda i: (i, 0))
    raw = pl.pallas_call(
        inner_kernel,
        grid=(blocks,),
        in_specs=[tokens, tokens, tokens, pl.BlockSpec((heads, SPAN), lambda i: (i, 0))],
        out_specs=tokens,
        out_shape=struct((count, width), F32),
        compiler_params=params(24),
        cost_estimate=work,
        name="inner",
    )(queries, keys, values, cumul)
    return raw, cumul


def finish_start(near, pieces, arrived, sums):
    mine = lax.axis_index("ctx") % near
    rows = arrived.shape[0] // near
    width = sums.shape[1]
    for apart in range(near):
        start = pl.multiple_of((mine ^ apart) * rows, rows)
        arrived[pl.ds(start, rows), :] = pieces[apart][...]
    sums[0:8, :] = jnp.zeros((8, width), F32)
    sums[8:16, :] = jnp.full((8, width), -jnp.inf, F32)
    sums[16:24, :] = jnp.full((8, width), jnp.inf, F32)


def finish_block(
    q_ref, raw_ref, first, entering_ref, before_ref, cumul, gain_ref, centered_ref, here, arrived, sums
):
    heads = cumul.shape[0]
    rows = span_at(first)
    block = 0 if isinstance(first, int) else first // SPAN
    factor = widen(jnp.exp(cumul))
    for group in range(0, heads, 4):
        members = range(group, min(group + 4, heads))
        outers = []
        for head in members:
            cols = head_columns(head)
            left = before_ref[block, head : head + 1, :]
            state = entering_ref[block, cols, :] + left * arrived[cols, :]
            query = q_ref[rows, cols]
            outers.append(
                dot(
                    jnp.concatenate([query, query], axis=1),
                    jnp.concatenate(split(state), axis=0),
                )
            )
        for head, outer in zip(members, outers):
            cols = head_columns(head)
            raw = raw_ref[rows, cols] + outer * factor[:, cols]
            power = jnp.mean(raw * raw, axis=1, keepdims=True)
            attended = (raw * lax.rsqrt(power + 1e-06) * gain_ref[:, cols]).astype(BF16)
            centered_ref[here, cols] = attended
            wide = attended.astype(F32).reshape(SPAN // 8, 8, HEAD_DIM)
            sums[0:8, cols] += jnp.sum(wide, axis=0)
            sums[8:16, cols] = jnp.maximum(sums[8:16, cols], jnp.max(wide, axis=0))
            sums[16:24, cols] = jnp.minimum(sums[16:24, cols], jnp.min(wide, axis=0))


def stat_lines(mean, sums):
    first, rest = split(mean)
    rest = mean - first.astype(F32)
    second, third = split(rest)
    top = jnp.max(sums[8:16, :], axis=0, keepdims=True)
    bottom = jnp.min(sums[16:24, :], axis=0, keepdims=True)
    lines = [first.astype(F32), second.astype(F32), third.astype(F32), top, bottom]
    lines.append(jnp.zeros((11, mean.shape[1]), F32))
    return jnp.concatenate(lines, axis=0).astype(BF16)


def finish_end(centered_ref, stats_ref, sums):
    count, width = centered_ref.shape
    mean = jnp.sum(sums[0:8, :], axis=0, keepdims=True) / count
    stats_ref[...] = stat_lines(mean, sums)

    @pl.loop(0, count // 128)
    def _(index):
        part = pl.ds(pl.multiple_of(index * 128, 128), 128)
        centered_ref[part, :] = (centered_ref[part, :].astype(F32) - mean).astype(BF16)


def finish_kernel(
    near, q_ref, raw_ref, entering_ref, before_ref, cumul_ref, gain_ref, *rest
):
    pieces, (centered_ref, stats_ref, arrived, sums) = rest[:near], rest[near:]
    step = pl.program_id(0)

    @pl.when(step == 0)
    def _():
        finish_start(near, pieces, arrived, sums)

    finish_block(
        q_ref,
        raw_ref,
        0,
        entering_ref,
        before_ref,
        cumul_ref[...],
        gain_ref,
        centered_ref,
        span_at(step * SPAN),
        arrived,
        sums,
    )

    @pl.when(step == pl.num_programs(0) - 1)
    def _():
        finish_end(centered_ref, stats_ref, sums)


def finish_part_kernel(
    near, part, q_ref, raw_ref, entering_ref, before_ref, cumul_ref, gain_ref, *rest
):
    pieces, rest = rest[: near // 2], rest[near // 2 :]
    earlier, (centered_ref, stats_ref, arrived, sums) = rest[:-4], rest[-4:]
    count, width = centered_ref.shape
    span = width // 2
    heads = span // HEAD_DIM
    blocks = count // SPAN
    rows = width // near
    mine = lax.axis_index("ctx") % near
    half = (mine // (near // 2)) ^ part
    low = pl.multiple_of(half * span, span)
    every = pl.ds(low, span)
    for ref, out_ref in zip(earlier, (centered_ref, stats_ref)):
        others = pl.ds(pl.multiple_of(span - low, span), span)
        out_ref[:, others] = ref[:, others]
    for place, piece in enumerate(pieces):
        start = pl.multiple_of((mine % (near // 2) ^ place) * rows, rows)
        arrived[pl.ds(start, rows), :] = piece[...]
    sums[0:8, :] = jnp.zeros((8, span), F32)
    sums[8:16, :] = jnp.full((8, span), -jnp.inf, F32)
    sums[16:24, :] = jnp.full((8, span), jnp.inf, F32)

    @pl.loop(0, blocks, unroll=2)
    def _(block):
        here = span_at(block * SPAN)
        cumul = cumul_ref[lines_at(cumul_ref, block, blocks), :]
        left = before_ref[block]
        cumul = jnp.where(half == 0, cumul[:heads], cumul[heads:])
        left = jnp.where(half == 0, left[:heads], left[heads:])
        factor = widen(jnp.exp(cumul))
        outers = []
        for head in range(heads):
            cols = pl.ds(pl.multiple_of(low + head * HEAD_DIM, HEAD_DIM), HEAD_DIM)
            state = entering_ref[block, cols, :]
            state = state + left[head : head + 1, :] * arrived[head_columns(head), :]
            query = q_ref[here, cols]
            outers.append(
                dot(
                    jnp.concatenate([query, query], axis=1),
                    jnp.concatenate(split(state), axis=0),
                )
            )
        for head, outer in enumerate(outers):
            cols = pl.ds(pl.multiple_of(low + head * HEAD_DIM, HEAD_DIM), HEAD_DIM)
            local = head_columns(head)
            raw = raw_ref[here, cols] + outer * factor[:, local]
            power = jnp.mean(raw * raw, axis=1, keepdims=True)
            attended = (raw * lax.rsqrt(power + 1e-06) * gain_ref[:, cols]).astype(BF16)
            centered_ref[here, cols] = attended
            wide = attended.astype(F32).reshape(SPAN // 8, 8, HEAD_DIM)
            sums[0:8, local] += jnp.sum(wide, axis=0)
            sums[8:16, local] = jnp.maximum(sums[8:16, local], jnp.max(wide, axis=0))
            sums[16:24, local] = jnp.minimum(sums[16:24, local], jnp.min(wide, axis=0))

    mean = jnp.sum(sums[0:8, :], axis=0, keepdims=True) / count
    stats_ref[:, every] = stat_lines(mean, sums)

    @pl.loop(0, count // 128)
    def _(index):
        part = pl.ds(pl.multiple_of(index * 128, 128), 128)
        centered_ref[part, every] = (centered_ref[part, every].astype(F32) - mean).astype(BF16)


def finish(queries, raw, entering, before, cumul, gain, pieces):
    count, width = queries.shape
    heads = width // HEAD_DIM
    near = len(pieces)
    shapes = [struct((count, width), BF16), struct((16, width), BF16)]
    scratch = [pltpu.VMEM((width, HEAD_DIM), F32), pltpu.VMEM((24, width), F32)]
    work = cost(4 * count * width * HEAD_DIM, 10 * count * width)
    operands = (queries, raw, entering, before, cumul, gain, *pieces)
    if fits(count, width) and width == 8 * HEAD_DIM:
        done = ()
        for part in range(2):
            mine = operands[:6] + tuple(pieces[part * near // 2 : (part + 1) * near // 2])
            done = pl.pallas_call(
                functools.partial(finish_part_kernel, near, part),
                in_specs=[vmem()] * (len(mine) + len(done)),
                out_specs=[vmem()] * 2,
                scratch_shapes=[
                    pltpu.VMEM((width // 2, HEAD_DIM), F32),
                    pltpu.VMEM((24, width // 2), F32),
                ],
                out_shape=shapes,
                compiler_params=params(16),
                cost_estimate=work,
                name="finish",
            )(*mine, *done)
        return done
    tokens = pl.BlockSpec((SPAN, width), lambda i: (i, 0))
    return pl.pallas_call(
        functools.partial(finish_kernel, near),
        grid=(count // SPAN,),
        in_specs=[
            tokens,
            tokens,
            pl.BlockSpec((1, width, HEAD_DIM), lambda i: (i, 0, 0)),
            pl.BlockSpec((1, heads, HEAD_DIM), lambda i: (i, 0, 0)),
            pl.BlockSpec((heads, SPAN), lambda i: (i, 0)),
            whole((1, width)),
        ]
        + [whole(pieces[0].shape)] * near,
        out_specs=[whole((count, width)), whole((16, width))],
        scratch_shapes=scratch,
        out_shape=shapes,
        compiler_params=params(32),
        cost_estimate=work,
        name="finish",
    )(*operands)


def places(count, inner, bit):
    return [
        (outer * 2 + bit) * inner + index
        for outer in range(count // inner // 2)
        for index in range(inner)
    ]


def side_of(side, block, shards):
    return side if side < 2 else (0 if block < shards // 2 else 1)


def gram_kernel(rows, blocks, apart, own_ref, other_ref, *rest):
    keep_ref, send_ref, turned = rest[-3:]
    width = own_ref.shape[1]
    shards = width // rows
    steps = sorted({step for step, _ in blocks})
    sides = {side for _, side in blocks}
    refs = [own_ref] if sides == {0} else [other_ref] if sides == {1} else [own_ref, other_ref]
    bit = (lax.axis_index("ctx") // apart) % 2
    if len(rest) > 4:
        send_ref[shards // 2 * rows :, :] = rest[0][...]
    for start in range(0, turned.shape[0], HEAD_DIM):
        here = start % width
        turned[start : start + HEAD_DIM, :] = own_ref[:, here : here + HEAD_DIM].T

    def fill(out_ref, row_blocks):
        for index, block in enumerate(row_blocks):
            line = slice(index * rows, (index + 1) * rows)
            here = slice(block * rows, (block + 1) * rows)
            left = turned[(block + steps[0]) * rows : (block + steps[-1] + 1) * rows, :]
            right = [ref[:, here] for ref in refs]
            right = right[0] if len(right) == 1 else jnp.concatenate(right, axis=1)
            out = dot(left, right).astype(out_ref.dtype)
            for place, (step, side) in enumerate(blocks):
                low = (step - steps[0]) * rows
                first = (side_of(side, block, shards) if len(refs) > 1 else 0) * rows
                target = slice(place * rows, (place + 1) * rows)
                out_ref[line, target] = out[low : low + rows, first : first + rows]

    for mine in range(2):

        @pl.when(bit == mine)
        def _():
            fill(send_ref, places(shards, apart, 1 - mine))
            fill(keep_ref, places(shards, apart, mine))


def gram_parts(own, other, extra, after, rows, blocks, apart):
    count, width = own.shape
    shards = width // rows
    size = len(blocks) * rows
    kept = (shards // 2 * rows, size)
    if rows % 128:
        full = [
            lax.dot_general(own, side, (((0,), (0,)), ((), ())), preferred_element_type=F32)
            for side in (own, other)
        ]
        parts = []
        for shard in range(shards):
            slabs = []
            for step, side in blocks:
                at = (shard + step) % shards * rows
                value = full[side_of(side, shard, shards)]
                slabs.append(value[at : at + rows, shard * rows : (shard + 1) * rows])
            parts.append(jnp.concatenate(slabs, axis=1))
        bit = (lax.axis_index("ctx") // apart) % 2
        parts = jnp.stack(parts).reshape(-1, 2, apart, rows, size)
        keep = lax.dynamic_index_in_dim(parts, bit, 1, False).reshape(kept)
        send = lax.dynamic_index_in_dim(parts, 1 - bit, 1, False).reshape(kept)
        return keep, jnp.concatenate([send.astype(BF16)] + extra)
    sent = (kept[0] + sum(value.shape[0] for value in extra), size)
    last = max(step for step, _ in blocks)
    return pl.pallas_call(
        functools.partial(gram_kernel, rows, blocks, apart),
        in_specs=[vmem()] * (2 + len(extra)) + [anywhere()],
        out_specs=[vmem(), vmem()],
        scratch_shapes=[pltpu.VMEM((width + last * rows, count), BF16)],
        out_shape=[struct(kept, F32), struct(sent, BF16)],
        compiler_params=params(16),
        cost_estimate=cost(2 * count * width * size, 4 * count * width),
        name="gram",
    )(own, other, *extra, after)


def merge(first, second, means):
    a, b = first.astype(F32), second.astype(F32)
    if b.shape[1] > a.shape[1]:
        b = jnp.concatenate([b[:, : a.shape[1]], b[:, a.shape[1] :]], axis=0)
    top, bottom = slice(means, means + RIDER_ROWS), slice(means + RIDER_ROWS, means + 2 * RIDER_ROWS)
    lines = [a[:means], b[:means], jnp.maximum(a[top], b[top]), jnp.minimum(a[bottom], b[bottom])]
    spare = -(2 * means + 2 * RIDER_ROWS) % 32
    if spare:
        lines.append(jnp.zeros((spare, a.shape[1]), F32))
    return jnp.concatenate(lines, axis=0).astype(BF16)


def fold_kernel(pieces, rows, inner, apart, means, *refs):
    keeps, others, rest = refs[:pieces], refs[pieces : 2 * pieces], refs[2 * pieces + 1 :]
    low = keeps[0].shape[0]
    bit = (lax.axis_index("ctx") // apart) % 2
    if means:
        riders_ref, kept_ref, send_ref, merged_ref = rest
        merged = merge(riders_ref[...], others[-1][low:, :], means)
        half, lines = merged.shape[0] // 2, merged.shape[1]
        send_ref[kept_ref.shape[0] :, :lines] = merged[:half]
        send_ref[kept_ref.shape[0] :, lines:] = merged[half:]
        merged_ref[...] = merged
    else:
        kept_ref, send_ref = rest

    for mine in range(2):

        @pl.when(bit == mine)
        def _():
            for out_ref, side in ((send_ref, 1 - mine), (kept_ref, mine)):
                for index, block in enumerate(places(low // rows, inner, side)):
                    line = slice(block * rows, (block + 1) * rows)
                    begin = 0
                    for keep_ref, other_ref in zip(keeps, others):
                        end = begin + keep_ref.shape[1]
                        total = keep_ref[line, :] + other_ref[line, :].astype(F32)
                        total = total.astype(out_ref.dtype)
                        out_ref[index * rows : (index + 1) * rows, begin:end] = total
                        begin = end


def fold(keeps, others, after, riders, means, rows, inner, apart):
    kept = (keeps[0].shape[0] // 2, sum(keep.shape[1] for keep in keeps))
    shapes = [struct(kept, F32), struct(kept, BF16)]
    if riders:
        merged = (-(-(2 * means + 2 * RIDER_ROWS) // 32) * 32, riders[0].shape[1])
        shapes = [struct(kept, F32), struct((kept[0] + merged[0] // 2, kept[1]), BF16)]
        shapes.append(struct(merged, BF16))
    return pl.pallas_call(
        functools.partial(fold_kernel, len(keeps), rows, inner, apart, means if riders else 0),
        in_specs=[vmem()] * (2 * len(keeps)) + [anywhere()] + [vmem()] * len(riders),
        out_specs=[vmem()] * len(shapes),
        out_shape=shapes,
        compiler_params=params(16),
        name="fold",
    )(*keeps, *others, after, *riders)


def close_kernel(rows, runs, waits, keep_ref, other_ref, *rest):
    total_ref, slab_refs = rest[waits], rest[waits + 1 :]
    total = keep_ref[...] + other_ref[:rows, :].astype(F32)
    total_ref[...] = total
    for run, slab_ref in zip(runs, slab_refs):
        for place, column in enumerate(run):
            slab = total[:, column * rows : (column + 1) * rows].astype(BF16)
            slab_ref[:, place * rows : (place + 1) * rows] = slab


def close(keep, other, after, rows, runs):
    out = pl.pallas_call(
        functools.partial(close_kernel, rows, runs, len(after)),
        in_specs=[vmem(), vmem()] + [anywhere()] * len(after),
        out_specs=[vmem()] * (1 + len(runs)),
        out_shape=[struct(keep.shape, F32)] + [struct((rows, len(run) * rows), BF16) for run in runs],
        compiler_params=params(16),
        name="close",
    )(keep, other, *after)
    return out[0], out[1:]


def assemble(put, upper, shards, chunks, mirrors, crossed):
    half = shards // 2
    for step in sorted({step for step, _ in chunks}):
        if step == 0:
            put(0, 0, chunks[(0, 0)])
            put(0, 1, chunks[(0, 1)])
        elif step < half:
            put(step, 0, chunks[(step, 0)].T)
            put(step, 1, crossed[step].T)
            put(-step, 0, mirrors[(step, 0)])
            put(-step, 1, mirrors[(step, 1)])
        else:
            last = jnp.where(upper, crossed[half].astype(F32), chunks[(half, 2)])
            put(half, upper, last.T)
            put(half, 1 - upper, mirrors[(half, 2)])


def pick(rows, names, values):
    out = {}
    for blocks, value in zip(names, values):
        for place, name in enumerate(blocks):
            out[name] = value[:, place * rows : (place + 1) * rows]
    return out


def putter(out_ref, rows, shards, total):
    mine, side = lax.axis_index("ctx"), lax.axis_index("head") & 1

    def put(step, flip, gram):
        shard = lax.rem(mine + step + shards, shards)
        at = pl.ds(pl.multiple_of(((side ^ flip) * shards + shard) * rows, rows), rows)
        out_ref[:, at] = (out_ref[:, at] + gram.astype(F32)) / total

    return put, jnp.where(mine >= shards // 2, 1, 0)


def cover_kernel(rows, shards, total, names, means_ref, others_ref, *refs):
    out_ref, spread = refs[-2:]
    width = rows * shards
    mine, side = lax.axis_index("ctx"), lax.axis_index("head") & 1
    for ref, place in ((means_ref, side), (others_ref, 1 - side)):
        value = ref[...]
        centre = jnp.sum(value, axis=0, keepdims=True) / shards
        spread[:, pl.ds(pl.multiple_of(place * width, width), width)] = value - centre
    own = pl.multiple_of((side * shards + mine) * rows, rows)
    left = spread[:, pl.ds(own, rows)].T
    count = total // shards
    out_ref[...] = count * jnp.dot(left, spread[...], precision=HIGHEST, preferred_element_type=F32)
    values = iter(refs[:-2])
    parts = [pick(rows, group, [next(values) for _ in group]) for group in names]
    put, upper = putter(out_ref, rows, shards, total)
    assemble(put, upper, shards, *parts)


def cover_rest_kernel(rows, shards, total, names, begun_ref, *refs):
    out_ref = refs[-1]
    out_ref[...] = begun_ref[...]
    values = iter(refs[:-1])
    parts = [pick(rows, group, [next(values) for _ in group]) for group in names]
    put, upper = putter(out_ref, rows, shards, total)
    assemble(put, upper, shards, *parts)


def cover(means, others, groups, names, rows, shards, total):
    width = rows * shards
    values = [value for group in groups for value in group]
    if rows % 128:
        mine, side = lax.axis_index("ctx"), lax.axis_index("head") & 1
        pair = [jnp.where(side == 0, means, others), jnp.where(side == 0, others, means)]
        spread = jnp.concatenate(pair, axis=1)
        spread = spread - jnp.mean(spread, axis=0)
        left = lax.dynamic_slice_in_dim(spread, (side * shards + mine) * rows, rows, 1)
        fix = (total // shards) * jnp.dot(left.T, spread, precision=HIGHEST)
        return cover_rest(fix, groups, names, rows, shards, total)
    return pl.pallas_call(
        functools.partial(cover_kernel, rows, shards, total, names),
        in_specs=[vmem()] * (2 + len(values)),
        out_specs=vmem(),
        scratch_shapes=[pltpu.VMEM((shards, 2 * width), F32)],
        out_shape=struct((rows, 2 * width), F32),
        compiler_params=params(16),
        name="cover",
    )(means, others, *values)


def cover_rest(begun, groups, names, rows, shards, total):
    values = [value for group in groups for value in group]
    if rows % 128:
        mine, side = lax.axis_index("ctx"), lax.axis_index("head") & 1
        out = [begun]

        def put(step, flip, gram):
            shard = lax.rem(mine + step + shards, shards)
            at = ((side ^ flip) * shards + shard) * rows
            old = lax.dynamic_slice_in_dim(out[0], at, rows, 1)
            new = (old + gram.astype(F32)) / total
            out[0] = lax.dynamic_update_slice_in_dim(out[0], new, at, 1)

        parts = [pick(rows, *pair) for pair in zip(names, groups)]
        assemble(put, jnp.where(mine >= shards // 2, 1, 0), shards, *parts)
        return out[0]
    return pl.pallas_call(
        functools.partial(cover_rest_kernel, rows, shards, total, names),
        in_specs=[vmem()] * (1 + len(values)),
        out_specs=vmem(),
        out_shape=struct(begun.shape, F32),
        compiler_params=params(16),
        name="cover_rest",
    )(begun, *values)


def body(queries, keys, values, log_decay, gain):
    count, width = queries.shape
    shards = lax.axis_size("ctx")
    sides = lax.axis_size("head")
    rows = width // shards
    mine = lax.axis_index("ctx")

    def to_shard(value, apart):
        return lax.ppermute(value, "ctx", [(a, a ^ apart) for a in range(shards)])

    def to_partner(value):
        return lax.ppermute(value, "head", [(a, a ^ 1) for a in range(sides)])

    near = shards // 2

    def nearby(values):
        return [values[0]] + [to_shard(values[apart], apart) for apart in range(1, near)]

    def forward(value, step):
        return lax.ppermute(value, "ctx", [(a, (a + step) % shards) for a in range(shards)])

    (entering, before, cumul), pieces, (keys, values) = local_states(
        keys, values, log_decay, near
    )
    raw, token = inner(queries, keys, values, cumul, 0)
    inside, left, leaving = chain(nearby(pieces), token)
    entered = lax.ppermute(leaving, "ctx", [(a, a + near) for a in range(near)])
    raw, token = inner(queries, keys, values, cumul, 1, raw, leaving)
    entry = nearby(spread_states(inside, left, entered, token))
    centered, stats = finish(
        queries, raw, entering, before, cumul, gain.reshape(1, width), entry
    )
    partner = to_partner(centered)

    half = shards // 2
    lines = width // RIDER_ROWS
    mean_rows = 3 * RIDER_ROWS
    extra = stats[:5].reshape(-1, lines)
    extra = jnp.pad(extra, ((0, -extra.shape[0] % 16), (0, 0)))
    near_steps = range(1, half // 2 + 1)
    far_steps = range(half // 2 + 1, half)
    plans = [
        [(step, side) for side in (0, 1) for step in near_steps],
        [(step, side) for step in far_steps for side in (0, 1)] + [(half, 2)],
        [(0, 0), (0, 1)],
    ]

    def begin(blocks, other, carried, after):
        keep, send = gram_parts(centered, other, carried, after, rows, blocks, 1)
        return [keep], [to_shard(send, 1)]

    def split_on(index, apart, after):
        keeps, others = kept[index]
        carried = riders if index == 0 else []
        keep, send, *merged = fold(
            keeps, others, after, carried, mean_rows * apart // 2, rows, 1, apart
        )
        riders[:] = merged or riders
        kept[index] = ([keep], [to_shard(send, apart)])
        return keep

    riders = [extra]
    blocks = plans[0]
    cut = len(blocks) // 2
    first = begin(blocks[:cut], centered, [], stats)
    second = begin(blocks[cut:], partner, riders, first[0][0])
    kept = [tuple(a + b for a, b in zip(first, second))]
    kept.append(begin(plans[1], partner, [], first[1][0]))
    after = split_on(0, 2, kept[1][0][0])
    kept.append(begin(plans[2], partner, [], after))
    aparts = [1 << place for place in range(1, shards.bit_length() - 1)]
    chunks, mirrors, crossed = [None] * 3, [[], [], []], [[], [], []]
    names = [plans, [[], [], []], [[], [], []]]

    def finished(index, after):
        blocks, ((keep,), (other,)) = plans[index], kept[index]
        steps = sorted({step for step, _ in blocks} - {0})
        runs = [[i for i, block in enumerate(blocks) if block[0] == step] for step in steps]
        crossing = [i for i, (step, side) in enumerate(blocks) if step and side]
        total, slabs = close(keep, other, after, rows, runs + [crossing] * bool(crossing))
        chunks[index] = total
        for step, run, slab in zip(steps, runs, slabs):
            mirrors[index].append(forward(slab, step))
            names[1][index].append([blocks[i] for i in run])
        if crossing:
            crossed[index].append(to_partner(slabs[-1]))
            names[2][index].append([blocks[i][0] for i in crossing])
        return total

    for apart in aparts[1:]:
        after = split_on(0, apart, after)
    every = merge(riders[0], kept[0][1][0][rows:], mean_rows * half)
    for apart in aparts:
        after = split_on(1, apart, after)
        if apart == aparts[-1]:
            after = finished(0, [after])
        after = split_on(2, apart, after)
    after = finished(1, [after])
    finished(2, [after])

    every = every.astype(F32)
    means = jnp.sum(every[: mean_rows * shards].reshape(shards, 3, width), axis=1)
    extremes = every[mean_rows * shards :][: 2 * RIDER_ROWS].reshape(2, width)
    shift = (extremes[0] + extremes[1]) / 2.0
    others = to_partner(means)
    begun = cover(
        means,
        others,
        (chunks[::2], mirrors[0] + mirrors[2], crossed[0] + crossed[2]),
        (names[0][::2], names[1][0] + names[1][2], names[2][0] + names[2][2]),
        rows,
        shards,
        count * shards,
    )
    covariance = cover_rest(
        begun,
        (chunks[1:2], mirrors[1], crossed[1]),
        (names[0][1:2], names[1][1], names[2][1]),
        rows,
        shards,
        count * shards,
    )
    return (shift, covariance)


def solution(mesh):
    placed = (P("ctx", "head"), P("ctx", "head"), P("ctx", "head"), P("head", "ctx"), P("head"))
    return jax.shard_map(
        body,
        mesh=mesh,
        in_specs=placed,
        out_specs=(P("head"), P(("head", "ctx"), None)),
        check_vma=False,
    )
```

```python
import functools
import math

import jax
import jax.numpy as jnp
from jax import lax
from jax.experimental import pallas as pl
from jax.experimental.pallas import tpu as pltpu
from jax.sharding import PartitionSpec as P

HEAD_DIM = 128
SPAN = 256
F32 = jnp.float32
BF16 = jnp.bfloat16
HIGHEST = lax.Precision.HIGHEST
MIB = 1 << 20
RIDER_ROWS = 4


def params(limit_mib):
    return pltpu.CompilerParams(vmem_limit_bytes=limit_mib * MIB)


def cost(flops, moved, transcendentals=0):
    return pl.CostEstimate(
        flops=int(flops) * 4, bytes_accessed=int(moved) * 4, transcendentals=int(transcendentals)
    )


def whole(shape):
    return pl.BlockSpec(shape, lambda *_: (0,) * len(shape))


def anywhere():
    return pl.BlockSpec(memory_space=pl.ANY)


def vmem():
    return pl.BlockSpec(memory_space=pltpu.VMEM)


def hbm():
    return pl.BlockSpec(memory_space=pltpu.HBM)


def struct(shape, dtype):
    return jax.ShapeDtypeStruct(shape, dtype)


def dot(a, b):
    return jnp.dot(a, b, preferred_element_type=F32)


def split(value):
    high = value.astype(BF16)
    return high, (value - high.astype(F32)).astype(BF16)


def running_sum(decay):
    rows = lax.broadcasted_iota(jnp.int32, (SPAN, SPAN), 0)
    columns = lax.broadcasted_iota(jnp.int32, (SPAN, SPAN), 1)
    ones = jnp.where(rows <= columns, 1.0, 0.0).astype(F32)
    return jnp.dot(decay, ones, precision=HIGHEST, preferred_element_type=F32)


def span_at(first, start=0, size=SPAN):
    if isinstance(first, int):
        return slice(first + start, first + start + size)
    return pl.ds(pl.multiple_of(first + start, math.gcd(start, SPAN)), size)


def lines_at(ref, index, blocks):
    heads = ref.shape[0] // blocks
    return pl.ds(pl.multiple_of(index * heads, heads), heads)


def fits(count, width):
    return count * width <= 1 << 20


def widen(value):
    heads = value.shape[0]
    first, rest = split(value)
    second, third = split(value - first.astype(F32))
    rows = lax.broadcasted_iota(jnp.int32, (heads, heads * HEAD_DIM), 0)
    columns = lax.broadcasted_iota(jnp.int32, (heads, heads * HEAD_DIM), 1)
    ones = jnp.where(columns // HEAD_DIM == rows, 1.0, 0.0)
    pieces = [first.astype(F32), second.astype(F32), third.astype(F32)]
    return lax.dot_general(
        jnp.concatenate(pieces, axis=0).astype(BF16),
        jnp.concatenate([ones] * 3, axis=0).astype(BF16),
        (((0,), (0,)), ((), ())),
        preferred_element_type=F32,
    )


def head_columns(head):
    return slice(head * HEAD_DIM, (head + 1) * HEAD_DIM)


def states_block(k_ref, v_ref, first, cumul, state, total):
    heads = cumul.shape[0]
    last = cumul[:, SPAN - 1 :]
    weight = jnp.exp(last - cumul)
    drop = jnp.exp(last)
    rows = span_at(first)
    for group in range(0, heads, 4):
        members = range(group, min(group + 4, heads))
        turned = [k_ref[rows, head_columns(head)].T for head in members]
        parts = []
        for head, key in zip(members, turned):
            high, low = split(key.astype(F32) * weight[head : head + 1, :])
            parts.append(jnp.concatenate([high, low], axis=0))
        updates = [dot(part, v_ref[rows, head_columns(head)]) for head, part in zip(members, parts)]
        for head, update in zip(members, updates):
            cols = head_columns(head)
            update = update[:HEAD_DIM] + update[HEAD_DIM:]
            state[cols, :] = state[cols, :] * drop[head : head + 1, :] + update
    total[...] = total[...] * drop


def states_out(near, state, total, pieces):
    mine = lax.axis_index("ctx") % near
    rows = state.shape[0] // near
    for apart in range(near):
        start = pl.multiple_of((mine ^ apart) * rows, rows)
        pieces[apart][:rows, :] = state[pl.ds(start, rows), :]
        pieces[apart][rows:, :] = jnp.zeros((8, HEAD_DIM), F32)
        for head in range(rows // HEAD_DIM):
            line = total[pl.ds(start // HEAD_DIM + head, 1), :]
            pieces[apart][rows + head : rows + head + 1, :] = line


def states_kernel(near, k_ref, v_ref, decay_ref, entering_ref, before_ref, cumul_ref, *rest):
    pieces, (state, total) = rest[:near], rest[near:]
    step = pl.program_id(0)

    @pl.when(step == 0)
    def _():
        state[...] = jnp.zeros_like(state)
        total[...] = jnp.ones_like(total)

    entering_ref[0] = state[...]
    before_ref[0] = total[...]
    cumul_ref[...] = running_sum(decay_ref[...])
    states_block(k_ref, v_ref, 0, cumul_ref[...], state, total)

    @pl.when(step == pl.num_programs(0) - 1)
    def _():
        states_out(near, state, total, pieces)


def states_fetch_kernel(near, k_any, v_any, decay_any, entering_ref, before_ref, cumul, *rest):
    pieces, (k_ref, v_ref, decay_ref, state, total, sems) = rest[:near], rest[near:]
    count = k_any.shape[0]
    blocks = count // SPAN
    heads = decay_ref.shape[0]

    def fetch(source, target, index, which):
        rows = span_at(index * SPAN)
        return pltpu.make_async_copy(source.at[rows, :], target.at[rows, :], sems.at[which, index])

    decays = pltpu.make_async_copy(decay_any, decay_ref, sems.at[2, 0])
    decays.start()
    for index in range(blocks):
        fetch(k_any, k_ref, index, 0).start()
        fetch(v_any, v_ref, index, 1).start()
    state[...] = jnp.zeros_like(state)
    total[...] = jnp.ones_like(total)
    decays.wait()
    lines = [decay_ref[:, index * SPAN : (index + 1) * SPAN] for index in range(blocks)]
    cumul[...] = running_sum(jnp.concatenate(lines, axis=0))

    @pl.loop(0, blocks)
    def _(index):
        fetch(k_any, k_ref, index, 0).wait()
        fetch(v_any, v_ref, index, 1).wait()
        entering_ref[index] = state[...]
        before_ref[index] = total[...]
        lines = cumul[pl.ds(pl.multiple_of(index * heads, heads), heads), :]
        states_block(k_ref, v_ref, index * SPAN, lines, state, total)

    states_out(near, state, total, pieces)


def local_states(keys, values, log_decay, near):
    count, width = keys.shape
    heads = width // HEAD_DIM
    blocks = count // SPAN
    rows = width // near
    piece = (rows + 8, HEAD_DIM)
    shapes = [(blocks, width, HEAD_DIM), (blocks, heads, HEAD_DIM), (blocks * heads, SPAN)]
    shapes += [piece] * near
    scratch = [pltpu.VMEM((width, HEAD_DIM), F32), pltpu.VMEM((heads, HEAD_DIM), F32)]
    if fits(count, width):
        kept = [struct(value.shape, value.dtype) for value in (keys, values)]
        out = pl.pallas_call(
            functools.partial(states_fetch_kernel, near),
            in_specs=[hbm()] * 3,
            out_specs=[vmem()] * (len(shapes) + 2),
            out_shape=[struct(shape, F32) for shape in shapes] + kept,
            scratch_shapes=[pltpu.VMEM((heads, count), F32)]
            + scratch
            + [pltpu.SemaphoreType.DMA((3, blocks))],
            compiler_params=params(48),
            cost_estimate=cost(4 * count * width * HEAD_DIM, 4 * count * width),
            name="local_states",
        )(keys, values, log_decay)
        return out[:3], out[3:-2], out[-2:]
    tokens = pl.BlockSpec((SPAN, width), lambda i: (i, 0))
    out = pl.pallas_call(
        functools.partial(states_kernel, near),
        grid=(blocks,),
        in_specs=[tokens, tokens, pl.BlockSpec((heads, SPAN), lambda i: (0, i))],
        out_specs=[
            pl.BlockSpec((1, width, HEAD_DIM), lambda i: (i, 0, 0)),
            pl.BlockSpec((1, heads, HEAD_DIM), lambda i: (i, 0, 0)),
            pl.BlockSpec((heads, SPAN), lambda i: (i, 0)),
        ]
        + [whole(piece)] * near,
        scratch_shapes=scratch,
        out_shape=[struct(shape, F32) for shape in shapes],
        compiler_params=params(56),
        cost_estimate=cost(4 * count * width * HEAD_DIM, 4 * count * width),
        name="local_states",
    )(keys, values, log_decay)
    return out[:3], out[3:], (keys, values)


def chain_kernel(near, *refs):
    arrived, (inside_ref, left_ref, leaving_ref, ordered) = refs[:near], refs[near + 1 :]
    mine = lax.axis_index("ctx") % near
    rows = leaving_ref.shape[0]
    heads = rows // HEAD_DIM
    for apart in range(near):
        ordered[mine ^ apart] = arrived[apart][...]
    left_ref[...] = jnp.zeros_like(left_ref)
    for head in range(heads):
        cols = head_columns(head)
        carried = jnp.zeros((HEAD_DIM, HEAD_DIM), F32)
        left = jnp.ones((1, HEAD_DIM), F32)
        for shard in range(near):
            inside_ref[shard, cols, :] = carried
            left_ref[shard, head : head + 1, :] = left
            drop = ordered[shard, rows + head : rows + head + 1, :]
            carried = carried * drop + ordered[shard, cols, :]
            left = left * drop
        leaving_ref[cols, :] = carried


def chain(pieces, after):
    near = len(pieces)
    rows = pieces[0].shape[0] - 8
    shapes = [(near, rows, HEAD_DIM), (near, 8, HEAD_DIM), (rows, HEAD_DIM)]
    return pl.pallas_call(
        functools.partial(chain_kernel, near),
        in_specs=[vmem()] * near + [anywhere()],
        out_specs=[vmem()] * 3,
        out_shape=[struct(shape, F32) for shape in shapes],
        scratch_shapes=[pltpu.VMEM((near, rows + 8, HEAD_DIM), F32)],
        compiler_params=params(16),
        name="chain",
    )(*pieces, after)


def spread_kernel(inside_ref, left_ref, entered_ref, _, *outs):
    near, rows, _ = inside_ref.shape
    mine = lax.axis_index("ctx") % near
    for apart, out_ref in enumerate(outs):
        shard = mine ^ apart
        left = left_ref[shard]
        for head in range(rows // HEAD_DIM):
            cols = head_columns(head)
            part = entered_ref[cols, :] * left[head : head + 1, :]
            out_ref[cols, :] = inside_ref[shard, cols, :] + part


def spread_states(inside, left, entered, after):
    near, rows, _ = inside.shape
    return pl.pallas_call(
        spread_kernel,
        in_specs=[vmem()] * 3 + [anywhere()],
        out_specs=[vmem()] * near,
        out_shape=[struct((rows, HEAD_DIM), F32)] * near,
        compiler_params=params(16),
        name="spread_states",
    )(inside, left, entered, after)


def inner_block(q_ref, k_ref, v_ref, first, cumul, raw_ref):
    heads = cumul.shape[0]
    columns = cumul.T
    half = SPAN // 2
    for part in range(2):
        rows = span_at(first, part * half, half)
        width = (part + 1) * half
        seen = span_at(first, 0, width)
        token = lax.broadcasted_iota(jnp.int32, (half, width), 0) + part * half
        earlier = lax.broadcasted_iota(jnp.int32, (half, width), 1)
        for group in range(0, heads, 4):
            members = range(group, min(group + 4, heads))
            scores = [
                lax.dot_general(
                    q_ref[rows, head_columns(head)],
                    k_ref[seen, head_columns(head)],
                    (((1,), (1,)), ((), ())),
                    preferred_element_type=F32,
                )
                for head in members
            ]
            weights = []
            for head, score in zip(members, scores):
                column = columns[part * half : (part + 1) * half, head : head + 1]
                diff = column - cumul[head : head + 1, :width]
                factor = jnp.exp(jnp.where(token >= earlier, diff, -jnp.inf))
                weights.append((score * factor).astype(BF16))
            for head, weight in zip(members, weights):
                cols = head_columns(head)
                raw_ref[rows, cols] = dot(weight, v_ref[seen, cols])


def inner_kernel(q_ref, k_ref, v_ref, cumul_ref, raw_ref):
    inner_block(q_ref, k_ref, v_ref, 0, cumul_ref[...], raw_ref)


def inner_loop_kernel(begin, end, q_ref, k_ref, v_ref, cumul_ref, *rest):
    raw_ref, token_ref = rest[-2:]
    token_ref[...] = jnp.zeros_like(token_ref)
    if begin:
        raw_ref[: begin * SPAN, :] = rest[0][: begin * SPAN, :]

    @pl.loop(begin, end)
    def _(index):
        cumul = cumul_ref[lines_at(cumul_ref, index, q_ref.shape[0] // SPAN), :]
        inner_block(q_ref, k_ref, v_ref, index * SPAN, cumul, raw_ref)


def inner(queries, keys, values, cumul, part, *earlier):
    count, width = keys.shape
    blocks = count // SPAN
    heads = width // HEAD_DIM
    token = struct((8, HEAD_DIM), F32)
    work = cost(4 * count * width * SPAN, 10 * count * width, count * heads * SPAN)
    if fits(count, width):
        begin, end = (0, blocks // 2) if part == 0 else (blocks // 2, blocks)
        return pl.pallas_call(
            functools.partial(inner_loop_kernel, begin, end),
            in_specs=[vmem()] * 4 + [vmem(), anywhere()][: len(earlier)],
            out_specs=[vmem()] * 2,
            out_shape=[struct((count, width), F32), token],
            compiler_params=params(16),
            cost_estimate=work,
            name="inner",
        )(queries, keys, values, cumul, *earlier)
    if part:
        return earlier[0], earlier[1]
    tokens = pl.BlockSpec((SPAN, width), lambda i: (i, 0))
    raw = pl.pallas_call(
        inner_kernel,
        grid=(blocks,),
        in_specs=[tokens, tokens, tokens, pl.BlockSpec((heads, SPAN), lambda i: (i, 0))],
        out_specs=tokens,
        out_shape=struct((count, width), F32),
        compiler_params=params(24),
        cost_estimate=work,
        name="inner",
    )(queries, keys, values, cumul)
    return raw, cumul


def finish_start(near, pieces, arrived, sums):
    mine = lax.axis_index("ctx") % near
    rows = arrived.shape[0] // near
    width = sums.shape[1]
    for apart in range(near):
        start = pl.multiple_of((mine ^ apart) * rows, rows)
        arrived[pl.ds(start, rows), :] = pieces[apart][...]
    sums[0:8, :] = jnp.zeros((8, width), F32)
    sums[8:16, :] = jnp.full((8, width), -jnp.inf, F32)
    sums[16:24, :] = jnp.full((8, width), jnp.inf, F32)


def finish_block(
    q_ref, raw_ref, first, entering_ref, before_ref, cumul, gain_ref, centered_ref, here, arrived, sums
):
    heads = cumul.shape[0]
    rows = span_at(first)
    block = 0 if isinstance(first, int) else first // SPAN
    factor = widen(jnp.exp(cumul))
    for group in range(0, heads, 4):
        members = range(group, min(group + 4, heads))
        outers = []
        for head in members:
            cols = head_columns(head)
            left = before_ref[block, head : head + 1, :]
            state = entering_ref[block, cols, :] + left * arrived[cols, :]
            query = q_ref[rows, cols]
            outers.append(
                dot(
                    jnp.concatenate([query, query], axis=1),
                    jnp.concatenate(split(state), axis=0),
                )
            )
        for head, outer in zip(members, outers):
            cols = head_columns(head)
            raw = raw_ref[rows, cols] + outer * factor[:, cols]
            power = jnp.mean(raw * raw, axis=1, keepdims=True)
            attended = (raw * lax.rsqrt(power + 1e-06) * gain_ref[:, cols]).astype(BF16)
            centered_ref[here, cols] = attended
            wide = attended.astype(F32).reshape(SPAN // 8, 8, HEAD_DIM)
            sums[0:8, cols] += jnp.sum(wide, axis=0)
            sums[8:16, cols] = jnp.maximum(sums[8:16, cols], jnp.max(wide, axis=0))
            sums[16:24, cols] = jnp.minimum(sums[16:24, cols], jnp.min(wide, axis=0))


def stat_lines(mean, sums):
    first, rest = split(mean)
    rest = mean - first.astype(F32)
    second, third = split(rest)
    top = jnp.max(sums[8:16, :], axis=0, keepdims=True)
    bottom = jnp.min(sums[16:24, :], axis=0, keepdims=True)
    lines = [first.astype(F32), second.astype(F32), third.astype(F32), top, bottom]
    lines.append(jnp.zeros((11, mean.shape[1]), F32))
    return jnp.concatenate(lines, axis=0).astype(BF16)


def finish_end(centered_ref, stats_ref, sums):
    count, width = centered_ref.shape
    mean = jnp.sum(sums[0:8, :], axis=0, keepdims=True) / count
    stats_ref[...] = stat_lines(mean, sums)

    @pl.loop(0, count // 128)
    def _(index):
        part = pl.ds(pl.multiple_of(index * 128, 128), 128)
        centered_ref[part, :] = (centered_ref[part, :].astype(F32) - mean).astype(BF16)


def finish_kernel(
    near, q_ref, raw_ref, entering_ref, before_ref, cumul_ref, gain_ref, *rest
):
    pieces, (centered_ref, stats_ref, arrived, sums) = rest[:near], rest[near:]
    step = pl.program_id(0)

    @pl.when(step == 0)
    def _():
        finish_start(near, pieces, arrived, sums)

    finish_block(
        q_ref,
        raw_ref,
        0,
        entering_ref,
        before_ref,
        cumul_ref[...],
        gain_ref,
        centered_ref,
        span_at(step * SPAN),
        arrived,
        sums,
    )

    @pl.when(step == pl.num_programs(0) - 1)
    def _():
        finish_end(centered_ref, stats_ref, sums)


def finish_part_kernel(
    near, part, q_ref, raw_ref, entering_ref, before_ref, cumul_ref, gain_ref, *rest
):
    pieces, rest = rest[: near // 2], rest[near // 2 :]
    earlier, (centered_ref, stats_ref, arrived, sums) = rest[:-4], rest[-4:]
    count, width = centered_ref.shape
    span = width // 2
    heads = span // HEAD_DIM
    blocks = count // SPAN
    rows = width // near
    mine = lax.axis_index("ctx") % near
    half = (mine // (near // 2)) ^ part
    low = pl.multiple_of(half * span, span)
    every = pl.ds(low, span)
    for ref, out_ref in zip(earlier, (centered_ref, stats_ref)):
        others = pl.ds(pl.multiple_of(span - low, span), span)
        out_ref[:, others] = ref[:, others]
    for place, piece in enumerate(pieces):
        start = pl.multiple_of((mine % (near // 2) ^ place) * rows, rows)
        arrived[pl.ds(start, rows), :] = piece[...]
    sums[0:8, :] = jnp.zeros((8, span), F32)
    sums[8:16, :] = jnp.full((8, span), -jnp.inf, F32)
    sums[16:24, :] = jnp.full((8, span), jnp.inf, F32)

    @pl.loop(0, blocks, unroll=2)
    def _(block):
        here = span_at(block * SPAN)
        cumul = cumul_ref[lines_at(cumul_ref, block, blocks), :]
        left = before_ref[block]
        cumul = jnp.where(half == 0, cumul[:heads], cumul[heads:])
        left = jnp.where(half == 0, left[:heads], left[heads:])
        factor = widen(jnp.exp(cumul))
        outers = []
        for head in range(heads):
            cols = pl.ds(pl.multiple_of(low + head * HEAD_DIM, HEAD_DIM), HEAD_DIM)
            state = entering_ref[block, cols, :]
            state = state + left[head : head + 1, :] * arrived[head_columns(head), :]
            query = q_ref[here, cols]
            outers.append(
                dot(
                    jnp.concatenate([query, query], axis=1),
                    jnp.concatenate(split(state), axis=0),
                )
            )
        for head, outer in enumerate(outers):
            cols = pl.ds(pl.multiple_of(low + head * HEAD_DIM, HEAD_DIM), HEAD_DIM)
            local = head_columns(head)
            raw = raw_ref[here, cols] + outer * factor[:, local]
            power = jnp.mean(raw * raw, axis=1, keepdims=True)
            attended = (raw * lax.rsqrt(power + 1e-06) * gain_ref[:, cols]).astype(BF16)
            centered_ref[here, cols] = attended
            wide = attended.astype(F32).reshape(SPAN // 8, 8, HEAD_DIM)
            sums[0:8, local] += jnp.sum(wide, axis=0)
            sums[8:16, local] = jnp.maximum(sums[8:16, local], jnp.max(wide, axis=0))
            sums[16:24, local] = jnp.minimum(sums[16:24, local], jnp.min(wide, axis=0))

    mean = jnp.sum(sums[0:8, :], axis=0, keepdims=True) / count
    stats_ref[:, every] = stat_lines(mean, sums)

    @pl.loop(0, count // 128)
    def _(index):
        part = pl.ds(pl.multiple_of(index * 128, 128), 128)
        centered_ref[part, every] = (centered_ref[part, every].astype(F32) - mean).astype(BF16)


def finish(queries, raw, entering, before, cumul, gain, pieces):
    count, width = queries.shape
    heads = width // HEAD_DIM
    near = len(pieces)
    shapes = [struct((count, width), BF16), struct((16, width), BF16)]
    scratch = [pltpu.VMEM((width, HEAD_DIM), F32), pltpu.VMEM((24, width), F32)]
    work = cost(4 * count * width * HEAD_DIM, 10 * count * width)
    operands = (queries, raw, entering, before, cumul, gain, *pieces)
    if fits(count, width) and width == 8 * HEAD_DIM:
        done = ()
        for part in range(2):
            mine = operands[:6] + tuple(pieces[part * near // 2 : (part + 1) * near // 2])
            done = pl.pallas_call(
                functools.partial(finish_part_kernel, near, part),
                in_specs=[vmem()] * (len(mine) + len(done)),
                out_specs=[vmem()] * 2,
                scratch_shapes=[
                    pltpu.VMEM((width // 2, HEAD_DIM), F32),
                    pltpu.VMEM((24, width // 2), F32),
                ],
                out_shape=shapes,
                compiler_params=params(16),
                cost_estimate=work,
                name="finish",
            )(*mine, *done)
        return done
    tokens = pl.BlockSpec((SPAN, width), lambda i: (i, 0))
    return pl.pallas_call(
        functools.partial(finish_kernel, near),
        grid=(count // SPAN,),
        in_specs=[
            tokens,
            tokens,
            pl.BlockSpec((1, width, HEAD_DIM), lambda i: (i, 0, 0)),
            pl.BlockSpec((1, heads, HEAD_DIM), lambda i: (i, 0, 0)),
            pl.BlockSpec((heads, SPAN), lambda i: (i, 0)),
            whole((1, width)),
        ]
        + [whole(pieces[0].shape)] * near,
        out_specs=[whole((count, width)), whole((16, width))],
        scratch_shapes=scratch,
        out_shape=shapes,
        compiler_params=params(32),
        cost_estimate=work,
        name="finish",
    )(*operands)


def places(count, inner, bit):
    return [
        (outer * 2 + bit) * inner + index
        for outer in range(count // inner // 2)
        for index in range(inner)
    ]


def side_of(side, block, shards):
    return side if side < 2 else (0 if block < shards // 2 else 1)


def gram_kernel(rows, blocks, apart, own_ref, other_ref, *rest):
    keep_ref, send_ref, turned = rest[-3:]
    width = own_ref.shape[1]
    shards = width // rows
    steps = sorted({step for step, _ in blocks})
    sides = {side for _, side in blocks}
    refs = [own_ref] if sides == {0} else [other_ref] if sides == {1} else [own_ref, other_ref]
    bit = (lax.axis_index("ctx") // apart) % 2
    if len(rest) > 4:
        send_ref[shards // 2 * rows :, :] = rest[0][...]
    for start in range(0, turned.shape[0], HEAD_DIM):
        here = start % width
        turned[start : start + HEAD_DIM, :] = own_ref[:, here : here + HEAD_DIM].T

    def fill(out_ref, row_blocks):
        for index, block in enumerate(row_blocks):
            line = slice(index * rows, (index + 1) * rows)
            here = slice(block * rows, (block + 1) * rows)
            left = turned[(block + steps[0]) * rows : (block + steps[-1] + 1) * rows, :]
            right = [ref[:, here] for ref in refs]
            right = right[0] if len(right) == 1 else jnp.concatenate(right, axis=1)
            out = dot(left, right).astype(out_ref.dtype)
            for place, (step, side) in enumerate(blocks):
                low = (step - steps[0]) * rows
                first = (side_of(side, block, shards) if len(refs) > 1 else 0) * rows
                target = slice(place * rows, (place + 1) * rows)
                out_ref[line, target] = out[low : low + rows, first : first + rows]

    for mine in range(2):

        @pl.when(bit == mine)
        def _():
            fill(send_ref, places(shards, apart, 1 - mine))
            fill(keep_ref, places(shards, apart, mine))


def gram_parts(own, other, extra, after, rows, blocks, apart):
    count, width = own.shape
    shards = width // rows
    size = len(blocks) * rows
    kept = (shards // 2 * rows, size)
    if rows % 128:
        full = [
            lax.dot_general(own, side, (((0,), (0,)), ((), ())), preferred_element_type=F32)
            for side in (own, other)
        ]
        parts = []
        for shard in range(shards):
            slabs = []
            for step, side in blocks:
                at = (shard + step) % shards * rows
                value = full[side_of(side, shard, shards)]
                slabs.append(value[at : at + rows, shard * rows : (shard + 1) * rows])
            parts.append(jnp.concatenate(slabs, axis=1))
        bit = (lax.axis_index("ctx") // apart) % 2
        parts = jnp.stack(parts).reshape(-1, 2, apart, rows, size)
        keep = lax.dynamic_index_in_dim(parts, bit, 1, False).reshape(kept)
        send = lax.dynamic_index_in_dim(parts, 1 - bit, 1, False).reshape(kept)
        return keep, jnp.concatenate([send.astype(BF16)] + extra)
    sent = (kept[0] + sum(value.shape[0] for value in extra), size)
    last = max(step for step, _ in blocks)
    return pl.pallas_call(
        functools.partial(gram_kernel, rows, blocks, apart),
        in_specs=[vmem()] * (2 + len(extra)) + [anywhere()],
        out_specs=[vmem(), vmem()],
        scratch_shapes=[pltpu.VMEM((width + last * rows, count), BF16)],
        out_shape=[struct(kept, F32), struct(sent, BF16)],
        compiler_params=params(16),
        cost_estimate=cost(2 * count * width * size, 4 * count * width),
        name="gram",
    )(own, other, *extra, after)


def merge(first, second, means):
    a, b = first.astype(F32), second.astype(F32)
    if b.shape[1] > a.shape[1]:
        b = jnp.concatenate([b[:, : a.shape[1]], b[:, a.shape[1] :]], axis=0)
    top, bottom = slice(means, means + RIDER_ROWS), slice(means + RIDER_ROWS, means + 2 * RIDER_ROWS)
    lines = [a[:means], b[:means], jnp.maximum(a[top], b[top]), jnp.minimum(a[bottom], b[bottom])]
    spare = -(2 * means + 2 * RIDER_ROWS) % 32
    if spare:
        lines.append(jnp.zeros((spare, a.shape[1]), F32))
    return jnp.concatenate(lines, axis=0).astype(BF16)


def fold_kernel(pieces, rows, inner, apart, means, *refs):
    keeps, others, rest = refs[:pieces], refs[pieces : 2 * pieces], refs[2 * pieces + 1 :]
    low = keeps[0].shape[0]
    bit = (lax.axis_index("ctx") // apart) % 2
    if means:
        riders_ref, kept_ref, send_ref, merged_ref = rest
        merged = merge(riders_ref[...], others[-1][low:, :], means)
        half, lines = merged.shape[0] // 2, merged.shape[1]
        send_ref[kept_ref.shape[0] :, :lines] = merged[:half]
        send_ref[kept_ref.shape[0] :, lines:] = merged[half:]
        merged_ref[...] = merged
    else:
        kept_ref, send_ref = rest

    for mine in range(2):

        @pl.when(bit == mine)
        def _():
            for out_ref, side in ((send_ref, 1 - mine), (kept_ref, mine)):
                for index, block in enumerate(places(low // rows, inner, side)):
                    line = slice(block * rows, (block + 1) * rows)
                    begin = 0
                    for keep_ref, other_ref in zip(keeps, others):
                        end = begin + keep_ref.shape[1]
                        total = keep_ref[line, :] + other_ref[line, :].astype(F32)
                        total = total.astype(out_ref.dtype)
                        out_ref[index * rows : (index + 1) * rows, begin:end] = total
                        begin = end


def fold(keeps, others, after, riders, means, rows, inner, apart):
    kept = (keeps[0].shape[0] // 2, sum(keep.shape[1] for keep in keeps))
    shapes = [struct(kept, F32), struct(kept, BF16)]
    if riders:
        merged = (-(-(2 * means + 2 * RIDER_ROWS) // 32) * 32, riders[0].shape[1])
        shapes = [struct(kept, F32), struct((kept[0] + merged[0] // 2, kept[1]), BF16)]
        shapes.append(struct(merged, BF16))
    return pl.pallas_call(
        functools.partial(fold_kernel, len(keeps), rows, inner, apart, means if riders else 0),
        in_specs=[vmem()] * (2 * len(keeps)) + [anywhere()] + [vmem()] * len(riders),
        out_specs=[vmem()] * len(shapes),
        out_shape=shapes,
        compiler_params=params(16),
        name="fold",
    )(*keeps, *others, after, *riders)


def close_kernel(rows, runs, waits, keep_ref, other_ref, *rest):
    total_ref, slab_refs = rest[waits], rest[waits + 1 :]
    total = keep_ref[...] + other_ref[:rows, :].astype(F32)
    total_ref[...] = total
    for run, slab_ref in zip(runs, slab_refs):
        for place, column in enumerate(run):
            slab = total[:, column * rows : (column + 1) * rows].astype(BF16)
            slab_ref[:, place * rows : (place + 1) * rows] = slab


def close(keep, other, after, rows, runs):
    out = pl.pallas_call(
        functools.partial(close_kernel, rows, runs, len(after)),
        in_specs=[vmem(), vmem()] + [anywhere()] * len(after),
        out_specs=[vmem()] * (1 + len(runs)),
        out_shape=[struct(keep.shape, F32)] + [struct((rows, len(run) * rows), BF16) for run in runs],
        compiler_params=params(16),
        name="close",
    )(keep, other, *after)
    return out[0], out[1:]


def assemble(put, upper, shards, chunks, mirrors, crossed):
    half = shards // 2
    for step in sorted({step for step, _ in chunks}):
        if step == 0:
            put(0, 0, chunks[(0, 0)])
            put(0, 1, chunks[(0, 1)])
        elif step < half:
            put(step, 0, chunks[(step, 0)].T)
            put(step, 1, crossed[step].T)
            put(-step, 0, mirrors[(step, 0)])
            put(-step, 1, mirrors[(step, 1)])
        else:
            last = jnp.where(upper, crossed[half].astype(F32), chunks[(half, 2)])
            put(half, upper, last.T)
            put(half, 1 - upper, mirrors[(half, 2)])


def pick(rows, names, values):
    out = {}
    for blocks, value in zip(names, values):
        for place, name in enumerate(blocks):
            out[name] = value[:, place * rows : (place + 1) * rows]
    return out


def putter(out_ref, rows, shards, total):
    mine, side = lax.axis_index("ctx"), lax.axis_index("head") & 1

    def put(step, flip, gram):
        shard = lax.rem(mine + step + shards, shards)
        at = pl.ds(pl.multiple_of(((side ^ flip) * shards + shard) * rows, rows), rows)
        out_ref[:, at] = (out_ref[:, at] + gram.astype(F32)) / total

    return put, jnp.where(mine >= shards // 2, 1, 0)


def cover_kernel(rows, shards, total, names, means_ref, others_ref, *refs):
    out_ref, spread = refs[-2:]
    width = rows * shards
    mine, side = lax.axis_index("ctx"), lax.axis_index("head") & 1
    for ref, place in ((means_ref, side), (others_ref, 1 - side)):
        value = ref[...]
        centre = jnp.sum(value, axis=0, keepdims=True) / shards
        spread[:, pl.ds(pl.multiple_of(place * width, width), width)] = value - centre
    own = pl.multiple_of((side * shards + mine) * rows, rows)
    left = spread[:, pl.ds(own, rows)].T
    count = total // shards
    out_ref[...] = count * jnp.dot(left, spread[...], precision=HIGHEST, preferred_element_type=F32)
    values = iter(refs[:-2])
    parts = [pick(rows, group, [next(values) for _ in group]) for group in names]
    put, upper = putter(out_ref, rows, shards, total)
    assemble(put, upper, shards, *parts)


def cover_rest_kernel(rows, shards, total, names, begun_ref, *refs):
    out_ref = refs[-1]
    out_ref[...] = begun_ref[...]
    values = iter(refs[:-1])
    parts = [pick(rows, group, [next(values) for _ in group]) for group in names]
    put, upper = putter(out_ref, rows, shards, total)
    assemble(put, upper, shards, *parts)


def cover(means, others, groups, names, rows, shards, total):
    width = rows * shards
    values = [value for group in groups for value in group]
    if rows % 128:
        mine, side = lax.axis_index("ctx"), lax.axis_index("head") & 1
        pair = [jnp.where(side == 0, means, others), jnp.where(side == 0, others, means)]
        spread = jnp.concatenate(pair, axis=1)
        spread = spread - jnp.mean(spread, axis=0)
        left = lax.dynamic_slice_in_dim(spread, (side * shards + mine) * rows, rows, 1)
        fix = (total // shards) * jnp.dot(left.T, spread, precision=HIGHEST)
        return cover_rest(fix, groups, names, rows, shards, total)
    return pl.pallas_call(
        functools.partial(cover_kernel, rows, shards, total, names),
        in_specs=[vmem()] * (2 + len(values)),
        out_specs=vmem(),
        scratch_shapes=[pltpu.VMEM((shards, 2 * width), F32)],
        out_shape=struct((rows, 2 * width), F32),
        compiler_params=params(16),
        cost_estimate=pl.CostEstimate(flops=1, bytes_accessed=1, transcendentals=0),
        name="cover",
    )(means, others, *values)


def cover_rest(begun, groups, names, rows, shards, total):
    values = [value for group in groups for value in group]
    if rows % 128:
        mine, side = lax.axis_index("ctx"), lax.axis_index("head") & 1
        out = [begun]

        def put(step, flip, gram):
            shard = lax.rem(mine + step + shards, shards)
            at = ((side ^ flip) * shards + shard) * rows
            old = lax.dynamic_slice_in_dim(out[0], at, rows, 1)
            new = (old + gram.astype(F32)) / total
            out[0] = lax.dynamic_update_slice_in_dim(out[0], new, at, 1)

        parts = [pick(rows, *pair) for pair in zip(names, groups)]
        assemble(put, jnp.where(mine >= shards // 2, 1, 0), shards, *parts)
        return out[0]
    return pl.pallas_call(
        functools.partial(cover_rest_kernel, rows, shards, total, names),
        in_specs=[vmem()] * (1 + len(values)),
        out_specs=vmem(),
        out_shape=struct(begun.shape, F32),
        compiler_params=params(16),
        name="cover_rest",
    )(begun, *values)


def body(queries, keys, values, log_decay, gain):
    count, width = queries.shape
    shards = lax.axis_size("ctx")
    sides = lax.axis_size("head")
    rows = width // shards
    mine = lax.axis_index("ctx")

    def to_shard(value, apart):
        return lax.ppermute(value, "ctx", [(a, a ^ apart) for a in range(shards)])

    def to_partner(value):
        return lax.ppermute(value, "head", [(a, a ^ 1) for a in range(sides)])

    near = shards // 2

    def nearby(values):
        return [values[0]] + [to_shard(values[apart], apart) for apart in range(1, near)]

    def forward(value, step):
        return lax.ppermute(value, "ctx", [(a, (a + step) % shards) for a in range(shards)])

    (entering, before, cumul), pieces, (keys, values) = local_states(
        keys, values, log_decay, near
    )
    raw, token = inner(queries, keys, values, cumul, 0)
    inside, left, leaving = chain(nearby(pieces), token)
    entered = lax.ppermute(leaving, "ctx", [(a, a + near) for a in range(near)])
    raw, token = inner(queries, keys, values, cumul, 1, raw, leaving)
    entry = nearby(spread_states(inside, left, entered, token))
    centered, stats = finish(
        queries, raw, entering, before, cumul, gain.reshape(1, width), entry
    )
    partner = to_partner(centered)

    half = shards // 2
    lines = width // RIDER_ROWS
    mean_rows = 3 * RIDER_ROWS
    extra = stats[:5].reshape(-1, lines)
    extra = jnp.pad(extra, ((0, -extra.shape[0] % 16), (0, 0)))
    near_steps = range(1, half // 2 + 1)
    far_steps = range(half // 2 + 1, half)
    plans = [
        [(step, side) for side in (0, 1) for step in near_steps],
        [(step, side) for step in far_steps for side in (0, 1)] + [(half, 2)],
        [(0, 0), (0, 1)],
    ]

    def begin(blocks, other, carried, after):
        keep, send = gram_parts(centered, other, carried, after, rows, blocks, 1)
        return [keep], [to_shard(send, 1)]

    def split_on(index, apart, after):
        keeps, others = kept[index]
        carried = riders if index == 0 else []
        keep, send, *merged = fold(
            keeps, others, after, carried, mean_rows * apart // 2, rows, 1, apart
        )
        riders[:] = merged or riders
        kept[index] = ([keep], [to_shard(send, apart)])
        return keep

    riders = [extra]
    blocks = plans[0]
    cut = len(blocks) // 2
    first = begin(blocks[:cut], centered, [], stats)
    second = begin(blocks[cut:], partner, riders, first[0][0])
    kept = [tuple(a + b for a, b in zip(first, second))]
    kept.append(begin(plans[1], partner, [], first[1][0]))
    after = split_on(0, 2, kept[1][0][0])
    kept.append(begin(plans[2], partner, [], after))
    aparts = [1 << place for place in range(1, shards.bit_length() - 1)]
    chunks, mirrors, crossed = [None] * 3, [[], [], []], [[], [], []]
    names = [plans, [[], [], []], [[], [], []]]

    def finished(index, after):
        blocks, ((keep,), (other,)) = plans[index], kept[index]
        steps = sorted({step for step, _ in blocks} - {0})
        runs = [[i for i, block in enumerate(blocks) if block[0] == step] for step in steps]
        crossing = [i for i, (step, side) in enumerate(blocks) if step and side]
        total, slabs = close(keep, other, after, rows, runs + [crossing] * bool(crossing))
        chunks[index] = total
        for step, run, slab in zip(steps, runs, slabs):
            mirrors[index].append(forward(slab, step))
            names[1][index].append([blocks[i] for i in run])
        if crossing:
            crossed[index].append(to_partner(slabs[-1]))
            names[2][index].append([blocks[i][0] for i in crossing])
        return total

    for apart in aparts[1:]:
        after = split_on(0, apart, after)
    every = merge(riders[0], kept[0][1][0][rows:], mean_rows * half)
    for apart in aparts:
        after = split_on(1, apart, after)
        if apart == aparts[-1]:
            after = finished(0, [after])
        after = split_on(2, apart, after)
    after = finished(1, [after])
    finished(2, [after])

    every = every.astype(F32)
    means = jnp.sum(every[: mean_rows * shards].reshape(shards, 3, width), axis=1)
    extremes = every[mean_rows * shards :][: 2 * RIDER_ROWS].reshape(2, width)
    shift = (extremes[0] + extremes[1]) / 2.0
    others = to_partner(means)
    begun = cover(
        means,
        others,
        (chunks[::2], mirrors[0] + mirrors[2], crossed[0] + crossed[2]),
        (names[0][::2], names[1][0] + names[1][2], names[2][0] + names[2][2]),
        rows,
        shards,
        count * shards,
    )
    covariance = cover_rest(
        begun,
        (chunks[1:2], mirrors[1], crossed[1]),
        (names[0][1:2], names[1][1], names[2][1]),
        rows,
        shards,
        count * shards,
    )
    return (shift, covariance)


def solution(mesh):
    placed = (P("ctx", "head"), P("ctx", "head"), P("ctx", "head"), P("head", "ctx"), P("head"))
    return jax.shard_map(
        body,
        mesh=mesh,
        in_specs=placed,
        out_specs=(P("head"), P(("head", "ctx"), None)),
        check_vma=False,
    )
```
